32 devices in a mesh: rows: 8 (over z, x), cols: 4 (over y, core).
Axes of the slice: x: 2, y: 2, z: 4, core: 2. Of those that a mesh axis runs over, the one named last changes fastest.
Arguments:
- images: float32 [8, 256, 256], P(None, 'rows', 'cols')
- fg_masks: int32 [8, 256, 256], P(None, 'rows', 'cols'), may hold values from 0 to 1, as said below
- ray_targets: int32 [8, 256, 256, 32], P(None, 'rows', 'cols'), may hold values from 0 to 48, as said below
- params: float32 [512193], replicated, may hold values from -0.82 to 0.82, as said below
- moment_one: float32 [512193], replicated, may hold values from -1.3972791e-06 to 1.3972791e-06
- moment_two: float32 [512193], replicated, may hold values from 2.4404862e-14 to 3.904778e-13
Outputs:
- new_params: float32 [512193], replicated
- new_moment_one: float32 [512193], replicated
- new_moment_two: float32 [512193], replicated
- loss_terms: float32 [3], replicated
- fg_count: float32 [], replicated
- grad_norm: float32 [], replicated
The draws below stay inside these ranges and needn't reach their ends.
Inputs may be any that keep to these rules, and one draw needn't show every extreme that they name: `fg_masks`: 1 marks foreground, 0 background; every patch holds both. `ray_targets`: 0 wherever fg_masks is 0, else 1 to 48. `params`: kernel entries lie within plus or minus the root of 6 over the kernel's fan-in, biases within 0.2.
All inputs are finite; a program needn't handle non-finite values.
Results may differ from the reference program's by a relative error of at most 0.0003.
The reference program's roundings to bfloat16 on the way count: a program that leaves them out, or rounds other values in their place, can miss the bound.
Values may be sent and summed in bfloat16 or wider, within the bound.
No kernel may reach another device: no remote copies, remote signals or barrier semaphores. Data moves between devices by JAX's collectives and lax.ppermute only.
A program may use at most 256 MiB of HBM per device.

```python
import math
import jax
import jax.numpy as jnp
from jax import lax

C1 = 32
C2 = 64
C3 = 128
FINAL = 128
RAYS = 32
PATCH = 256
NPATCH = 8
PARAMS = 512193


def layer_shapes_drawn():
    return [(3, 3, 1, C1), (3, 3, C1, C1), (3, 3, C1, C2), (3, 3, C2, C2), (3, 3, C2, C3), (3, 3, C3, C3), (3, 3, C3 + C2, C2), (3, 3, C2, C2), (3, 3, C2 + C1, C1), (3, 3, C1, C1), (3, 3, C1, FINAL), (FINAL, 1 + RAYS)]


def shared_labels(key):
    base_key = jax.random.fold_in(key, 7)
    shape = (NPATCH, PATCH, PATCH)
    rolls = jax.random.randint(jax.random.fold_in(base_key, 1), shape, 0, 1000)
    factor = jax.random.randint(jax.random.fold_in(base_key, 3), (NPATCH, 1, 1), 1, 11)
    row_place = lax.broadcasted_iota(jnp.int32, shape, 1)
    col_place = lax.broadcasted_iota(jnp.int32, shape, 2)
    limit_value = factor * 10 * (PATCH + 2 * row_place) * (PATCH + 2 * col_place) // (PATCH * PATCH)
    foreground = (rolls < limit_value).astype(jnp.int32)
    corner_last = (row_place == PATCH - 1) & (col_place == PATCH - 1)
    corner_first = (row_place == 0) & (col_place == 0)
    foreground = jnp.where(corner_last, 1, jnp.where(corner_first, 0, foreground))
    ray_values = jax.random.randint(jax.random.fold_in(base_key, 2), (NPATCH, PATCH, PATCH, RAYS), 1, 49)
    return (foreground, ray_values * foreground[..., None])


def draw_fg_masks(key, part):
    return shared_labels(key)[0]


def draw_ray_targets(key, part):
    return shared_labels(key)[1]


def draw_images(key, part):
    key = jax.random.fold_in(key, 11)
    shape = (NPATCH, PATCH, PATCH)
    row_frac = lax.broadcasted_iota(jnp.float32, shape, 1) / PATCH
    col_frac = lax.broadcasted_iota(jnp.float32, shape, 2) / PATCH
    base = jnp.clip(jax.random.normal(key, shape, jnp.float32), -4.0, 4.0)
    return base * (0.5 + row_frac) * (0.5 + col_frac)


def draw_params(key, part):
    key = jax.random.fold_in(key, 5)
    limits = []
    for kernel_shape in layer_shapes_drawn():
        entry_count = math.prod(kernel_shape)
        fan_value = entry_count // kernel_shape[-1]
        limits.append(jnp.full((entry_count,), (6.0 / fan_value) ** 0.5, jnp.float32))
        limits.append(jnp.full((kernel_shape[-1],), 0.2, jnp.float32))
    return jax.random.uniform(key, (PARAMS,), jnp.float32, -1.0, 1.0) * jnp.concatenate(limits)


def setup_inputs(seed: int = 0) -> dict:
    key_list = jax.random.split(jax.random.key(seed), 7)
    images = draw_images(jax.random.fold_in(key_list[6], 71), 0)
    fg_masks = draw_fg_masks(jax.random.fold_in(key_list[6], 71), 0)
    ray_targets = draw_ray_targets(jax.random.fold_in(key_list[6], 71), 0)
    params = draw_params(jax.random.fold_in(key_list[6], 71), 0)
    moment_one = jnp.clip(jax.random.uniform(key_list[4], (PARAMS,), jnp.float32, -1.3972791066407808e-06, 1.3972791066407808e-06), -1.3972791066407808e-06, 1.3972791066407808e-06)
    moment_two = jnp.clip(jnp.exp(jax.random.uniform(key_list[5], (PARAMS,), jnp.float32, math.log(2.4404862354089618e-14), math.log(3.904777976654339e-13))), 2.4404862354089618e-14, 3.904777976654339e-13)
    return {"images": images, "fg_masks": fg_masks, "ray_targets": ray_targets, "params": params, "moment_one": moment_one, "moment_two": moment_two}


@jax.custom_vjp
def low(v):
    return lax.optimization_barrier(v.astype(jnp.bfloat16)).astype(jnp.float32)

@jax.custom_vjp
def low_back(v):
    return v

def low_keep(v):
    return (low(v), None)

def low_pass(kept, grad):
    return (grad,)

def back_keep(v):
    return (v, None)

def back_low(kept, grad):
    return (low(grad),)
low.defvjp(low_keep, low_pass)
low_back.defvjp(back_keep, back_low)
beta_one = 0.9
beta_two = 0.999
learn_rate = 0.05
decay_rate = 0.01
adam_eps = 1e-08
clip_limit = 0.005
step_count = 10.0
ray_scale = 16.0

def layer_shapes():
    return [(3, 3, 1, C1), (3, 3, C1, C1), (3, 3, C1, C2), (3, 3, C2, C2), (3, 3, C2, C3), (3, 3, C3, C3), (3, 3, C3 + C2, C2), (3, 3, C2, C2), (3, 3, C2 + C1, C1), (3, 3, C1, C1), (3, 3, C1, FINAL), (FINAL, 1 + RAYS)]

def unpack(flat_params):
    result_list = []
    offset = 0
    for kernel_shape in layer_shapes():
        entry_count = math.prod(kernel_shape)
        weight = flat_params[offset:offset + entry_count].reshape(kernel_shape)
        offset = offset + entry_count
        bias_vec = flat_params[offset:offset + kernel_shape[-1]]
        offset = offset + kernel_shape[-1]
        result_list.append((weight, bias_vec))
    return result_list

def conv_layer(inputs, weight, bias_vec):
    summed = lax.conv_general_dilated(inputs, low(weight), (1, 1), 'SAME', dimension_numbers=('NHWC', 'HWIO', 'NHWC'), precision=lax.Precision.HIGHEST) + bias_vec
    return low(jax.nn.silu(low_back(summed)))

def shrink(values):
    return low(values.reshape(values.shape[0], values.shape[1] // 2, 2, values.shape[2] // 2, 2, values.shape[3]).mean(axis=(2, 4)))

def widen(values):
    return jnp.repeat(jnp.repeat(values, 2, axis=1), 2, axis=2)

def forward(flat_params, images, fg_masks, ray_targets):
    layers = unpack(flat_params)

    def run_layer(layer_index, inputs):
        return conv_layer(inputs, layers[layer_index][0], layers[layer_index][1])
    start_in = low(images).reshape(NPATCH, PATCH, PATCH, 1)
    skip_top = run_layer(1, run_layer(0, start_in))
    skip_mid = run_layer(3, run_layer(2, shrink(skip_top)))
    hidden = run_layer(5, run_layer(4, shrink(skip_mid)))
    hidden = run_layer(7, run_layer(6, jnp.concatenate([widen(hidden), skip_mid], axis=3)))
    hidden = run_layer(9, run_layer(8, jnp.concatenate([widen(hidden), skip_top], axis=3)))
    features = run_layer(10, hidden)
    head_out = jnp.einsum('phwc,ck->phwk', features, low(layers[11][0]), precision=lax.Precision.HIGHEST) + layers[11][1]
    head_out = low_back(head_out)
    logits = head_out[..., 0]
    distances = head_out[..., 1:]
    labels = fg_masks.astype(jnp.float32)
    target = ray_targets.astype(jnp.float32) / ray_scale
    fg_total = jnp.sum(labels)
    bg_total = NPATCH * PATCH * PATCH - fg_total
    cross_terms = jnp.maximum(logits, 0.0) - logits * labels + jnp.log1p(jnp.exp(-jnp.abs(logits)))
    diff = distances - target
    sum_fg = jnp.sum(cross_terms * labels)
    sum_bg = jnp.sum(cross_terms * (1.0 - labels))
    sum_ray = jnp.sum(jnp.sqrt(diff * diff + 1.0) * labels[..., None])
    loss = sum_fg / (2.0 * fg_total) + sum_bg / (2.0 * bg_total) + sum_ray / (fg_total * RAYS)
    return (loss, (jnp.stack([sum_fg, sum_bg, sum_ray]), fg_total))

def reference(images, fg_masks, ray_targets, params, moment_one, moment_two):

    def loss_of(flat_params):
        return forward(flat_params, images, fg_masks, ray_targets)
    loss_value, pull_back, extras = jax.vjp(loss_of, params, has_aux=True)
    grads = pull_back(jnp.ones((), jnp.float32))[0]
    grad_norm = jnp.sqrt(jnp.sum(grads * grads))
    clipped = grads * jnp.minimum(1.0, clip_limit / (grad_norm + 1e-06))
    new_one = beta_one * moment_one + (1.0 - beta_one) * clipped
    new_two = beta_two * moment_two + (1.0 - beta_two) * clipped * clipped
    first_hat = new_one / (1.0 - beta_one ** step_count)
    second_hat = new_two / (1.0 - beta_two ** step_count)
    new_params = params - learn_rate * (first_hat / (jnp.sqrt(second_hat) + adam_eps) + decay_rate * params)
    return (new_params, new_one, new_two, extras[0], extras[1], grad_norm)
```

```python
import functools
import math

import jax
import jax.numpy as jnp
from jax import lax
from jax.experimental import pallas as pl
from jax.experimental.pallas import tpu as pltpu
from jax.sharding import Mesh, PartitionSpec as P

C1 = 32
C2 = 64
C3 = 128
FINAL = 128
RAYS = 32

beta_one = 0.9
beta_two = 0.999
learn_rate = 0.05
decay_rate = 0.01
adam_eps = 1e-08
clip_limit = 0.005
step_count = 10.0
ray_scale = 16.0

bf16 = jnp.bfloat16
f32 = jnp.float32

LANES = 128
VMEM = pl.BlockSpec(memory_space=pltpu.VMEM)
SMEM = pl.BlockSpec(memory_space=pltpu.SMEM)

SHAPES = {
    1: (C1, C1), 2: (C1, C2), 3: (C2, C2), 4: (C2, C3), 5: (C3, C3),
    6: (C3 + C2, C2), 7: (C2, C2), 8: (C2 + C1, C1), 9: (C1, C1), 10: (C1, FINAL),
}

WIDE1 = [[0, 1, 2, 3], [4, None, None, -1]]
WIDE2 = [[0, 1], [2, -1]]
WIDE3 = [[0], [1], [-1]]
POOL1 = [[0, 2, 1, -1]]
POOL2 = [[0, -1], [1, None]]
UP2 = [[0, 2], [1, 3], [4, -1]]
UP3 = [[0], [1], [2], [-1]]
WIDE10 = [[0], [1], [2], [3], [4], [-1]]

INPUTS = {
    1: [(WIDE1, C1)], 2: [(POOL1, C1)], 3: [(WIDE2, C2)], 4: [(POOL2, C2)], 5: [(WIDE3, C3)],
    6: [(UP3, C3), (WIDE2, C2)], 7: [(WIDE2, C2)], 8: [(UP2, C2), (WIDE1, C1)], 9: [(WIDE1, C1)],
    10: [(WIDE1, C1)],
}
COLS = {1: 4, 2: 2, 3: 2, 4: 1, 5: 1, 6: 2, 7: 2, 8: 4, 9: 4, 10: 4}
GRADS = {1: WIDE1, 2: WIDE2, 3: WIDE2, 4: WIDE3, 5: WIDE3, 6: WIDE2, 7: WIDE2, 8: WIDE1, 9: WIDE1,
         10: WIDE10}
BACKS = {
    1: [[[0, 1, 2, 3]]], 2: [[[0, 0, 1, 1]]], 3: [[[0, 1]]], 4: [[[0, 0]]], 5: [[[0]]],
    6: [[[0], [1]], [[0, 1]]], 7: [[[0, 1]]], 8: [[[0, 2], [1, 3]], [[0, 1, 2, 3]]], 9: [[[0, 1, 2, 3]]],
    10: [[[0, 1, 2, 3]]],
}


def fwd_rows(k):
    return 3 if k == 10 else 4


def fwd_shape(k):
    per_row = sum(len(segs) for segs, _ in INPUTS[k]) * LANES
    outs = COLS[k] * SHAPES[k][1]
    return (fwd_rows(k) * per_row, outs if k == 10 else 2 * outs)


def back_shape(k):
    return (4 * len(GRADS[k]) * LANES, 2 * sum(len(s) for s in BACKS[k]) * LANES)


def prep_layer(k, w_ref, bias_ref, fwd_ref, tiled_ref, back_ref, flip_ref):
    ci, co = SHAPES[k]
    n = COLS[k]
    pair = (0,) if k == 10 else (0, 1)
    starts = [0]
    for _, ch in INPUTS[k]:
        starts.append(starts[-1] + ch)

    def tap(a, c, first, count):
        row = (a * 3 + c) * ci + first
        return w_ref[row : row + count, :]

    row = 0
    for j in range(fwd_rows(k)):
        for (segs, ch), first in zip(INPUTS[k], starts):
            zero = jnp.zeros((ch, co), bf16)
            for seg in segs:
                for h in seg:
                    parts = []
                    for q in pair:
                        for p in range(n):
                            a = j - q
                            c = None if h is None else h - p + 1
                            good = h is not None and 0 <= a <= 2 and 0 <= c <= 2
                            parts.append(tap(a, c, first, ch) if good else zero)
                    fwd_ref[row : row + ch, :] = jnp.concatenate(parts, axis=1)
                    row += ch
    bias = bias_ref[...]
    tiled_ref[...] = jnp.concatenate([bias] * (n * len(pair)), axis=1)
    col = 0
    for q in (0, 1):
        for (segs, ch), backs, first in zip(INPUTS[k], BACKS[k], starts):
            zero = jnp.zeros((ch, co), bf16)
            for seg in backs:
                row = 0
                for p in seg:
                    parts = []
                    for j in range(4):
                        for gseg in GRADS[k]:
                            for h in gseg:
                                a = q - j + 2
                                c = None if h is None else p - h + 1
                                good = h is not None and 0 <= a <= 2 and 0 <= c <= 2
                                parts.append(tap(a, c, first, ch) if good else zero)
                    flip_ref[row : row + ch, 0 : back_ref.shape[0]] = jnp.concatenate(parts, axis=1)
                    row += ch
                back_ref[:, col : col + LANES] = flip_ref[:, 0 : back_ref.shape[0]].T
                col += LANES


def prep_kernel(ks, *refs):
    count = len(ks)
    ins, outs = refs[: 2 * count], refs[2 * count : 5 * count]
    scratch, flip, sems = refs[5 * count : 8 * count], refs[8 * count], refs[8 * count + 1]
    copies = []
    for i, k in enumerate(ks):
        mine = scratch[3 * i : 3 * i + 3]
        prep_layer(k, ins[2 * i], ins[2 * i + 1], *mine, flip)
        for m in range(3):
            copy = pltpu.make_async_copy(mine[m], outs[3 * i + m], sems.at[3 * i + m])
            copy.start()
            copies.append(copy)
    for copy in copies:
        copy.wait()


def prep(ks, weights, biases):
    ins, shapes = [], []
    for k in ks:
        ins += [weights[k], biases[k]]
        fs = fwd_shape(k)
        shapes += [
            jax.ShapeDtypeStruct(fs, bf16),
            jax.ShapeDtypeStruct((1, fs[1]), f32),
            jax.ShapeDtypeStruct(back_shape(k), bf16),
        ]
    flat = pl.pallas_call(
        functools.partial(prep_kernel, ks),
        out_shape=shapes,
        in_specs=[VMEM] * len(ins),
        out_specs=[pl.BlockSpec(memory_space=pltpu.HBM)] * len(shapes),
        scratch_shapes=[pltpu.VMEM(v.shape, v.dtype) for v in shapes]
        + [
            pltpu.VMEM((LANES, max(back_shape(k)[0] for k in ks)), bf16),
            pltpu.SemaphoreType.DMA((len(shapes),)),
        ],
        name="prep",
        compiler_params=pltpu.CompilerParams(vmem_limit_bytes=26 * 2**20),
    )(*ins)
    return {k: tuple(flat[3 * i : 3 * i + 3]) for i, k in enumerate(ks)}


def divisor(count, limit):
    return max(d for d in range(1, min(count, limit) + 1) if count % d == 0)


def mm(a, b):
    return lax.dot_general(a, b, (((1,), (0,)), ((), ())), preferred_element_type=f32)


def mm_t(a, b):
    return lax.dot_general(a, b, (((0,), (0,)), ((), ())), preferred_element_type=f32)


def shifted(v):
    zero = jnp.zeros((v.shape[0], 1, v.shape[2]), v.dtype)
    left = jnp.concatenate([zero, v[:, :-1]], axis=1)
    right = jnp.concatenate([v[:, 1:], zero], axis=1)
    return left, right


def lane_of(width=LANES):
    return lax.broadcasted_iota(jnp.int32, (1, 1, width), 2)


def widen_row(v, three):
    left, right = shifted(v)
    if three:
        return jnp.concatenate([v, right, left], axis=2).astype(bf16)
    return jnp.concatenate([v, jnp.where(lane_of() < 64, right, left)], axis=2).astype(bf16)


def flat2(v):
    return v.reshape(v.shape[0] * v.shape[1], v.shape[2])


def pair_slab(ref, base, T, j, lanes=None):
    p, q = divmod(j + 1, 2)
    return flat2(ref[pl.ds(base + p - 1, T), q])


def row_slab(ref, base, T, j):
    return flat2(ref[pl.ds(base + (-1, 0, 0, 1)[j], T)])


def lhs_of(kinds, refs, bases, T, j, repeat):
    parts = []
    for kind, ref, base in zip(kinds, refs, bases):
        if kind == "up":
            v = row_slab(ref, base, T, j)
            if repeat:
                parts.append(v[:, :LANES])
            parts.append(v)
        else:
            parts.append(pair_slab(ref, base, T, j))
    return parts


def clear(ref, start, stop):
    def step(i, _):
        ref[i] = jnp.zeros(ref.shape[1:], ref.dtype)

    lax.fori_loop(start, stop, step, None)


def clear_outside(ref, count, pad, valid, unit):
    lo, hi = valid
    low = jnp.clip(lo, 0, count) // unit
    high = jnp.clip(hi, 0, count) // unit
    clear(ref, 0, pad // unit + low)
    clear(ref, pad // unit + high, (count + 2 * pad) // unit)


def silu(z):
    s = 1.0 / (1.0 + jnp.exp(-z))
    a = z * s
    return a, s + a - a * s


SLOPE_STEP = 1.0 / 26000.0
SLOPE_LOW = 0.125


def pack_slope(v):
    return (v * 26000.0 + (26000.0 * SLOPE_LOW + 0.5)).astype(jnp.int32).astype(jnp.int16)


def unpack_slope(v):
    return v.astype(jnp.int32).astype(f32) * SLOPE_STEP - SLOPE_LOW


def split_pair(v, T):
    g = v.shape[0] // T
    half = v.shape[1] // 2
    return [v[:, half * q : half * (q + 1)].reshape(T, g, half) for q in range(2)]


def fwd_kernel(cfg, *refs):
    kinds, T, count, offs, three, pool = (
        cfg["kinds"], cfg["T"], cfg["count"], cfg["offs"], cfg["three"], cfg["pool"]
    )
    n_in = len(kinds)
    valid_ref, ins, w_ref, b_ref = refs[0], refs[1 : 1 + n_in], refs[1 + n_in], refs[2 + n_in]
    out_ref, slope_ref = refs[3 + n_in], refs[4 + n_in]
    pool_ref = refs[5 + n_in] if pool else None

    def block(i, _):
        r = i * T
        parts = []
        for j in range(4):
            parts += lhs_of(kinds, ins, [r + o for o in offs], T, j, True)
        lhs = jnp.concatenate(parts, axis=1)
        a, slope = silu(mm(lhs, w_ref[...]) + b_ref[...])
        rows = split_pair(a, T)
        slopes = split_pair(slope, T)
        for q in range(2):
            slope_ref[pl.ds(r, T), q] = pack_slope(slopes[q])
            out_ref[pl.ds(r + 1, T), q] = widen_row(rows[q], three)
        if pool:
            x = sum(v.astype(bf16).astype(f32) for v in rows) * 0.25
            lane = lane_of()
            if pool == 1:
                near = x + pltpu.roll(x, LANES - C1, 2)
                far = x + pltpu.roll(x, C1, 2)
                left, right = shifted(far)
                mix = jnp.where(lane < 64, right, left)
                pooled = jnp.where((lane & 32) == 0, near, mix)
            else:
                y = x + pltpu.roll(x, C2, 2)
                left, right = shifted(y)
                pooled = jnp.concatenate([jnp.where(lane < 64, y, left), right], axis=2)
            pool_ref[pl.ds(r + 2, T)] = pooled.astype(bf16)

    lax.fori_loop(0, count // T, block, None)
    valid = (valid_ref[0] - cfg["lo"], valid_ref[1] - cfg["lo"])
    clear_outside(out_ref, count, 1, valid, 1)
    if pool:
        clear_outside(pool_ref, count, 2, valid, 1)


def forward(k, valid, lo, count, ins, offs, kinds, weight, bias, groups, three=False, pool=0):
    T = divisor(count, 18)
    cfg = dict(kinds=kinds, T=T, count=count, offs=offs, three=three, pool=pool, lo=lo)
    wide = (3 if three else 2) * LANES
    shapes = [
        jax.ShapeDtypeStruct((count + 2, 2, groups, wide), bf16),
        jax.ShapeDtypeStruct((count, 2, groups, LANES), jnp.int16),
    ]
    if pool:
        shapes.append(jax.ShapeDtypeStruct((count + 4, groups, pool * LANES), bf16))
    rows = 2 * count * groups
    return pl.pallas_call(
        functools.partial(fwd_kernel, cfg),
        out_shape=shapes,
        in_specs=[SMEM] + [VMEM] * (len(ins) + 2),
        out_specs=[VMEM] * len(shapes),
        cost_estimate=pl.CostEstimate(
            flops=rows * weight.shape[0] * weight.shape[1], bytes_accessed=rows * 1024, transcendentals=rows * 128
        ),
        name=f"conv{k}",
        compiler_params=pltpu.CompilerParams(vmem_limit_bytes=20 * 2**20),
    )(valid, *ins, weight, bias)


def head_kernel(cfg, scal_ref, x_ref, w_ref, b_ref, hw_ref, hwt_ref, hb_ref, ray_ref,
                grad_ref, dw_ref, db_ref, head_ref, dbh_ref, loss_ref, acc_ref, dhead_ref):
    T, rows, off, cols, per = cfg["T"], cfg["rows"], cfg["off"], cfg["cols"], cfg["per"]
    groups = x_ref.shape[1]
    M = T * groups
    fg_scale, bg_scale, ray_scale_ = scal_ref[0], scal_ref[1], scal_ref[2]
    lane = lane_of()[0]
    is_logit = (lane & 31) == 0
    ones = jnp.ones((8, M), bf16)
    for ref in (acc_ref, db_ref, dhead_ref, dbh_ref, loss_ref):
        ref[...] = jnp.zeros(ref.shape, ref.dtype)

    def block(i, _):
        r = i * T
        slabs = [flat2(x_ref[pl.ds(r + off + d, T)]) for d in (-1, 0, 1)]
        a, slope = silu(mm(jnp.concatenate(slabs, axis=1), w_ref[...]) + b_ref[...])
        feat = a.astype(bf16)
        head = mm(feat, hw_ref[...]) + hb_ref[...]
        dist, logit = head[:, :LANES], head[:, LANES:]
        part, first = r // per, r % per
        rays = jnp.concatenate(
            [ray_ref[part, c, pl.ds(first, T)] for c in range(cols)], axis=1
        )
        rays = flat2(rays.astype(f32))
        y = jnp.where(rays > 0.0, 1.0, 0.0)
        diff = dist - rays * (1.0 / ray_scale)
        square = diff * diff + 1.0
        smooth = jnp.sqrt(square)
        g_dist = diff / smooth * (y * ray_scale_)
        small = jnp.exp(-jnp.abs(logit))
        cross = jnp.maximum(logit, 0.0) - logit * y + jnp.log(1.0 + small)
        cross = jnp.where(is_logit, cross, 0.0)
        sig = 1.0 / (1.0 + jnp.exp(-logit))
        g_logit = jnp.where(is_logit, (sig - y) * (y * fg_scale + (1.0 - y) * bg_scale), 0.0)
        loss_ref[0:1] += jnp.sum(cross * y, axis=0, keepdims=True)
        loss_ref[1:2] += jnp.sum(cross * (1.0 - y), axis=0, keepdims=True)
        loss_ref[2:3] += jnp.sum(smooth * y, axis=0, keepdims=True)
        g_head = jnp.concatenate([g_dist, g_logit], axis=1).astype(bf16)
        dhead_ref[...] += mm_t(feat, g_head)
        dbh_ref[...] += mm(ones, g_head)
        gz = mm(g_head, hwt_ref[...]) * slope
        center = gz.astype(bf16)
        db_ref[...] += mm(ones, center)
        for a_ in range(3):
            acc_ref[a_] += mm_t(slabs[a_], center)
        left = shifted(gz[:, 3 * LANES :].reshape(T, groups, LANES))[0]
        right = shifted(gz[:, :LANES].reshape(T, groups, LANES))[1]
        grad_ref[pl.ds(r + 4, T)] = jnp.concatenate(
            [center.reshape(T, groups, 4 * LANES), right.astype(bf16), left.astype(bf16)], axis=2
        )

    lax.fori_loop(0, rows // T, block, None)
    clear(grad_ref, 0, 4)
    clear(grad_ref, rows + 4, rows + 8)
    for q in range(4):
        rows_ = dhead_ref[FINAL * q : FINAL * (q + 1), :]
        piece = pltpu.roll(rows_[:, :LANES], LANES - RAYS * q, 1) if q else rows_[:, :LANES]
        first = pltpu.roll(rows_[:, LANES:], LANES - RAYS * q, 1) if q else rows_[:, LANES:]
        both = jnp.where(lane == 0, first, pltpu.roll(piece, 1, 1))
        if q == 0:
            head_ref[...] = both
        else:
            head_ref[...] += both
    ci = SHAPES[10][0]
    for (a, c, start), total in sum_back({"k": 10}, lambda a: acc_ref[a]).items():
        row = (a * 3 + c) * ci + start
        dw_ref[row : row + total.shape[0], :] = total


def sum_back(cfg, acc):
    k = cfg["k"]
    ci, co = SHAPES[k]
    n = COLS[k]
    pieces = {}
    for a in range(3):
        value = acc(a)
        base = 0
        start = 0
        for segs, ch in INPUTS[k]:
            uses = {}
            unique = segs
            if segs is UP2:
                unique = [[(0, 1), (2, 3)], [(4,), (-1,)]]
            elif segs is UP3:
                unique = [[(0, 1)], [(2,)], [(-1,)]]
            else:
                unique = [[() if h is None else (h,) for h in seg] for seg in segs]
            for seg in unique:
                for hs in seg:
                    for h in hs:
                        for p in range(n):
                            c = h - p + 1
                            if 0 <= c <= 2:
                                uses.setdefault(c, []).append((base, p))
                    base += ch
            for c, places in uses.items():
                total = None
                for row, p in places:
                    piece = value[row : row + ch, p * co : (p + 1) * co]
                    total = piece if total is None else total + piece
                pieces[a, c, start] = total
            start += ch
    return pieces


def back_kernel(cfg, *refs):
    k, kinds, T, count, lo = cfg["k"], cfg["kinds"], cfg["T"], cfg["count"], cfg["lo"]
    goff, xoffs, mode = cfg["goff"], cfg["xoffs"], cfg["mode"]
    ci, co = SHAPES[k]
    wgrad = cfg["wgrad"]
    refs = list(refs)
    take = lambda m: [refs.pop(0) for _ in range(m)]
    (valid_ref, grad_ref, w_ref, slope_ref) = take(4)
    extra = take(1)[0] if mode in ("pool",) else None
    cols_ref = take(1)[0] if mode == "last" else None
    xs = take(len(kinds)) if wgrad else []
    out_ref = take(1)[0]
    side_ref = take(1)[0] if mode == "join" else None
    dw_ref, db_ref = take(2) if wgrad else (None, None)
    d0_ref, db0_ref = take(2) if mode == "last" else (None, None)
    acc_ref = take(1)[0] if wgrad else None

    if wgrad:
        Tw, wcount, glo = cfg["Tw"], cfg["wcount"], cfg["gpad"]
        ones = jnp.ones((8, Tw * grad_ref.shape[2]), bf16)
        acc_ref[...] = jnp.zeros(acc_ref.shape, f32)
        db_ref[...] = jnp.zeros(db_ref.shape, f32)

        def wblock(i, _):
            r = i * Tw
            g = jnp.concatenate(
                [flat2(grad_ref[pl.ds(r + glo, Tw), q, :, 0:LANES]) for q in range(2)], axis=1
            )
            db_ref[...] += mm(ones, g)
            for j in range(4):
                x = jnp.concatenate(lhs_of(kinds, xs, [r + o for o in xoffs], Tw, j, False), axis=1)
                acc_ref[j] += mm_t(x, g)

        lax.fori_loop(0, wcount // Tw, wblock, None)
        pieces = sum_back(cfg, lambda a: acc_ref[a, :, 0:LANES] + acc_ref[a + 1, :, LANES : 2 * LANES])
        for (a, c, start), total in pieces.items():
            row = (a * 3 + c) * ci + start
            dw_ref[row : row + total.shape[0], :] = total

    if mode == "last":
        d0_ref[...] = jnp.zeros(d0_ref.shape, f32)
        db0_ref[...] = jnp.zeros(db0_ref.shape, f32)

    if mode == "join":
        side_ref[...] = jnp.zeros(side_ref.shape, f32)

    def block(i, _):
        r = i * T
        lhs = jnp.concatenate([pair_slab(grad_ref, r + goff, T, j) for j in range(4)], axis=1)
        acc = mm(lhs, w_ref[...])
        groups = grad_ref.shape[2]
        if mode in ("plain", "last"):
            vals = split_pair(acc, T)
            for q in range(2):
                gz = vals[q] * unpack_slope(slope_ref[pl.ds(r, T), q])
                if mode == "last":
                    out_ref[pl.ds(r, T), q] = gz.astype(bf16)
                else:
                    out_ref[pl.ds(r + 2, T), q] = widen_row(gz, cfg["three"])
        elif mode == "join":
            parts = [acc[:, LANES * m : LANES * (m + 1)].reshape(T, groups, LANES) for m in range(6)]
            up = (parts[0] + parts[1]) + (parts[3] + parts[4])
            gz = up * unpack_slope(slope_ref[pl.ds(r, T)])
            out_ref[pl.ds(r + 4, T)] = widen_row(gz, cfg["three"])
            for q in range(2):
                side_ref[pl.ds(r + cfg["soff"], T), q] = parts[2 + 3 * q]
        else:
            vals = split_pair(acc, T)
            for q in range(2):
                for e in range(2):
                    total = vals[q] * 0.25 + extra[pl.ds(r, T), q, e]
                    gz = total * unpack_slope(slope_ref[pl.ds(r, T), q, e])
                    out_ref[pl.ds(r + 1, T), q, e] = widen_row(gz, cfg["three"])

    lax.fori_loop(0, count // T, block, None)
    valid = (valid_ref[0] - lo, valid_ref[1] - lo)
    if mode == "plain":
        clear_outside(out_ref, count, 2, valid, 1)
    elif mode == "last":
        clear_outside(out_ref, count, 0, valid, 1)
        ones = jnp.ones((8, T * out_ref.shape[2]), bf16)

        def block0(i, _):
            r = i * T
            g = jnp.concatenate([flat2(out_ref[pl.ds(r, T), q]) for q in range(2)], axis=1)
            db0_ref[...] += mm(ones, g)
            d0_ref[...] += mm_t(flat2(cols_ref[pl.ds(r, T)]), g)

        lax.fori_loop(0, count // T, block0, None)
    elif mode == "join":
        clear_outside(out_ref, count, 4, valid, 1)
    else:
        clear_outside(out_ref, 2 * count, 2, valid, 2)


def backward(k, mode, valid, lo, count, grad, goff, weight, slope, groups, three=False, xs=(), xoffs=(),
             kinds=(), wcount=0, gpad=2, extra=None, cols=None, side=None, soff=0):
    ci, co = SHAPES[k]
    T = divisor(count, 18 if mode != "pool" else 13)
    wide = (3 if three else 2) * LANES
    cfg = dict(k=k, mode=mode, T=T, count=count, lo=lo, goff=goff, three=three, kinds=kinds, xoffs=xoffs,
               wgrad=bool(xs), soff=soff, gpad=gpad)
    args = [valid, grad, weight, slope]
    if mode == "pool":
        args.append(extra)
    if mode == "last":
        args.append(cols)
    args += list(xs)
    if mode == "plain":
        shapes = [jax.ShapeDtypeStruct((count + 4, 2, groups, wide), bf16)]
    elif mode == "last":
        shapes = [jax.ShapeDtypeStruct((count, 2, groups, LANES), bf16)]
    elif mode == "join":
        shapes = [
            jax.ShapeDtypeStruct((count + 8, groups, wide), bf16),
            jax.ShapeDtypeStruct(side, f32),
        ]
    else:
        shapes = [jax.ShapeDtypeStruct((count + 2, 2, 2, groups, wide), bf16)]
    scratch = []
    if xs:
        cfg["wcount"] = wcount
        cfg["Tw"] = divisor(wcount, 18)
        per_row = sum(x.shape[-1] for x in xs)
        shapes += [jax.ShapeDtypeStruct((9 * ci, co), f32), jax.ShapeDtypeStruct((8, 2 * LANES), f32)]
        scratch = [pltpu.VMEM((4, per_row, 2 * LANES), f32)]
    if mode == "last":
        shapes += [
            jax.ShapeDtypeStruct((cols.shape[2], 2 * LANES), f32),
            jax.ShapeDtypeStruct((8, 2 * LANES), f32),
        ]
    rows = 2 * count * groups
    return pl.pallas_call(
        functools.partial(back_kernel, cfg),
        out_shape=shapes,
        in_specs=[SMEM] + [VMEM] * (len(args) - 1),
        out_specs=[VMEM] * len(shapes),
        scratch_shapes=scratch,
        name=f"grad{k}",
        cost_estimate=pl.CostEstimate(
            flops=2 * rows * weight.shape[0] * weight.shape[1], bytes_accessed=rows * 1024, transcendentals=0
        ),
        compiler_params=pltpu.CompilerParams(vmem_limit_bytes=22 * 2**20),
    )(*args)


def head_prep_kernel(w_ref, b_ref, hw_ref, hwt_ref, hb_ref):
    w = w_ref[...]
    zero = jnp.zeros((FINAL, RAYS), bf16)
    for q in range(4):
        parts = [w[:, :RAYS] if p == q else zero for p in range(4)]
        parts += [w[:, RAYS:] if p == q else zero for p in range(4)]
        hw_ref[FINAL * q : FINAL * (q + 1), :] = jnp.concatenate(parts, axis=1)
    hwt_ref[...] = hw_ref[...].T
    b = b_ref[...]
    hb_ref[...] = jnp.concatenate([b[:, :RAYS]] * 4 + [b[:, RAYS:]] * 4, axis=1)


def head_prep(weight, bias):
    return pl.pallas_call(
        head_prep_kernel,
        out_shape=[
            jax.ShapeDtypeStruct((4 * FINAL, 2 * LANES), bf16),
            jax.ShapeDtypeStruct((2 * LANES, 4 * FINAL), bf16),
            jax.ShapeDtypeStruct((1, 2 * LANES), f32),
        ],
        in_specs=[VMEM] * 2,
        out_specs=[VMEM] * 3,
    )(weight, bias)


def head(scal, a9, weight, bias, hw, hwt, hb, rays, rows):
    parts, cols, per = rays.shape[:3]
    groups = a9.shape[1]
    T = divisor(math.gcd(rows, per), 8)
    cfg = dict(T=T, rows=rows, off=4, cols=cols, per=per)
    return pl.pallas_call(
        functools.partial(head_kernel, cfg),
        out_shape=[
            jax.ShapeDtypeStruct((rows + 8, groups, 6 * LANES), bf16),
            jax.ShapeDtypeStruct((9 * C1, FINAL), f32),
            jax.ShapeDtypeStruct((8, 4 * FINAL), f32),
            jax.ShapeDtypeStruct((FINAL, LANES), f32),
            jax.ShapeDtypeStruct((8, 2 * LANES), f32),
            jax.ShapeDtypeStruct((8, LANES), f32),
        ],
        in_specs=[SMEM] + [VMEM] * 7,
        out_specs=[VMEM] * 6,
        scratch_shapes=[pltpu.VMEM((3, 2 * LANES, 4 * FINAL), f32), pltpu.VMEM((4 * FINAL, 2 * LANES), f32)],
        name="head",
        cost_estimate=pl.CostEstimate(flops=10**10, bytes_accessed=10**7, transcendentals=10**6),
        compiler_params=pltpu.CompilerParams(vmem_limit_bytes=24 * 2**20),
    )(scal, a9, weight, bias, hw, hwt, hb, rays)


def layer_shapes():
    return [(3, 3, 1, C1)] + [(3, 3, *SHAPES[k]) for k in range(1, 11)] + [(FINAL, 1 + RAYS)]


def unpack(flat_params):
    result_list = []
    offset = 0
    for kernel_shape in layer_shapes():
        entry_count = math.prod(kernel_shape)
        weight = flat_params[offset : offset + entry_count].reshape(-1, kernel_shape[-1])
        offset = offset + entry_count
        bias_vec = flat_params[offset : offset + kernel_shape[-1]].reshape(1, -1)
        offset = offset + kernel_shape[-1]
        result_list.append((weight, bias_vec))
    return result_list


HALO = 24
EDGE = 8


def first_kernel(cfg, valid_ref, got_ref, w_ref, bias_ref, out_ref, slope_ref, cols_ref, x_ref, xt_ref, v_ref, b_ref):
    own, hi, strips, tiles_across, per = cfg["own"], cfg["hi"], cfg["strips"], cfg["cols"], cfg["per"]
    count, T = cfg["count"], cfg["T"]
    strip = valid_ref[2]
    rows = own + 2 * HALO
    reach = -(-HALO // per)
    x_ref[...] = jnp.zeros(x_ref.shape, f32)
    for d in range(-reach, hi + reach):
        tile = strip * hi + d
        start = HALO + d * per
        first, last = max(0, -start), min(per, rows - start)

        @pl.when((tile >= 0) & (tile < strips * hi))
        def _():
            parts = [got_ref[tile * tiles_across + c].astype(f32) for c in range(tiles_across)]
            value = jnp.concatenate(parts, axis=1)
            x_ref[start + first : start + last, :] = value[first:last]

    width = x_ref.shape[1]
    groups = width // 4
    xt_ref[0:EDGE] = jnp.zeros((EDGE, LANES), f32)
    xt_ref[EDGE + width : 2 * EDGE + width] = jnp.zeros((EDGE, LANES), f32)
    xt_ref[EDGE : EDGE + width] = x_ref[...].T
    for m in range(6):
        v_ref[m] = xt_ref[pl.ds(EDGE + m - 1, groups, stride=4), :]
    lane = lax.broadcasted_iota(jnp.int32, (1, LANES), 1)

    def gather(i, _):
        total = jnp.zeros((groups, LANES), f32)
        for m in range(6):
            turned = pltpu.roll(v_ref[m], 4 * m + LANES - (2 * i + 1), 1)
            total = jnp.where((lane >= 4 * m) & (lane < 4 * m + 4), turned, total)
        cols_ref[i] = total.astype(bf16)

    lax.fori_loop(0, count, gather, None)
    b_ref[...] = jnp.zeros(b_ref.shape, f32)
    zero = jnp.zeros((1, C1), f32)
    for m in range(6):
        for j in range(4):
            parts = []
            for q in range(2):
                for p in range(4):
                    a, c = j - q, m - p
                    good = 0 <= a <= 2 and 0 <= c <= 2
                    parts.append(w_ref[a * 3 + c : a * 3 + c + 1, :] if good else zero)
            b_ref[4 * m + j : 4 * m + j + 1, :] = jnp.concatenate(parts, axis=1)
    weight = b_ref[...].astype(bf16)
    bias = jnp.concatenate([bias_ref[...]] * 8, axis=1)

    def block(i, _):
        r = i * T
        a, slope = silu(mm(flat2(cols_ref[pl.ds(r, T)]), weight) + bias)
        rows_, slopes = split_pair(a, T), split_pair(slope, T)
        for q in range(2):
            slope_ref[pl.ds(r, T), q] = pack_slope(slopes[q])
            out_ref[pl.ds(r + 1, T), q] = widen_row(rows_[q], False)

    lax.fori_loop(0, count // T, block, None)
    valid = (valid_ref[0] - cfg["lo"], valid_ref[1] - cfg["lo"])
    clear_outside(out_ref, count, 1, valid, 1)


def first_layer(valid, got, weight, bias, own, hi, strips, cols, per, width):
    groups = width // 4
    count = own // 2 + 22
    cfg = dict(own=own, hi=hi, strips=strips, cols=cols, per=per, count=count, lo=-11, T=divisor(count, 18))
    return pl.pallas_call(
        functools.partial(first_kernel, cfg),
        out_shape=[
            jax.ShapeDtypeStruct((count + 2, 2, groups, 2 * LANES), bf16),
            jax.ShapeDtypeStruct((count, 2, groups, LANES), jnp.int16),
            jax.ShapeDtypeStruct((count, groups, LANES), bf16),
        ],
        in_specs=[SMEM] + [VMEM] * 3,
        out_specs=[VMEM] * 3,
        scratch_shapes=[
            pltpu.VMEM((LANES, width), f32),
            pltpu.VMEM((width + 2 * EDGE, LANES), f32),
            pltpu.VMEM((6, groups, LANES), f32),
            pltpu.VMEM((LANES, 2 * LANES), f32),
        ],
        name="conv0",
        compiler_params=pltpu.CompilerParams(vmem_limit_bytes=12 * 2**20),
    )(valid, got, weight, bias)


def network(got, strip, tiling, rays, fg_total, bg_total, valid_at, params, own):
    groups = tiling[-1] // 4
    h, h2, h3 = own // 2, own // 4, own // 8
    layers = unpack(params)
    weights = {k: layers[k][0].astype(bf16) for k in range(12)}
    biases = {k: layers[k][1] for k in range(12)}
    ks = tuple(range(1, 11))
    ready = prep(ks, weights, biases)
    w11, b11 = weights[11], biases[11]
    tail = ((0, 0), (0, RAYS - 1))
    hw, hwt, hb = head_prep(
        jnp.concatenate([w11[:, 1:], jnp.pad(w11[:, :1], tail)], axis=1),
        jnp.concatenate([b11[:, 1:], jnp.pad(b11[:, :1], tail)], axis=1),
    )
    v1, v2, v3 = valid_at

    a0, sl0, cols = first_layer(
        jnp.concatenate([v1, strip[None]]), got, weights[0].astype(f32), biases[0], own, *tiling
    )
    count0 = h + 22
    s1, sl1, p1 = forward(1, v1, -10, h + 20, [a0], (2,), ("pair",), *ready[1][:2], groups, pool=1)
    p1 = p1.reshape(h2 + 12, 2, groups, LANES)
    a2, sl2 = forward(2, v2, -5, h2 + 10, [p1], (1,), ("pair",), *ready[2][:2], groups)
    s2, sl3, p2 = forward(3, v2, -4, h2 + 8, [a2], (2,), ("pair",), *ready[3][:2], groups, pool=2)
    p2 = p2.reshape(h3 + 6, 2, groups, 2 * LANES)
    a4, sl4 = forward(4, v3, -2, h3 + 4, [p2], (1,), ("pair",), *ready[4][:2], groups, three=True)
    t3, sl5 = forward(5, v3, -1, h3 + 2, [a4], (2,), ("pair",), *ready[5][:2], groups, three=True)
    t3 = t3.reshape(-1, groups, 3 * LANES)
    a6, sl6 = forward(6, v2, -2, h2 + 4, [t3, s2], (2, 3), ("up", "pair"), *ready[6][:2], groups)
    t2, sl7 = forward(7, v2, -1, h2 + 2, [a6], (2,), ("pair",), *ready[7][:2], groups)
    t2 = t2.reshape(-1, groups, 2 * LANES)
    a8, sl8 = forward(8, v1, -1, h + 2, [t2, s1], (3, 10), ("up", "pair"), *ready[8][:2], groups)
    a9, sl9 = forward(9, v1, -1, h + 2, [a8], (1,), ("pair",), *ready[9][:2], groups)

    scal = jnp.stack([0.5 / fg_total, 0.5 / bg_total, 1.0 / (fg_total * RAYS)])
    gz, dw10, db10, dhead, dbh, losses = head(
        scal, a9.reshape(-1, groups, 2 * LANES), *ready[10][:2], hw, hwt, hb, rays, own
    )
    grads = {10: (dw10, db10)}
    folded = dbh[:1].reshape(2, 4, RAYS).sum(1)
    tail = jnp.concatenate([dhead[:, : 1 + RAYS].reshape(-1), folded[1, :1], folded[0], losses[:3].sum(axis=1)])

    def take(k, dw, db):
        grads[k] = (dw, db)

    def pairs(v):
        return v.reshape(v.shape[0] // 2, 2, *v.shape[1:])

    def whole(v):
        return v.reshape(v.shape[0] * v.shape[1], *v.shape[2:])

    (gz,) = backward(10, "plain", v1, -1, h + 2, pairs(gz), 1, ready[10][2], sl9, groups)
    gz, dw, db = backward(9, "plain", v1, -1, h + 2, gz, 2, ready[9][2], sl8, groups, xs=(a8,), xoffs=(1,),
                          kinds=("pair",), wcount=h + 2)
    take(9, dw, db)
    gz, gs1, dw, db = backward(8, "join", v1, -2, h + 4, gz, 1, ready[8][2], whole(sl7), groups, xs=(t2, s1),
                               xoffs=(3, 10), kinds=("up", "pair"), wcount=h + 2,
                               side=(h + 20, 2, groups, LANES), soff=8)
    take(8, dw, db)
    gz, dw, db = backward(7, "plain", v2, -2, h2 + 4, pairs(gz), 1, ready[7][2], sl6, groups, xs=(a6,),
                          xoffs=(2,), kinds=("pair",), wcount=h2 + 2)
    take(7, dw, db)
    gz, gs2, dw, db = backward(6, "join", v2, -2, h2 + 4, gz, 2, ready[6][2], whole(sl5), groups, three=True,
                               xs=(t3, s2), xoffs=(2, 3), kinds=("up", "pair"), wcount=h2 + 4,
                               side=(h2 + 8, 2, groups, LANES), soff=2)
    take(6, dw, db)
    gz, dw, db = backward(5, "plain", v3, -2, h3 + 4, pairs(gz), 1, ready[5][2], sl4, groups, three=True,
                          xs=(a4,), xoffs=(2,), kinds=("pair",), wcount=h3 + 2)
    take(5, dw, db)
    gz, dw, db = backward(4, "pool", v2, -4, h3 + 4, gz, 2, ready[4][2], pairs(sl3), groups, xs=(p2,),
                          xoffs=(1,), kinds=("pair",), wcount=h3 + 4, extra=pairs(gs2))
    take(4, dw, db)
    gz, dw, db = backward(3, "plain", v2, -5, h2 + 10, whole(gz), 1, ready[3][2], sl2, groups, xs=(a2,),
                          xoffs=(2,), kinds=("pair",), wcount=h2 + 8)
    take(3, dw, db)
    gz, dw, db = backward(2, "pool", v1, -10, h2 + 10, gz, 2, ready[2][2], pairs(sl1), groups, xs=(p1,),
                          xoffs=(1,), kinds=("pair",), wcount=h2 + 10, extra=pairs(gs1))
    take(2, dw, db)
    _, dw, db, dw0, db0 = backward(1, "last", v1, -11, count0, whole(gz), 1, ready[1][2], sl0, groups,
                                   xs=(a0,), xoffs=(2,), kinds=("pair",), wcount=h + 20,
                                   cols=cols)
    take(1, dw, db)
    return assemble(grads, dw0, db0, tail)


def offset_of(k):
    return sum(math.prod(v) + v[-1] for v in layer_shapes()[:k])


def place(out_ref, value, offset):
    row, lane0 = divmod(offset, LANES)
    n = value.shape[0]
    if lane0 == 0:
        out_ref[row : row + n, :] += value
        return
    lane = lax.broadcasted_iota(jnp.int32, (1, LANES), 1)
    turned = pltpu.roll(value, lane0, 1)
    out_ref[row : row + n, :] += jnp.where(lane >= lane0, turned, 0.0)
    out_ref[row + 1 : row + 1 + n, :] += jnp.where(lane < lane0, turned, 0.0)


def assemble_kernel(ks, *refs):
    dws, dbs = refs[: len(ks)], refs[len(ks) : 2 * len(ks)]
    dw0_ref, db0_ref, tail_ref, out_ref, tmp_ref = refs[2 * len(ks) :]
    lane = lax.broadcasted_iota(jnp.int32, (1, LANES), 1)
    out_ref[...] = jnp.zeros(out_ref.shape, f32)

    def fold(ref, co):
        total = ref[0:1, 0:LANES]
        for m in range(1, ref.shape[1] // LANES):
            total = total + ref[0:1, LANES * m : LANES * (m + 1)]
        width = LANES
        while width > co:
            width //= 2
            total = total + pltpu.roll(total, width, 1)
        return jnp.where(lane < co, total, 0.0)

    for k, dw_ref, db_ref in zip(ks, dws, dbs):
        ci, co = SHAPES[k]
        size = 9 * ci * co
        n = size // LANES
        fill = LANES // co
        if fill == 1:
            value = dw_ref[...]
        else:
            value = jnp.concatenate([dw_ref[pl.ds(m, n, stride=fill), :] for m in range(fill)], axis=1)
        place(out_ref, value, offset_of(k))
        place(out_ref, fold(db_ref, co), offset_of(k) + size)
    tmp_ref[...] = jnp.zeros(tmp_ref.shape, f32)
    for a in range(3):
        for c in range(3):
            total = None
            for q in range(2):
                for p in range(4):
                    m, j = p + c, a + q
                    at = (q * 4 + p) * C1
                    piece = dw0_ref[4 * m + j : 4 * m + j + 1, at : at + C1]
                    total = piece if total is None else total + piece
            spot = a * 3 + c
            row, at = divmod(spot * C1, LANES)
            tmp_ref[row : row + 1, at : at + C1] = total
    place(out_ref, tmp_ref[...], 0)
    place(out_ref, fold(db0_ref, C1), 9 * C1)
    place(out_ref, tail_ref[...], offset_of(11))


def assemble(grads, dw0, db0, tail):
    ks = tuple(range(1, 11))
    rows = -(-(offset_of(12) + 3) // (LANES * 32)) * 32
    rows = -(-rows // 256) * 256
    tail = jnp.pad(tail, (0, -tail.shape[0] % LANES)).reshape(-1, LANES)
    args = [grads[k][0] for k in ks] + [grads[k][1] for k in ks] + [dw0, db0, tail]
    return pl.pallas_call(
        functools.partial(assemble_kernel, ks),
        out_shape=jax.ShapeDtypeStruct((rows, LANES), f32),
        in_specs=[VMEM] * len(args),
        out_specs=VMEM,
        scratch_shapes=[pltpu.VMEM((8, LANES), f32)],
        name="assemble",
        compiler_params=pltpu.CompilerParams(vmem_limit_bytes=12 * 2**20),
    )(*args)


def sum_all(value):
    strips = lax.axis_size("strip")
    pairs = lax.axis_size("hi") * lax.axis_size("half")
    core = lax.axis_index("core")
    swap = [(0, 1), (1, 0)]
    half = value.shape[0] // 2
    keep = lax.dynamic_slice_in_dim(value, core * half, half)
    send = lax.dynamic_slice_in_dim(value, (1 - core) * half, half)
    part = keep + lax.ppermute(send, "core", swap)
    for axes, n in ((("hi", "half"), pairs), (("strip",), strips)):
        part = lax.all_to_all(part, axes, 0, 0, tiled=True)
        part = part.reshape(n, -1, LANES).sum(0)
    for axes, n in ((("strip",), strips), (("hi", "half"), pairs)):
        part = lax.all_to_all(jnp.tile(part, (n, 1)), axes, 0, 0, tiled=True)
    other = lax.ppermute(part, "core", swap)
    return jnp.where(
        core == 0, jnp.concatenate([part, other]), jnp.concatenate([other, part])
    )


def adam_update(grad_sum, grad_norm, weights, first_old, second_old):
    clipped = grad_sum * jnp.minimum(1.0, clip_limit / (grad_norm + 1e-06))
    new_one = beta_one * first_old + (1.0 - beta_one) * clipped
    new_two = beta_two * second_old + (1.0 - beta_two) * clipped * clipped
    first_hat = new_one / (1.0 - beta_one**step_count)
    second_hat = new_two / (1.0 - beta_two**step_count)
    new_weights = weights - learn_rate * (
        first_hat / (jnp.sqrt(second_hat) + adam_eps) + decay_rate * weights
    )
    return (new_weights, new_one, new_two)


AXES = ("strip", "hi", "half", "core")
GROUP = ("hi", "half", "core")


def body(patch, images, fg_masks, ray_targets, params, moment_one, moment_two):
    strips, hi, half, core = (lax.axis_size(a) for a in AXES)
    cols = half * core
    count, rows_here, cols_here = images.shape
    own = rows_here * hi
    strip = lax.axis_index("strip")

    labels = jnp.sum(fg_masks)
    digits = jnp.stack([labels % 128, labels // 128 % 128, labels // 16384]).astype(bf16)
    below = -(-(rows_here + 1) // 16) * 16 - rows_here
    digits = jnp.pad(digits[None, None], ((0, 0), (0, below - 1), (0, cols_here - 3)))
    tiles = jnp.concatenate([images.astype(bf16), jnp.broadcast_to(digits, (count, *digits.shape[1:]))], axis=1)
    tiles = jnp.tile(tiles, (strips, 1, 1))
    got = lax.all_to_all(tiles, AXES, 0, 0, tiled=True)
    digits = got[:, rows_here, :3].astype(f32).sum(0)
    fg_total = digits[0] + 128.0 * digits[1] + 16384.0 * digits[2]
    bg_total = float(count * patch * patch) - fg_total

    rays = ray_targets.astype(bf16).reshape(count, rows_here, cols_here // 4, 4 * RAYS)
    rays = lax.all_to_all(rays, GROUP, 0, 0, tiled=True)
    rays = rays.reshape(hi, cols, rows_here, cols_here // 4, 4 * RAYS)

    bounds = [
        jnp.stack([-strip * (own // d), patch // d - strip * (own // d)]).astype(jnp.int32)
        for d in (2, 4, 8)
    ]
    tiling = (hi, strips, cols, rows_here, patch)
    flat = network(got, strip.astype(jnp.int32), tiling, rays, fg_total, bg_total, bounds, params, own)
    total = sum_all(flat).reshape(-1)
    size = params.shape[0]
    grad_sum, loss_terms = total[:size], total[size : size + 3]
    grad_norm = jnp.sqrt(jnp.sum(grad_sum * grad_sum))
    new_params, new_one, new_two = adam_update(grad_sum, grad_norm, params, moment_one, moment_two)
    return (new_params, new_one, new_two, loss_terms, fg_total, grad_norm)


def solution(mesh):
    rows, cols = mesh.shape["rows"], mesh.shape["cols"]
    patches = 8
    hi = patches // cols
    split = Mesh(mesh.devices.reshape(rows // hi, hi, cols // 2, 2), AXES)
    tiled = P(None, ("strip", "hi"), ("half", "core"))
    in_specs = (tiled, tiled, P(None, ("strip", "hi"), ("half", "core"), None), P(), P(), P())
    out_specs = (P(),) * 6

    def step(images, *rest):
        if images.shape[0] != patches:
            raise ValueError("eight patches")
        part = functools.partial(body, images.shape[1])
        return jax.shard_map(part, mesh=split, in_specs=in_specs, out_specs=out_specs, check_vma=False)(
            images, *rest
        )

    return step
```

```python
import functools
import math

import jax
import jax.numpy as jnp
from jax import lax
from jax.experimental import pallas as pl
from jax.experimental.pallas import tpu as pltpu
from jax.sharding import Mesh, PartitionSpec as P

C1 = 32
C2 = 64
C3 = 128
FINAL = 128
RAYS = 32

beta_one = 0.9
beta_two = 0.999
learn_rate = 0.05
decay_rate = 0.01
adam_eps = 1e-08
clip_limit = 0.005
step_count = 10.0
ray_scale = 16.0

bf16 = jnp.bfloat16
f32 = jnp.float32

LANES = 128
FORWARD = range(1, 10)
GRANT = 60 * 2**20
HALO = 24
EDGE = 8
VMEM = pl.BlockSpec(memory_space=pltpu.VMEM)
SMEM = pl.BlockSpec(memory_space=pltpu.SMEM)
ANY = pl.BlockSpec(memory_space=pl.ANY)

SHAPES = {
    1: (C1, C1), 2: (C1, C2), 3: (C2, C2), 4: (C2, C3), 5: (C3, C3),
    6: (C3 + C2, C2), 7: (C2, C2), 8: (C2 + C1, C1), 9: (C1, C1), 10: (C1, FINAL),
}

WIDE1 = [[0, 1, 2, 3], [4, None, None, -1]]
WIDE2 = [[0, 1], [2, -1]]
WIDE3 = [[0], [1], [-1]]
POOL1 = [[0, 2, 1, -1]]
POOL2 = [[0, -1], [1, None]]
UP2 = [[0, 2], [1, 3], [4, -1]]
UP3 = [[0], [1], [2], [-1]]
WIDE10 = [[0], [1], [2], [3], [4], [-1]]

INPUTS = {
    1: [(WIDE1, C1)], 2: [(POOL1, C1)], 3: [(WIDE2, C2)], 4: [(POOL2, C2)], 5: [(WIDE3, C3)],
    6: [(UP3, C3), (WIDE2, C2)], 7: [(WIDE2, C2)], 8: [(UP2, C2), (WIDE1, C1)], 9: [(WIDE1, C1)],
    10: [(WIDE1, C1)],
}
COLS = {1: 4, 2: 2, 3: 2, 4: 1, 5: 1, 6: 2, 7: 2, 8: 4, 9: 4, 10: 4}
GRADS = {1: WIDE1, 2: WIDE2, 3: WIDE2, 4: WIDE3, 5: WIDE3, 6: WIDE2, 7: WIDE2, 8: WIDE1, 9: WIDE1,
         10: WIDE10}
BACKS = {
    1: [[[0, 1, 2, 3]]], 2: [[[0, 0, 1, 1]]], 3: [[[0, 1]]], 4: [[[0, 0]]], 5: [[[0]]],
    6: [[[0], [1]], [[0, 1]]], 7: [[[0, 1]]], 8: [[[0, 2], [1, 3]], [[0, 1, 2, 3]]], 9: [[[0, 1, 2, 3]]],
    10: [[[0, 1, 2, 3]]],
}


def fwd_rows(k):
    return 3 if k == 10 else 4


def fwd_shape(k):
    per_row = sum(len(segs) for segs, _ in INPUTS[k]) * LANES
    outs = COLS[k] * SHAPES[k][1]
    return (fwd_rows(k) * per_row, outs if k == 10 else 2 * outs)


def back_shape(k):
    return (2 * sum(len(s) for s in BACKS[k]) * LANES, 4 * len(GRADS[k]) * LANES)


def lanes_iota():
    return lax.broadcasted_iota(jnp.int32, (1, LANES), 1)


def dense_rows(p_ref, offset, n):
    row, lane0 = divmod(offset, LANES)
    value = p_ref[row : row + n, :]
    if lane0 == 0:
        return value
    both = jnp.where(lanes_iota() >= lane0, value, p_ref[row + 1 : row + 1 + n, :])
    return pltpu.roll(both, LANES - lane0, 1)


def load_flat(flat_ref, p_ref):
    size = flat_ref.shape[0]
    whole = size // 1024
    many = divisor(whole, 25)

    def step(i, _):
        value = flat_ref[pl.ds(pl.multiple_of(i * many * 1024, 1024), many * 1024)]
        p_ref[pl.ds(pl.multiple_of(i * many * 8, 8), many * 8), :] = value.reshape(many * 8, LANES)

    lax.fori_loop(0, whole // many, step, None)
    rest = size - whole * 1024
    if rest:
        full, part = divmod(rest, LANES)
        if full:
            value = flat_ref[pl.ds(whole * 1024, full * LANES)]
            p_ref[8 * whole : 8 * whole + full, :] = value.reshape(full, LANES)
        if part:
            p_ref[8 * whole + full : 8 * whole + full + 1, 0:part] = flat_ref[pl.ds(size - part, part)].reshape(1, part)


def flat_rows(size):
    return -(-size // 1024) * 8


def turn(value, lanes):
    lanes %= LANES
    return pltpu.roll(value, lanes, 1) if lanes else value


def natural_rows(k, p_ref, nat_ref, natural):
    ci, co = SHAPES[k]
    size = 9 * ci * co
    fill = LANES // co
    dense = dense_rows(p_ref, offset_of(k), size // LANES)
    if fill == 1:
        natural[0 : 9 * ci, :] = dense.astype(bf16)
        return
    for m in range(fill):
        nat_ref[pl.ds(m, size // LANES, stride=fill), :] = turn(dense, -co * m)
    natural[0 : 9 * ci, :] = nat_ref[0 : 9 * ci, :].astype(bf16)


def input_starts(k):
    starts = [0]
    for _, ch in INPUTS[k]:
        starts.append(starts[-1] + ch)
    return starts


def band(k, natural, places, first, ch):
    ci, co = SHAPES[k]
    zero = jnp.zeros((ch, co), bf16)
    parts = []
    for a, c in places:
        if c is not None and 0 <= a <= 2 and 0 <= c <= 2:
            row = (a * 3 + c) * ci + first
            parts.append(natural[row : row + ch, 0:co])
        else:
            parts.append(zero)
    return jnp.concatenate(parts, axis=1)


def forward_weights(k, p_ref, natural, fwd_ref, tiled_ref):
    ci, co = SHAPES[k]
    n = COLS[k]
    pair = (0,) if k == 10 else (0, 1)
    row = 0
    for j in range(fwd_rows(k)):
        for (segs, ch), first in zip(INPUTS[k], input_starts(k)):
            for seg in segs:
                for h in seg:
                    places = [(j - q, None if h is None else h - p + 1) for q in pair for p in range(n)]
                    fwd_ref[row : row + ch, :] = band(k, natural, places, first, ch)
                    row += ch
    bias = dense_rows(p_ref, offset_of(k) + 9 * ci * co, 1)[:, :co]
    tiled_ref[...] = jnp.concatenate([bias] * (n * len(pair)), axis=1)


def backward_weights(k, natural, back_ref):
    row = 0
    for q in (0, 1):
        for (_, ch), backs, first in zip(INPUTS[k], BACKS[k], input_starts(k)):
            for seg in backs:
                for p in seg:
                    places = [
                        (q - j + 2, None if h is None else p - h + 1) for j in range(4) for s in GRADS[k] for h in s
                    ]
                    back_ref[row : row + ch, 0 : len(GRADS[k]) * 4 * LANES] = band(k, natural, places, first, ch)
                    row += ch


def prep_first(p_ref, w_ref, tiled_ref, wide_ref):
    taps = [turn(p_ref[i * C1 // LANES : i * C1 // LANES + 1, :], -i * C1)[:, :C1] for i in range(10)]
    zero = jnp.zeros((1, C1), f32)
    wide_ref[...] = jnp.zeros(wide_ref.shape, f32)
    for m in range(6):
        for j in range(4):
            parts = []
            for q in range(2):
                for p in range(4):
                    a, c = j - q, m - p
                    parts.append(taps[a * 3 + c] if 0 <= a <= 2 and 0 <= c <= 2 else zero)
            wide_ref[4 * m + j : 4 * m + j + 1, :] = jnp.concatenate(parts, axis=1)
    w_ref[...] = wide_ref[...].astype(bf16)
    tiled_ref[...] = jnp.concatenate([taps[9]] * 8, axis=1)


def prep_head(p_ref, hw_ref, hwt_ref, hb_ref, nat_ref):
    wide = 1 + RAYS
    at = offset_of(11)
    for e in range(FINAL):
        nat_ref[e : e + 1, :] = dense_rows(p_ref, at + wide * e, 1)
    w = nat_ref[0:FINAL, :]
    b = dense_rows(p_ref, at + wide * FINAL, 1)
    lane = lanes_iota()
    left = right = 0.0
    for q in range(4):
        chunk = (lane >= RAYS * q) & (lane < RAYS * (q + 1))
        rows = slice(FINAL * q, FINAL * (q + 1))
        hw_ref[rows, 0:LANES] = jnp.where(chunk, turn(w, RAYS * q - 1), 0.0).astype(bf16)
        hw_ref[rows, LANES : 2 * LANES] = jnp.where(lane == RAYS * q, turn(w, RAYS * q), 0.0).astype(bf16)
        left += jnp.where(chunk, turn(b, RAYS * q - 1), 0.0)
        right += jnp.where(lane == RAYS * q, turn(b, RAYS * q), 0.0)
    hwt_ref[...] = hw_ref[...].T
    hb_ref[:, 0:LANES] = left
    hb_ref[:, LANES : 2 * LANES] = right


def prep_kernel(flat_ref, rays_hbm, *refs):
    count = 2 * len(FORWARD) + 3
    outs, scratch = refs[:count], refs[count : 2 * count]
    p_ref, nat, natural, wide, rays_ref, sems, ray_sems = refs[2 * count :]
    patches = rays_hbm.shape[0]
    loads = [pltpu.make_async_copy(rays_hbm.at[p], rays_ref.at[p], ray_sems.at[p]) for p in range(patches)]
    for copy in loads:
        copy.start()
    copies = []

    def send(*places):
        for m in places:
            copy = pltpu.make_async_copy(scratch[m], outs[m], sems.at[m])
            copy.start()
            copies.append(copy)

    last = 2 * len(FORWARD)
    load_flat(flat_ref, p_ref)
    prep_first(p_ref, scratch[last], scratch[last + 1], wide)
    send(last, last + 1)
    for i, k in enumerate(FORWARD):
        natural_rows(k, p_ref, nat, natural)
        forward_weights(k, p_ref, natural, scratch[2 * i], scratch[2 * i + 1])
        send(2 * i, 2 * i + 1)
    for p in range(patches):
        loads[p].wait()
        group_rays(rays_ref, scratch[last + 2], p)
    send(last + 2)
    for copy in copies:
        copy.wait()


def group_rays(rays_ref, out_ref, p):
    rows, rays, cols = rays_ref.shape[1:]
    per = LANES // rays
    quarter = cols // 4
    lane = lanes_iota()
    to = lax.broadcasted_iota(jnp.int32, (cols, cols), 0)
    of = lax.broadcasted_iota(jnp.int32, (cols, cols), 1)
    pick = jnp.where(of == (to % quarter) * 4 + to // quarter, 1.0, 0.0).astype(bf16)
    for r in range(rows // per):
        x = rays_ref[p, per * r : per * (r + 1)].reshape(LANES, cols).astype(f32).astype(bf16)
        turned = lax.dot_general(pick, x, (((1,), (1,)), ((), ())), preferred_element_type=f32)
        parts = [turned[quarter * q : quarter * (q + 1)] for q in range(4)]
        for e in range(per):
            total = turn(parts[0], -rays * e)
            for q in range(1, 4):
                total = jnp.where(lane >= rays * q, turn(parts[q], rays * (q - e)), total)
            out_ref[p, per * r + e] = total.astype(bf16)


def prep(flat, rays):
    count, rows, width, cols = rays.shape
    shapes = []
    for k in FORWARD:
        fs = fwd_shape(k)
        shapes += [jax.ShapeDtypeStruct(fs, bf16), jax.ShapeDtypeStruct((1, fs[1]), f32)]
    shapes += [
        jax.ShapeDtypeStruct((LANES, 2 * LANES), bf16),
        jax.ShapeDtypeStruct((1, 2 * LANES), f32),
        jax.ShapeDtypeStruct((count, rows, cols // 4, 4 * width), bf16),
    ]
    outs = pl.pallas_call(
        prep_kernel,
        out_shape=shapes,
        in_specs=[VMEM, ANY],
        out_specs=[ANY] * len(shapes),
        scratch_shapes=[pltpu.VMEM(v.shape, v.dtype) for v in shapes]
        + [
            pltpu.VMEM((flat_rows(flat.shape[0]), LANES), f32),
            pltpu.VMEM((9 * (C3 + C2), LANES), f32),
            pltpu.VMEM((9 * (C3 + C2), LANES), bf16),
            pltpu.VMEM((LANES, 2 * LANES), f32),
            pltpu.VMEM(rays.shape, jnp.int32),
            pltpu.SemaphoreType.DMA((len(shapes),)),
            pltpu.SemaphoreType.DMA((count,)),
        ],
        name="prep",
        cost_estimate=pl.CostEstimate(flops=10**9, bytes_accessed=2 * 10**7, transcendentals=0),
        compiler_params=pltpu.CompilerParams(vmem_limit_bytes=GRANT),
    )(flat, rays)
    ready = {k: tuple(outs[2 * i : 2 * i + 2]) for i, k in enumerate(FORWARD)}
    ready[0] = tuple(outs[-3:-1])
    return ready, outs[-1]


def tiles_kernel(strips, images_ref, masks_ref, out_ref):
    patches, rows, cols = images_ref.shape
    fold_ = LANES // cols
    high = rows // fold_
    below = out_ref.shape[1] - high
    total = jnp.sum(masks_ref[...].astype(f32).reshape(patches * rows, cols))
    top = jnp.floor(total * (1.0 / 16384.0))
    middle = jnp.floor((total - 16384.0 * top) * (1.0 / 128.0))
    low = total - 16384.0 * top - 128.0 * middle
    lane = lax.broadcasted_iota(jnp.int32, (below, LANES), 1)
    row = lax.broadcasted_iota(jnp.int32, (below, LANES), 0)
    digits = jnp.where(lane == 0, low, jnp.where(lane == 1, middle, jnp.where(lane == 2, top, 0.0)))
    digits = jnp.where(row == 0, digits, 0.0)
    for p in range(patches):
        x = images_ref[p]
        x = jnp.concatenate([x[high * m : high * (m + 1)] for m in range(fold_)], axis=1)
        value = jnp.concatenate([x, digits], axis=0).astype(bf16)
        for s in range(strips):
            out_ref[patches * s + p] = value


def tiles_of(images, masks, strips):
    patches, rows, cols = images.shape
    height = -(-(rows * cols // LANES + 1) // 16) * 16
    return pl.pallas_call(
        functools.partial(tiles_kernel, strips),
        out_shape=jax.ShapeDtypeStruct((strips * patches, height, LANES), bf16),
        in_specs=[VMEM] * 2,
        out_specs=VMEM,
        name="tiles",
    )(images, masks)


def layer_shapes():
    return [(3, 3, 1, C1)] + [(3, 3, *SHAPES[k]) for k in range(1, 11)] + [(FINAL, 1 + RAYS)]


def offset_of(k):
    return sum(math.prod(v) + v[-1] for v in layer_shapes()[:k])


def divisor(count, limit):
    return max(d for d in range(1, min(count, limit) + 1) if count % d == 0)


def mm(a, b):
    return lax.dot_general(a, b, (((1,), (0,)), ((), ())), preferred_element_type=f32)


def mm_t(a, b):
    return lax.dot_general(a, b, (((0,), (0,)), ((), ())), preferred_element_type=f32)


def mm_n(a, b):
    return lax.dot_general(a, b, (((1,), (1,)), ((), ())), preferred_element_type=f32)


def shifted(v):
    zero = jnp.zeros((v.shape[0], 1, v.shape[2]), v.dtype)
    left = jnp.concatenate([zero, v[:, :-1]], axis=1)
    right = jnp.concatenate([v[:, 1:], zero], axis=1)
    return left, right


def lane_of(width=LANES):
    return lax.broadcasted_iota(jnp.int32, (1, 1, width), 2)


def flat2(v):
    return v.reshape(v.shape[0] * v.shape[1], v.shape[2])


def segments(v, three):
    left, right = shifted(v)
    if three:
        return [v, right, left]
    return [v, jnp.where(lane_of() < 64, right, left)]


def rows_of(view):
    return view.reshape(view.shape[0] * 2, *view.shape[2:])


def fours_of(view):
    return view.reshape(view.shape[0] // 2, 2, *view.shape[1:])


def store(view, index, v, three):
    for s, part in enumerate(segments(v, three)):
        view[(*index, s)] = part.astype(bf16)


def lhs_parts(kind, view, base, T, j, repeat):
    segs = range(view.shape[-3])
    if kind == "up":
        at = base + (-1, 0, 0, 1)[j]
        parts = [flat2(view[pl.ds(at, T), s]) for s in segs]
        return parts[:1] + parts if repeat else parts
    p, q = divmod(j + 1, 2)
    return [flat2(view[pl.ds(base + p - 1, T), q, s]) for s in segs]


def lhs_of(sources, r, T, repeat):
    parts = []
    for j in range(4):
        for kind, view, off in sources:
            parts += lhs_parts(kind, view, r + off, T, j, repeat)
    return jnp.concatenate(parts, axis=1)


def each_block(count, limit, block):
    T = -(-count // -(-count // limit))
    steps = -(-count // T)

    def step(i, _):
        block(jnp.minimum(i * T, count - T), T)

    lax.fori_loop(0, steps, step, None)


def each_part(count, limit, block):
    T = -(-count // -(-count // limit))
    whole = count // T

    def step(i, _):
        block(i * T, T)

    lax.fori_loop(0, whole, step, None)
    if count % T:
        block(whole * T, count % T)


def clear(view, start, stop):
    def step(i, _):
        view[i] = jnp.zeros(view.shape[1:], view.dtype)

    lax.fori_loop(start, stop, step, None)


def clear_outside(view, count, pad, lo, hi):
    clear(view, 0, pad + jnp.clip(lo, 0, count))
    clear(view, pad + jnp.clip(hi, 0, count), count + 2 * pad)


def silu(z):
    s = 0.5 * jnp.tanh(0.5 * z) + 0.5
    a = z * s
    return a, s + a - a * s


SLOPE_STEP = 1.0 / 26000.0
SLOPE_LOW = 0.125


def pack_slope(v):
    return (v * 26000.0 + (26000.0 * SLOPE_LOW + 0.5)).astype(jnp.int32).astype(jnp.int16)


def unpack_slope(v):
    return v.astype(jnp.int32).astype(f32) * SLOPE_STEP - SLOPE_LOW


def split_pair(v, T):
    g = v.shape[0] // T
    half = v.shape[1] // 2
    return [v[:, half * q : half * (q + 1)].reshape(T, g, half) for q in range(2)]


def pooled(x, level):
    lane = lane_of()
    if level == 1:
        near = x + pltpu.roll(x, LANES - C1, 2)
        far = x + pltpu.roll(x, C1, 2)
        left, right = shifted(far)
        return [jnp.where((lane & 32) == 0, near, jnp.where(lane < 64, right, left))]
    y = x + pltpu.roll(x, C2, 2)
    left, right = shifted(y)
    return [jnp.where(lane < 64, y, left), right]


def conv(sources, w, bias, out, slopes, count, lo, valid, three=False, pool=None, limit=18):
    def block(r, T):
        a, slope = silu(mm(lhs_of(sources, r, T, True), w[...]) + bias[...])
        rows, slope = split_pair(a, T), split_pair(slope, T)
        for q in range(2):
            slopes[pl.ds(r, T), q] = pack_slope(slope[q])
            store(out, (pl.ds(r + 1, T), q), rows[q], three)
        if pool:
            x = sum(v.astype(bf16).astype(f32) for v in rows) * 0.25
            for s, part in enumerate(pooled(x, pool[1])):
                pool[0][pl.ds(r + 2, T), s] = part.astype(bf16)

    each_block(count, limit, block)
    clear_outside(out, count, 1, valid[0] - lo, valid[1] - lo)
    if pool:
        clear_outside(pool[0], count, 2, valid[0] - lo, valid[1] - lo)


def first_conv(tiling, own, strip, valid, got, w_ref, bias_ref, out, slopes, xcols, x_ref, xt_ref, v_ref):
    hi, strips, across, per, width = tiling
    count = own // 2 + 22
    rows = own + 2 * HALO
    reach = -(-HALO // per)
    wide = width // across
    high = per * wide // LANES
    x_ref[...] = jnp.zeros(x_ref.shape, f32)
    for d in range(-reach, hi + reach):
        tile = strip * hi + d
        start = HALO + d * per
        first, last = max(0, -start), min(per, rows - start)

        @pl.when((tile >= 0) & (tile < strips * hi))
        def _():
            parts = [got[tile * across + c].astype(f32)[:high] for c in range(across)]
            here = [[v[:, wide * m : wide * (m + 1)] for v in parts] for m in range(LANES // wide)]
            value = jnp.concatenate([jnp.concatenate(v, axis=1) for v in here], axis=0)
            x_ref[start + first : start + last, :] = value[first:last]

    groups = width // 4
    xt_ref[0:EDGE] = jnp.zeros((EDGE, LANES), f32)
    xt_ref[EDGE + width : 2 * EDGE + width] = jnp.zeros((EDGE, LANES), f32)
    xt_ref[EDGE : EDGE + width] = x_ref[...].T
    for m in range(6):
        v_ref[m] = xt_ref[pl.ds(EDGE + m - 1, groups, stride=4), :]
    lane = lax.broadcasted_iota(jnp.int32, (1, LANES), 1)
    many = divisor(count, 6)

    def gather(i, _):
        for u in range(many):
            at = i * many + u
            total = jnp.zeros((groups, LANES), f32)
            for m in range(6):
                turned = pltpu.roll(v_ref[m], 4 * m + LANES - (2 * at + 1), 1)
                total = jnp.where((lane >= 4 * m) & (lane < 4 * m + 4), turned, total)
            xcols[at] = total.astype(bf16)

    lax.fori_loop(0, count // many, gather, None)
    def block(r, T):
        a, slope = silu(mm(flat2(xcols[pl.ds(r, T)]), w_ref[...]) + bias_ref[...])
        rows_, slope = split_pair(a, T), split_pair(slope, T)
        for q in range(2):
            slopes[pl.ds(r, T), q] = pack_slope(slope[q])
            store(out, (pl.ds(r + 1, T), q), rows_[q], False)

    each_block(count, 18, block)
    clear_outside(out, count, 1, valid[0] + 11, valid[1] + 11)


def act_shapes(own, groups):
    h, h2, h3 = own // 2, own // 4, own // 8
    pairs = dict(
        a0=(h + 24, 2), s1=(h + 22, 2), p1=(h2 + 12, 1), a2=(h2 + 12, 2), s2=(h2 + 10, 2), p2=(h3 + 6, 2),
        a4=(h3 + 6, 3), t3=(h3 + 4, 3), a6=(h2 + 6, 2), t2=(h2 + 4, 2), a8=(h + 4, 2), a9=(h + 4, 2),
    )
    shapes = {k: (n, 2, segs, groups, LANES) for k, (n, segs) in pairs.items()}
    shapes["xc"] = (h + 22, groups, LANES)
    return shapes


def slope_shapes(own, groups):
    h, h2, h3 = own // 2, own // 4, own // 8
    counts = [h + 22, h + 20, h2 + 10, h2 + 8, h3 + 4, h3 + 2, h2 + 4, h2 + 2, h + 2, h + 2]
    return {f"sl{k}": (n, 2, groups, LANES) for k, n in enumerate(counts)}


def grad_shapes(own, groups):
    h, h2, h3 = own // 2, own // 4, own // 8
    pairs = {
        10: (h + 4, 6), 9: (h + 6, 2), 8: (h + 6, 2), 7: (h2 + 6, 2), 6: (h2 + 8, 2), 5: (h3 + 6, 3),
        4: (h3 + 8, 3), 3: (h2 + 12, 2), 2: (h2 + 14, 2), 1: (h + 24, 2), 0: (h + 22, 1),
    }
    return {f"g{k}": (n, 2, segs, groups, LANES) for k, (n, segs) in pairs.items()}


def loss_scales(got, tiling, pixels, scal_ref):
    _, _, across, per, width = tiling
    high = per * (width // across) // LANES
    digits = jnp.sum(got[...].astype(f32), axis=0)[high : high + 1, :]
    lane = lanes_iota()
    digits = jnp.where(lane == 0, digits, jnp.where(lane == 1, 128.0 * digits, 16384.0 * digits))
    fg = jnp.sum(jnp.where(lane < 3, digits, 0.0), axis=1, keepdims=True) * jnp.ones((1, LANES), f32)
    scal_ref[0:1] = 0.5 / fg
    scal_ref[1:2] = 0.5 / (pixels - fg)
    scal_ref[2:3] = 1.0 / (fg * RAYS)
    scal_ref[3:4] = fg


def forward_kernel(cfg, sc, got, w0, b0, *refs):
    own, tiling = cfg["own"], cfg["tiling"]
    h, h2, h3 = own // 2, own // 4, own // 8
    refs = list(refs)
    take = lambda m: [refs.pop(0) for _ in range(m)]
    w_hbm, bias = take(9), take(9)
    names = list(cfg["outs"])
    outs = dict(zip(names, take(len(names))))
    scal_ref = take(1)[0]
    here = dict(zip(names, take(len(names))))
    w_vmem = take(9)
    x_ref, xt_ref, v_ref, w_sem, out_sem = refs
    fetch = {}
    for i, k in enumerate(FORWARD):
        fetch[k] = pltpu.make_async_copy(w_hbm[i], w_vmem[i], w_sem.at[i])
        fetch[k].start()
    sent = []

    def send(*keys):
        for key in keys:
            copy = pltpu.make_async_copy(here[key], outs[key], out_sem.at[names.index(key)])
            copy.start()
            sent.append(copy)

    v1, v2, v3 = [(sc[2 * i], sc[2 * i + 1]) for i in range(3)]
    loss_scales(got, tiling, cfg["pixels"], scal_ref)
    first_conv(tiling, own, sc[6], v1, got, w0, b0, here["a0"], here["sl0"], here["xc"],
               x_ref, xt_ref, v_ref)
    send("a0", "sl0", "xc")

    def layer(k, out, sources, count, lo, valid, three=False, pool=None):
        fetch[k].wait()
        conv(sources, w_vmem[k - 1], bias[k - 1], here[out], here[f"sl{k}"], count, lo, valid, three, pool,
             13 if k in (6, 8) else 18)
        send(out, f"sl{k}")

    layer(1, "s1", [("pair", here["a0"], 2)], h + 20, -10, v1, pool=(rows_of(here["p1"]), 1))
    send("p1")
    layer(2, "a2", [("pair", here["p1"], 1)], h2 + 10, -5, v2)
    layer(3, "s2", [("pair", here["a2"], 2)], h2 + 8, -4, v2, pool=(rows_of(here["p2"]), 2))
    send("p2")
    layer(4, "a4", [("pair", here["p2"], 1)], h3 + 4, -2, v3, True)
    layer(5, "t3", [("pair", here["a4"], 2)], h3 + 2, -1, v3, True)
    layer(6, "a6", [("up", rows_of(here["t3"]), 2), ("pair", here["s2"], 3)], h2 + 4, -2, v2)
    layer(7, "t2", [("pair", here["a6"], 2)], h2 + 2, -1, v2)
    layer(8, "a8", [("up", rows_of(here["t2"]), 3), ("pair", here["s1"], 10)], h + 2, -1, v1)
    layer(9, "a9", [("pair", here["a8"], 1)], h + 2, -1, v1)
    for copy in sent:
        copy.wait()


def forward(sc, got, ready, own, tiling, pixels):
    groups = tiling[-1] // 4
    shapes = {k: jax.ShapeDtypeStruct(v, bf16) for k, v in act_shapes(own, groups).items()}
    shapes |= {k: jax.ShapeDtypeStruct(v, jnp.int16) for k, v in slope_shapes(own, groups).items()}
    weights = [ready[k][0] for k in FORWARD]
    biases = [ready[k][1] for k in FORWARD]
    width = tiling[-1]
    outs = pl.pallas_call(
        functools.partial(forward_kernel, dict(own=own, tiling=tiling, outs=tuple(shapes), pixels=float(pixels))),
        out_shape=[*shapes.values(), jax.ShapeDtypeStruct((8, LANES), f32)],
        in_specs=[SMEM] + [VMEM] * 3 + [ANY] * 9 + [VMEM] * 9,
        out_specs=[ANY] * len(shapes) + [VMEM],
        scratch_shapes=[pltpu.VMEM(v.shape, v.dtype) for v in shapes.values()]
        + [pltpu.VMEM(w.shape, bf16) for w in weights]
        + [
            pltpu.VMEM((LANES, width), f32),
            pltpu.VMEM((width + 2 * EDGE, LANES), f32),
            pltpu.VMEM((6, groups, LANES), f32),
            pltpu.SemaphoreType.DMA((9,)),
            pltpu.SemaphoreType.DMA((len(shapes),)),
        ],
        name="forward",
        cost_estimate=pl.CostEstimate(flops=2 * 10**10, bytes_accessed=5 * 10**7, transcendentals=10**7),
        compiler_params=pltpu.CompilerParams(vmem_limit_bytes=GRANT),
    )(sc, got, *ready[0], *weights, *biases)
    return dict(zip(shapes, outs)), outs[-1]


def sum_back(k, acc):
    ci, co = SHAPES[k]
    n = COLS[k]
    pieces = {}
    for a in range(3):
        value = acc(a)
        base = start = 0
        for segs, ch in INPUTS[k]:
            if segs is UP2:
                unique = [[(0, 1), (2, 3)], [(4,), (-1,)]]
            elif segs is UP3:
                unique = [[(0, 1)], [(2,)], [(-1,)]]
            else:
                unique = [[() if c is None else (c,) for c in seg] for seg in segs]
            uses = {}
            for seg in unique:
                for columns in seg:
                    for col in columns:
                        for p in range(n):
                            c = col - p + 1
                            if 0 <= c <= 2:
                                uses.setdefault(c, []).append((base, p))
                    base += ch
            for c, places in uses.items():
                total = None
                for row, p in places:
                    piece = value[row : row + ch, p * co : (p + 1) * co]
                    total = piece if total is None else total + piece
                pieces[(a * 3 + c) * ci + start] = total
            start += ch
    return pieces


def place(out, value, offset):
    out, base = out
    row, lane0 = divmod(offset - base * LANES, LANES)
    n = value.shape[0]
    if lane0 == 0:
        out[row : row + n, :] += value
        return
    lane = lax.broadcasted_iota(jnp.int32, (1, LANES), 1)
    turned = pltpu.roll(value, lane0, 1)
    out[row : row + n, :] += jnp.where(lane >= lane0, turned, 0.0)
    out[row + 1 : row + 1 + n, :] += jnp.where(lane < lane0, turned, 0.0)


def fold(row, co):
    total = row[:, 0:LANES]
    for m in range(1, row.shape[1] // LANES):
        total = total + row[:, LANES * m : LANES * (m + 1)]
    width = LANES
    while width > co:
        width //= 2
        total = total + pltpu.roll(total, width, 1)
    lane = lax.broadcasted_iota(jnp.int32, (1, LANES), 1)
    return jnp.where(lane < co, total, 0.0)


def place_layer(k, pieces, db, nat, out):
    ci, co = SHAPES[k]
    n = 9 * ci * co // LANES
    fill = LANES // co
    for row, total in pieces.items():
        nat[row : row + total.shape[0], 0:co] = total
    if fill == 1:
        value = nat[0:n, :]
    else:
        value = jnp.concatenate([nat[pl.ds(m, n, stride=fill), :][:, :co] for m in range(fill)], axis=1)
    place(out, value, offset_of(k))
    place(out, fold(db, co), offset_of(k) + 9 * ci * co)


def head_part(own, scal, x, w, bias, hw, hwt, hb, rays, grad, acc, dhead, nat, out):
    _, cols, per = rays.shape[:3]
    x, grad = rows_of(x), rows_of(grad)
    groups = x.shape[2]
    T = divisor(math.gcd(own, per), 8)
    M = T * groups
    fg_scale, bg_scale, ray_scale_ = scal[0:1], scal[1:2], scal[2:3]
    lane = lax.broadcasted_iota(jnp.int32, (1, LANES), 1)
    is_logit = (lane & 31) == 0
    ones = jnp.ones((8, M), bf16)
    acc[...] = jnp.zeros(acc.shape, f32)
    dhead[...] = jnp.zeros(dhead.shape, f32)

    def block(i, carry):
        db, dbh, fg_loss, bg_loss, ray_loss = carry
        r = i * T
        slabs = [
            jnp.concatenate([flat2(x[pl.ds(r + 4 + d, T), s]) for s in range(2)], axis=1) for d in (-1, 0, 1)
        ]
        a, slope = silu(mm(jnp.concatenate(slabs, axis=1), w[...]) + bias[...])
        feat = a.astype(bf16)
        head = mm(feat, hw[...]) + hb[...]
        dist, logit = head[:, :LANES], head[:, LANES:]
        part, first = r // per, r % per
        ray = jnp.concatenate([rays[part, c, pl.ds(first, T)] for c in range(cols)], axis=1)
        ray = flat2(ray.astype(f32))
        y = jnp.where(ray > 0.0, 1.0, 0.0)
        diff = dist - ray * (1.0 / ray_scale)
        smooth = jnp.sqrt(diff * diff + 1.0)
        g_dist = diff / smooth * (y * ray_scale_)
        cross = jnp.maximum(logit, 0.0) - logit * y + jnp.log(1.0 + jnp.exp(-jnp.abs(logit)))
        cross = jnp.where(is_logit, cross, 0.0)
        sig = 1.0 / (1.0 + jnp.exp(-logit))
        g_logit = jnp.where(is_logit, (sig - y) * (y * fg_scale + (1.0 - y) * bg_scale), 0.0)
        fg_loss += jnp.sum((cross * y).reshape(M // 8, 8, LANES), axis=0)
        bg_loss += jnp.sum((cross * (1.0 - y)).reshape(M // 8, 8, LANES), axis=0)
        ray_loss += jnp.sum((smooth * y).reshape(M // 8, 8, LANES), axis=0)
        g_head = jnp.concatenate([g_dist, g_logit], axis=1).astype(bf16)
        dhead[...] += mm_t(feat, g_head)
        gz = mm(g_head, hwt[...]) * slope
        center = gz.astype(bf16)
        for a_ in range(3):
            acc[a_] += mm_t(slabs[a_], center)
        for s in range(4):
            grad[pl.ds(r + 4, T), s] = center[:, LANES * s : LANES * (s + 1)].reshape(T, groups, LANES)
        left = shifted(gz[:, 3 * LANES :].reshape(T, groups, LANES))[0]
        right = shifted(gz[:, :LANES].reshape(T, groups, LANES))[1]
        grad[pl.ds(r + 4, T), 4] = right.astype(bf16)
        grad[pl.ds(r + 4, T), 5] = left.astype(bf16)
        return db + mm(ones, center), dbh + mm(ones, g_head), fg_loss, bg_loss, ray_loss

    zero = jnp.zeros((8, LANES), f32)
    start = (jnp.zeros((8, 4 * FINAL), f32), jnp.zeros((8, 2 * LANES), f32), zero, zero, zero)
    db, dbh, *losses = lax.fori_loop(0, own // T, block, start)
    clear(grad, 0, 4)
    clear(grad, own + 4, own + 8)
    place_layer(10, sum_back(10, lambda a: acc[a]), db[0:1], nat, out)
    both = jnp.zeros((FINAL, LANES), f32)
    for q in range(4):
        rows = dhead[FINAL * q : FINAL * (q + 1), :]
        piece, first = rows[:, :LANES], rows[:, LANES:]
        if q:
            piece = pltpu.roll(piece, LANES - RAYS * q, 1)
            first = pltpu.roll(first, LANES - RAYS * q, 1)
        both += jnp.where(lane == 0, first, pltpu.roll(piece, 1, 1))
    wide = 1 + RAYS
    nat[0:FINAL, :] = jnp.where(lane < wide, both, 0.0)
    at = offset_of(11)
    flat, base = out
    for e in range(FINAL):
        row, lane0 = divmod(at - base * LANES + wide * e, LANES)
        value = pltpu.roll(nat[e : e + 1, :], lane0, 1) if lane0 else nat[e : e + 1, :]
        if lane0 + wide <= LANES:
            flat[row : row + 1, :] += value
        else:
            flat[row : row + 1, :] += jnp.where(lane >= lane0, value, 0.0)
            flat[row + 1 : row + 2, :] += jnp.where(lane < lane0, value, 0.0)
    dist_sum, logit_sum = fold(dbh[0:1, :LANES], RAYS), fold(dbh[0:1, LANES:], RAYS)
    value = jnp.where(lane == 0, logit_sum, pltpu.roll(dist_sum, 1, 1))
    place(out, jnp.where(lane < wide, value, 0.0), at + FINAL * wide)
    terms = jnp.zeros((1, LANES), f32)
    for m, part in enumerate(losses):
        terms = jnp.where(lane == m, jnp.sum(part), terms)
    place(out, terms, offset_of(12))


def weight_grad(k, sources, grad, count, acc, nat, out, limit=18):
    rows = sum(v.shape[-3] for _, v, _ in sources) * LANES
    groups = grad.shape[3]
    acc[...] = jnp.zeros(acc.shape, f32)

    def block(r, T, db):
        g = jnp.concatenate([flat2(grad[pl.ds(r + 2, T), q, 0]) for q in range(2)], axis=1)
        for j in range(4):
            parts = []
            for kind, view, off in sources:
                parts += lhs_parts(kind, view, r + off, T, j, False)
            acc[j, 0:rows] += mm_t(jnp.concatenate(parts, axis=1), g)
        return db + mm(jnp.ones((8, T * groups), bf16), g)

    T = -(-count // -(-count // limit))
    whole = count // T
    db = lax.fori_loop(0, whole, lambda i, db: block(i * T, T, db), jnp.zeros((8, 2 * LANES), f32))
    if count % T:
        db = block(whole * T, count % T, db)
    pieces = sum_back(k, lambda a: acc[a, 0:rows, 0:LANES] + acc[a + 1, 0:rows, LANES : 2 * LANES])
    place_layer(k, pieces, db[0:1], nat, out)


def input_grad(mode, grad, goff, w, slopes, out, count, valid, lo, three=False, extra=None, side=None, limit=18):
    def block(r, T):
        groups = grad.shape[3]
        acc = mm_n(lhs_of([("pair", grad, goff)], r, T, False), w[...])
        if mode == "join":
            parts = [acc[:, LANES * m : LANES * (m + 1)].reshape(T, groups, LANES) for m in range(6)]
            gz = ((parts[0] + parts[1]) + (parts[3] + parts[4])) * unpack_slope(slopes[pl.ds(r, T)])
            store(out, (pl.ds(r + 4, T),), gz, three)
            for q in range(2):
                side[0][pl.ds(r + side[1], T), q] = parts[2 + 3 * q]
            return
        vals = split_pair(acc, T)
        for q in range(2):
            if mode == "pool":
                for e in range(2):
                    total = vals[q] * 0.25 + extra[pl.ds(r, T), q, e]
                    store(out, (pl.ds(r + 1, T), q, e), total * unpack_slope(slopes[pl.ds(r, T), q, e]), three)
                continue
            gz = vals[q] * unpack_slope(slopes[pl.ds(r, T), q])
            if mode == "last":
                out[pl.ds(r, T), q, 0] = gz.astype(bf16)
            else:
                store(out, (pl.ds(r + 2, T), q), gz, three)

    if mode == "join":
        side[0][...] = jnp.zeros(side[0].shape, f32)
    each_block(count, limit, block)
    low, high = valid[0] - lo, valid[1] - lo
    if mode == "plain":
        clear_outside(out, count, 2, low, high)
    elif mode == "last":
        clear_outside(out, count, 0, low, high)
    elif mode == "join":
        clear_outside(out, count, 4, low, high)
    else:
        clear_outside(out, count, 1, low // 2, high // 2)


def first_grad(grad, xcols, count, out, tmp):
    groups = grad.shape[3]

    def block(r, T, carry):
        g = jnp.concatenate([flat2(grad[pl.ds(r, T), q, 0]) for q in range(2)], axis=1)
        return carry[0] + mm_t(flat2(xcols[pl.ds(r, T)]), g), carry[1] + mm(jnp.ones((8, T * groups), bf16), g)

    T = divisor(count, 18)
    start = (jnp.zeros((LANES, 2 * LANES), f32), jnp.zeros((8, 2 * LANES), f32))
    dw, db = lax.fori_loop(0, count // T, lambda i, c: block(i * T, T, c), start)
    tmp[...] = jnp.zeros(tmp.shape, f32)
    for a in range(3):
        for c in range(3):
            total = None
            for q in range(2):
                for p in range(4):
                    m, j = p + c, a + q
                    at = (q * 4 + p) * C1
                    piece = dw[4 * m + j : 4 * m + j + 1, at : at + C1]
                    total = piece if total is None else total + piece
            row, at = divmod((a * 3 + c) * C1, LANES)
            tmp[row : row + 1, at : at + C1] = total
    place(out, tmp[...], 0)
    place(out, fold(db[0:1], C1), 9 * C1)


def arena_plan(own, groups, places):
    sizes = act_shapes(own, groups) | grad_shapes(own, groups)
    tiles = {k: math.prod(v[:-2]) for k, v in sizes.items()}
    at, top = {}, 0
    for lists in places:
        ends = []
        for names in lists:
            spot = top
            for name in names:
                at[name] = spot
                spot += tiles[name]
            ends.append(spot)
        top = max(ends)
    return sizes, tiles, at, top


SLOTS = {k: "x" if k in (8, 6) else "y" for k in SHAPES}
DEEP = dict(
    acts=("a9", "a8", "t2", "s1", "a6", "t3", "s2", "a4", "p2"),
    slopes=("sl9", "sl8", "sl7", "sl6", "sl5", "sl4"),
    layers=(10, 9, 8, 7, 6, 5),
    places=([["g10"]], [["g9"], ["g7"], ["g5"]], [["g8"], ["g6"], ["g4"]], [["a9", "a8"]], [["t2", "s1"]],
            [["a6", "t3", "s2", "a4", "p2"]]),
)
MIDDLE = dict(
    acts=("a2", "p1"),
    slopes=("sl3", "sl2", "sl1"),
    layers=(4, 3, 2),
    places=([["g4"]], [["g3"]], [["g2"]], [["g1"]], [["a2", "p1"]]),
)
FIRST = dict(
    acts=("a0", "xc"),
    slopes=("sl0",),
    layers=(1,),
    places=([["g1"]], [["g0"]], [["a0", "xc"]]),
)
SPLIT = 504
SHARE = 256


def split_rows():
    high = offset_of(12) + 3 - SPLIT * LANES
    return -(-high // (LANES * SHARE)) * SHARE, -(-offset_of(4) // (LANES * SHARE)) * SHARE


class Part:
    def __init__(self, stage, plan, arena, slopes, slots, hbm, sems, p_ref, nat, natural):
        self.stage, self.arena, self.slopes, self.hbm, self.sems = stage, arena, slopes, hbm, sems
        self.sizes, self.tiles, self.at, _ = plan
        self.slots, self.p_ref, self.nat, self.natural = slots, p_ref, nat, natural
        self.copies = {}

    def view(self, name):
        return self.arena.at[pl.ds(self.at[name], self.tiles[name])].reshape(*self.sizes[name])

    def fetch(self, key, target=None):
        if target is None:
            target = self.slopes[key] if key in self.slopes else self.view(key)
        copy = pltpu.make_async_copy(self.hbm[key], target, self.sems.at[list(self.hbm).index(key)])
        copy.start()
        self.copies[key] = copy

    def need(self, *keys):
        for key in keys:
            self.copies[key].wait()

    def weight(self, k):
        rows, lanes = back_shape(k)
        ref = self.slots[SLOTS[k]].at[pl.ds(0, rows), pl.ds(0, lanes)]
        natural_rows(k, self.p_ref, self.nat, self.natural)
        backward_weights(k, self.natural, ref)
        return ref


def deep_kernel(cfg, sc, scal, flat_ref, *refs):
    own, groups = cfg["own"], cfg["groups"]
    h, h2, h3 = own // 2, own // 4, own // 8
    refs = list(refs)
    take = lambda m: [refs.pop(0) for _ in range(m)]
    names = DEEP["acts"] + DEEP["slopes"] + ("rays",)
    hbm = dict(zip(names, take(len(names))))
    keep_hbm, send_hbm, g4_hbm, gs1_hbm, gs2_hbm = take(5)
    arena = take(1)[0]
    slopes = dict(zip(DEEP["slopes"], take(len(DEEP["slopes"]))))
    slots = dict(zip("yx", take(2)))
    p_ref, w10, bias10, hw, hwt, hb, rays, gs1, gs2, acc, acc10, dhead, nat, natural, flat, sems, out_sems = refs
    part = Part(DEEP, cfg["plan"], arena, slopes, slots, hbm, sems, p_ref, nat, natural)
    view, need = part.view, part.need
    part.fetch("a9")
    part.fetch("rays", rays)
    for key in ("sl9", "a8", "sl8", "t2", "s1", "sl7", "a6", "sl6", "t3", "s2", "sl5", "a4", "sl4", "p2"):
        part.fetch(key)
    out = (flat, SPLIT)
    flat[...] = jnp.zeros(flat.shape, f32)
    v1, v2, v3 = [(sc[2 * i], sc[2 * i + 1]) for i in range(3)]
    load_flat(flat_ref, p_ref)
    natural_rows(10, p_ref, nat, natural)
    forward_weights(10, p_ref, natural, w10, bias10)
    prep_head(p_ref, hw, hwt, hb, nat)
    need("a9", "rays")
    head_part(own, scal, view("a9"), w10, bias10, hw, hwt, hb, rays, view("g10"), acc10, dhead, nat, out)

    weight = part.weight(10)
    need("sl9")
    input_grad("plain", view("g10"), 1, weight, slopes["sl9"], view("g9"), h + 2, v1, -1, limit=12)

    need("a8", "sl8")
    weight_grad(9, [("pair", view("a8"), 1)], view("g9"), h + 2, acc, nat, out)
    weight = part.weight(9)
    input_grad("plain", view("g9"), 2, weight, slopes["sl8"], view("g8"), h + 2, v1, -1)

    need("t2", "s1", "sl7")
    weight_grad(8, [("up", rows_of(view("t2")), 3), ("pair", view("s1"), 10)], view("g8"), h + 2, acc, nat, out)
    weight = part.weight(8)
    input_grad("join", view("g8"), 1, weight, rows_of(slopes["sl7"]), rows_of(view("g7")), h + 4, v1, -2,
               side=(gs1, 8))
    outs = [pltpu.make_async_copy(gs1, gs1_hbm, out_sems.at[0])]
    outs[0].start()

    need("a6", "sl6")
    weight_grad(7, [("pair", view("a6"), 2)], view("g7"), h2 + 2, acc, nat, out)
    weight = part.weight(7)
    input_grad("plain", view("g7"), 1, weight, slopes["sl6"], view("g6"), h2 + 4, v2, -2)

    need("t3", "s2", "sl5")
    weight_grad(6, [("up", rows_of(view("t3")), 2), ("pair", view("s2"), 3)], view("g6"), h2 + 4, acc, nat, out)
    weight = part.weight(6)
    input_grad("join", view("g6"), 2, weight, rows_of(slopes["sl5"]), rows_of(view("g5")), h2 + 4, v2, -2,
               three=True, side=(gs2, 2))
    outs.append(pltpu.make_async_copy(gs2, gs2_hbm, out_sems.at[1]))
    outs[-1].start()

    need("a4", "sl4")
    weight_grad(5, [("pair", view("a4"), 2)], view("g5"), h3 + 2, acc, nat, out)
    weight = part.weight(5)
    input_grad("plain", view("g5"), 1, weight, slopes["sl4"], view("g4"), h3 + 4, v3, -2, three=True)

    outs.append(pltpu.make_async_copy(view("g4"), g4_hbm, out_sems.at[2]))
    outs[-1].start()

    need("p2")
    weight_grad(4, [("pair", view("p2"), 1)], view("g4"), h3 + 4, acc, nat, out)
    half = flat.shape[0] // 2
    for m, (core, target) in enumerate(((sc[7], keep_hbm), (1 - sc[7], send_hbm))):
        rows = pl.ds(pl.multiple_of(core * half, 8), half)
        outs.append(pltpu.make_async_copy(flat.at[rows], target, out_sems.at[3 + m]))
        outs[-1].start()
    for copy in outs:
        copy.wait()


def stage_scratch(stage, own, groups, plan, params):
    def slot(s):
        return tuple(max([back_shape(k)[d] for k in stage["layers"] if SLOTS[k] == s] + [8]) for d in (0, 1))

    slopes = slope_shapes(own, groups)
    return (
        [pltpu.VMEM((plan[3], groups, LANES), bf16)]
        + [pltpu.VMEM(slopes[k], jnp.int16) for k in stage["slopes"]]
        + [pltpu.VMEM(slot(s), bf16) for s in "yx" if any(SLOTS[k] == s for k in stage["layers"])]
        + [pltpu.VMEM((flat_rows(params.shape[0]), LANES), f32)]
    )


def deep(sc, scal, params, kept, rays, own, groups):
    plan = arena_plan(own, groups, DEEP["places"])
    h, h2 = own // 2, own // 4
    args = [kept[k] for k in DEEP["acts"] + DEEP["slopes"]] + [rays]
    rows = split_rows()[0]
    gs1, gs2 = (h + 20, 2, groups, LANES), (h2 + 8, 2, groups, LANES)
    return pl.pallas_call(
        functools.partial(deep_kernel, dict(own=own, groups=groups, plan=plan)),
        out_shape=[
            jax.ShapeDtypeStruct((rows // 2, LANES), f32),
            jax.ShapeDtypeStruct((rows // 2, LANES), f32),
            jax.ShapeDtypeStruct(grad_shapes(own, groups)["g4"], bf16),
            jax.ShapeDtypeStruct(gs1, f32),
            jax.ShapeDtypeStruct(gs2, f32),
        ],
        in_specs=[SMEM, VMEM, VMEM] + [ANY] * len(args),
        out_specs=[ANY] * 5,
        scratch_shapes=stage_scratch(DEEP, own, groups, plan, params)
        + [
            pltpu.VMEM(fwd_shape(10), bf16),
            pltpu.VMEM((1, fwd_shape(10)[1]), f32),
            pltpu.VMEM((4 * FINAL, 2 * LANES), bf16),
            pltpu.VMEM((2 * LANES, 4 * FINAL), bf16),
            pltpu.VMEM((1, 2 * LANES), f32),
            pltpu.VMEM(rays.shape, bf16),
            pltpu.VMEM(gs1, f32),
            pltpu.VMEM(gs2, f32),
            pltpu.VMEM((4, 5 * LANES, 2 * LANES), f32),
            pltpu.VMEM((3, 2 * LANES, 4 * FINAL), f32),
            pltpu.VMEM((4 * FINAL, 2 * LANES), f32),
            pltpu.VMEM((9 * (C3 + C2), LANES), f32),
            pltpu.VMEM((9 * (C3 + C2), LANES), bf16),
            pltpu.VMEM((rows, LANES), f32),
            pltpu.SemaphoreType.DMA((len(args),)),
            pltpu.SemaphoreType.DMA((5,)),
        ],
        name="deep",
        cost_estimate=pl.CostEstimate(flops=5 * 10**10, bytes_accessed=5 * 10**7, transcendentals=10**7),
        compiler_params=pltpu.CompilerParams(vmem_limit_bytes=GRANT),
    )(sc, scal, params, *args)


def middle_kernel(cfg, sc, flat_ref, *refs):
    own, groups = cfg["own"], cfg["groups"]
    h, h2, h3 = own // 2, own // 4, own // 8
    refs = list(refs)
    take = lambda m: [refs.pop(0) for _ in range(m)]
    names = MIDDLE["acts"] + MIDDLE["slopes"] + ("g4", "gs1", "gs2")
    hbm = dict(zip(names, take(len(names))))
    flat, g1_hbm, arena = take(3)
    slopes = dict(zip(MIDDLE["slopes"], take(len(MIDDLE["slopes"]))))
    slots = dict(zip("y", take(1)))
    p_ref, gs1, gs2, acc, nat, natural, sems, out_sem = refs
    part = Part(MIDDLE, cfg["plan"], arena, slopes, slots, hbm, sems, p_ref, nat, natural)
    view, need = part.view, part.need
    for key in ("g4", "sl3"):
        part.fetch(key)
    part.fetch("gs2", gs2)
    for key in ("a2", "sl2", "p1", "sl1"):
        part.fetch(key)
    part.fetch("gs1", gs1)
    out = (flat, 0)
    flat[...] = jnp.zeros(flat.shape, f32)
    load_flat(flat_ref, p_ref)
    v1, v2 = [(sc[2 * i], sc[2 * i + 1]) for i in range(2)]
    weight = part.weight(4)
    need("g4", "sl3", "gs2")
    input_grad("pool", view("g4"), 2, weight, fours_of(slopes["sl3"]), fours_of(view("g3")), h3 + 4, v2, -4,
               extra=fours_of(gs2))

    need("a2", "sl2")
    weight_grad(3, [("pair", view("a2"), 2)], view("g3"), h2 + 8, acc, nat, out)
    weight = part.weight(3)
    input_grad("plain", view("g3"), 1, weight, slopes["sl2"], view("g2"), h2 + 10, v2, -5)

    need("p1", "sl1", "gs1")
    weight = part.weight(2)
    input_grad("pool", view("g2"), 2, weight, fours_of(slopes["sl1"]), fours_of(view("g1")), h2 + 10, v1, -10,
               extra=fours_of(gs1), limit=13)
    copy = pltpu.make_async_copy(view("g1"), g1_hbm, out_sem)
    copy.start()
    weight_grad(2, [("pair", view("p1"), 1)], view("g2"), h2 + 10, acc, nat, out)
    copy.wait()


def middle(sc, params, kept, g4, gs1, gs2, own, groups):
    plan = arena_plan(own, groups, MIDDLE["places"])
    args = [kept[k] for k in MIDDLE["acts"] + MIDDLE["slopes"]] + [g4, gs1, gs2]
    return pl.pallas_call(
        functools.partial(middle_kernel, dict(own=own, groups=groups, plan=plan)),
        out_shape=[
            jax.ShapeDtypeStruct((split_rows()[1], LANES), f32),
            jax.ShapeDtypeStruct(grad_shapes(own, groups)["g1"], bf16),
        ],
        in_specs=[SMEM, VMEM] + [ANY] * len(args),
        out_specs=[VMEM, ANY],
        scratch_shapes=stage_scratch(MIDDLE, own, groups, plan, params)
        + [
            pltpu.VMEM(gs1.shape, f32),
            pltpu.VMEM(gs2.shape, f32),
            pltpu.VMEM((4, 2 * LANES, 2 * LANES), f32),
            pltpu.VMEM((9 * C3, LANES), f32),
            pltpu.VMEM((9 * C3, LANES), bf16),
            pltpu.SemaphoreType.DMA((len(args),)),
            pltpu.SemaphoreType.DMA,
        ],
        name="middle",
        cost_estimate=pl.CostEstimate(flops=10**10, bytes_accessed=2 * 10**7, transcendentals=10**7),
        compiler_params=pltpu.CompilerParams(vmem_limit_bytes=GRANT),
    )(sc, params, *args)


def first_kernel(cfg, sc, flat_ref, low_ref, *refs):
    own, groups = cfg["own"], cfg["groups"]
    h = own // 2
    refs = list(refs)
    take = lambda m: [refs.pop(0) for _ in range(m)]
    names = FIRST["acts"] + FIRST["slopes"] + ("g1",)
    hbm = dict(zip(names, take(len(names))))
    flat, arena = take(2)
    slopes = dict(zip(FIRST["slopes"], take(len(FIRST["slopes"]))))
    slots = dict(zip("y", take(1)))
    p_ref, acc, nat, natural, tmp, sems = refs
    part = Part(FIRST, cfg["plan"], arena, slopes, slots, hbm, sems, p_ref, nat, natural)
    view, need = part.view, part.need
    for key in ("g1", "sl0", "a0", "xc"):
        part.fetch(key)
    out = (flat, 0)
    flat[...] = low_ref[...]
    load_flat(flat_ref, p_ref)
    v1 = (sc[0], sc[1])
    weight = part.weight(1)
    need("g1", "sl0")
    input_grad("last", view("g1"), 1, weight, slopes["sl0"], view("g0"), h + 22, v1, -11)
    need("a0", "xc")
    weight_grad(1, [("pair", view("a0"), 2)], view("g1"), h + 20, acc, nat, out)
    first_grad(view("g0"), view("xc"), h + 22, out, tmp)


def first(sc, params, low, kept, g1, own, groups):
    plan = arena_plan(own, groups, FIRST["places"])
    args = [kept[k] for k in FIRST["acts"] + FIRST["slopes"]] + [g1]
    return pl.pallas_call(
        functools.partial(first_kernel, dict(own=own, groups=groups, plan=plan)),
        out_shape=jax.ShapeDtypeStruct(low.shape, f32),
        in_specs=[SMEM, VMEM, VMEM] + [ANY] * len(args),
        out_specs=VMEM,
        scratch_shapes=stage_scratch(FIRST, own, groups, plan, params)
        + [
            pltpu.VMEM((4, 2 * LANES, 2 * LANES), f32),
            pltpu.VMEM((9 * C1, LANES), f32),
            pltpu.VMEM((9 * C1, LANES), bf16),
            pltpu.VMEM((8, LANES), f32),
            pltpu.SemaphoreType.DMA((len(args),)),
        ],
        name="first",
        cost_estimate=pl.CostEstimate(flops=10**10, bytes_accessed=2 * 10**7, transcendentals=10**7),
        compiler_params=pltpu.CompilerParams(vmem_limit_bytes=GRANT),
    )(sc, params, low, *args)


def add_up(value, n):
    return value.reshape(n, -1, LANES).sum(0)


def gather_up(value, axes, n):
    return lax.all_to_all(jnp.tile(value, (n, 1)), axes, 0, 0, tiled=True)


def sum_all(keep, send, middle_of, first_of):
    strips = lax.axis_size("strip")
    plane = lax.axis_size("hi") * lax.axis_size("half")
    swap = [(0, 1), (1, 0)]
    part = keep + lax.ppermute(send, "core", swap)
    part = lax.all_to_all(part, ("hi", "half"), 0, 0, tiled=True)
    part, made = lax.optimization_barrier((part, middle_of()))
    part = lax.all_to_all(add_up(part, plane), ("strip",), 0, 0, tiled=True)
    part, low = lax.optimization_barrier((part, first_of(*made)))
    low = lax.all_to_all(low, ("core", "hi", "half", "strip"), 0, 0, tiled=True)
    part = jnp.concatenate([add_up(part, strips), add_up(low, 2 * plane * strips)], axis=0)
    part = gather_up(part, ("strip",), strips)
    part = gather_up(part, ("hi", "half"), plane)
    return part, lax.ppermute(part, "core", swap)


def adam_kernel(chunks, low_rows, sc, mine, other, weights, first, second, *refs):
    outs, info, grads, news, sems = refs[:3], refs[3], refs[4], refs[5:8], refs[8]
    size = weights.shape[0]
    low_share = low_rows // (2 * chunks)
    high_share = mine.shape[0] // chunks - low_share
    half = high_share * chunks
    for c, parts in enumerate(((mine, other), (other, mine))):

        @pl.when(sc[7] == c)
        def _():
            for m, ref in enumerate(parts):
                for n in range(chunks):
                    start = n * (high_share + low_share)
                    row = SPLIT + m * half + n * high_share
                    grads[row : row + high_share] = ref[start : start + high_share]
            for m, ref in enumerate(parts):
                for n in range(chunks):
                    start = n * (high_share + low_share) + high_share
                    row = (m * chunks + n) * low_share
                    same = min(max(SPLIT - row, 0), low_share)
                    if same:
                        grads[row : row + same] = ref[start : start + same]
                    if same < low_share:
                        grads[row + same : row + low_share] += ref[start + same : start + low_share]

    whole = size // 1024
    many = divisor(whole, 25)
    steps = whole // many

    def square(i, total):
        g = grads[pl.ds(pl.multiple_of(i * many * 8, 8), many * 8), :]
        return total + jnp.sum((g * g).reshape(many, 8, LANES), axis=0)

    total = lax.fori_loop(0, steps, square, jnp.zeros((8, LANES), f32))
    last = grads[8 * whole : 8 * whole + 8, :]
    index = lax.broadcasted_iota(jnp.int32, (8, LANES), 0) * LANES + lax.broadcasted_iota(jnp.int32, (8, LANES), 1)
    total += jnp.where(index < size - 1024 * whole, last * last, 0.0)
    norm = jnp.sqrt(jnp.sum(total, axis=(0, 1), keepdims=True))
    info[...] = jnp.concatenate([norm * jnp.ones((8, LANES), f32), last], axis=0)
    scale = jnp.minimum(1.0, clip_limit / (norm + 1e-06))

    def update(where, g):
        clipped = g * scale[0, 0]
        one = beta_one * first[where] + (1.0 - beta_one) * clipped
        two = beta_two * second[where] + (1.0 - beta_two) * clipped * clipped
        first_hat = one / (1.0 - beta_one**step_count)
        second_hat = two / (1.0 - beta_two**step_count)
        w = weights[where]
        news[0][where] = w - learn_rate * (first_hat / (jnp.sqrt(second_hat) + adam_eps) + decay_rate * w)
        news[1][where] = one
        news[2][where] = two

    copies = []

    def send(n, where):
        for m in range(3):
            copy = pltpu.make_async_copy(news[m].at[where], outs[m].at[where], sems.at[n, m])
            copy.start()
            copies.append(copy)

    groups = 4
    for n in range(groups):
        first_step, last_step = steps * n // groups, steps * (n + 1) // groups

        def step(i, _):
            g = grads[pl.ds(pl.multiple_of(i * many * 8, 8), many * 8), :].reshape(many * 1024)
            update(pl.ds(pl.multiple_of(i * many * 1024, 1024), many * 1024), g)

        lax.fori_loop(first_step, last_step, step, None)
        if n < groups - 1:
            send(n, pl.ds(first_step * many * 1024, (last_step - first_step) * many * 1024))
    rest = size - 1024 * whole
    if rest:
        update(pl.ds(1024 * whole, rest), last.reshape(1024)[:rest])
    start = steps * (groups - 1) // groups * many * 1024
    send(groups - 1, pl.ds(start, size - start))
    for copy in copies:
        copy.wait()


def adam(sc, mine, other, params, first, second):
    chunks = math.prod(lax.axis_size(a) for a in AXES) // 2
    low_rows = split_rows()[1]
    flat = jax.ShapeDtypeStruct(params.shape, f32)
    return pl.pallas_call(
        functools.partial(adam_kernel, chunks, low_rows),
        out_shape=[flat, flat, flat, jax.ShapeDtypeStruct((16, LANES), f32)],
        in_specs=[SMEM] + [VMEM] * 5,
        out_specs=[ANY] * 3 + [VMEM],
        scratch_shapes=[pltpu.VMEM((SPLIT + 2 * mine.shape[0] - low_rows, LANES), f32)]
        + [pltpu.VMEM(params.shape, f32)] * 3
        + [pltpu.SemaphoreType.DMA((4, 3))],
        name="adam",
        cost_estimate=pl.CostEstimate(flops=10**7, bytes_accessed=14 * 10**6, transcendentals=10**6),
        compiler_params=pltpu.CompilerParams(vmem_limit_bytes=12 * 2**20),
    )(sc, mine, other, params, first, second)


AXES = ("strip", "hi", "half", "core")
GROUP = ("hi", "half", "core")


def body(patch, images, fg_masks, ray_targets, params, moment_one, moment_two):
    strips, hi, half, core = (lax.axis_size(a) for a in AXES)
    cols = half * core
    count, rows_here, cols_here = images.shape
    own = rows_here * hi
    strip = lax.axis_index("strip")

    got = lax.all_to_all(tiles_of(images, fg_masks, strips), AXES, 0, 0, tiled=True)
    ready, rays = prep(params, jnp.transpose(ray_targets, (0, 1, 3, 2)))
    rays = lax.all_to_all(rays, GROUP, 0, 0, tiled=True)
    rays = rays.reshape(hi, cols, rows_here, cols_here // 4, 4 * RAYS)

    bounds = [
        jnp.stack([-strip * (own // d), patch // d - strip * (own // d)]).astype(jnp.int32)
        for d in (2, 4, 8)
    ]
    sc = jnp.concatenate([*bounds, jnp.stack([strip, lax.axis_index("core")]).astype(jnp.int32)])
    tiling = (hi, strips, cols, rows_here, patch)
    kept, scal = forward(sc, got, ready, own, tiling, count * patch * patch)
    groups = patch // 4
    keep, send, g4, gs1, gs2 = deep(sc, scal, params, kept, rays, own, groups)
    mine, other = sum_all(
        keep,
        send,
        lambda: middle(sc, params, kept, g4, gs1, gs2, own, groups),
        lambda low, g1: first(sc, params, low, kept, g1, own, groups),
    )
    new_params, new_one, new_two, info = adam(sc, mine, other, params, moment_one, moment_two)
    at = params.shape[0] % 1024
    loss_terms = info[8:].reshape(-1)[at : at + 3]
    return (new_params, new_one, new_two, loss_terms, scal[3, 0], info[0, 0])


def solution(mesh):
    rows, cols = mesh.shape["rows"], mesh.shape["cols"]
    patches = 8
    hi = patches // cols
    split = Mesh(mesh.devices.reshape(rows // hi, hi, cols // 2, 2), AXES)
    tiled = P(None, ("strip", "hi"), ("half", "core"))
    in_specs = (tiled, tiled, P(None, ("strip", "hi"), ("half", "core"), None), P(), P(), P())
    out_specs = (P(),) * 6

    def step(images, *rest):
        if images.shape[0] != patches:
            raise ValueError("eight patches")
        part = functools.partial(body, images.shape[1])
        return jax.shard_map(part, mesh=split, in_specs=in_specs, out_specs=out_specs, check_vma=False)(
            images, *rest
        )

    return step
```

```python
import functools
import math

import jax
import jax.numpy as jnp
from jax import lax
from jax.experimental import pallas as pl
from jax.experimental.pallas import tpu as pltpu
from jax.sharding import Mesh, PartitionSpec as P

C1 = 32
C2 = 64
C3 = 128
FINAL = 128
RAYS = 32

beta_one = 0.9
beta_two = 0.999
learn_rate = 0.05
decay_rate = 0.01
adam_eps = 1e-08
clip_limit = 0.005
step_count = 10.0
ray_scale = 16.0

bf16 = jnp.bfloat16
f32 = jnp.float32

LANES = 128
FORWARD = range(1, 10)
GRANT = 60 * 2**20
BLOCK = 4
HEAD_ROWS = 8
HALO = 24
EDGE = 8
VMEM = pl.BlockSpec(memory_space=pltpu.VMEM)
SMEM = pl.BlockSpec(memory_space=pltpu.SMEM)
ANY = pl.BlockSpec(memory_space=pl.ANY)

SHAPES = {
    1: (C1, C1), 2: (C1, C2), 3: (C2, C2), 4: (C2, C3), 5: (C3, C3),
    6: (C3 + C2, C2), 7: (C2, C2), 8: (C2 + C1, C1), 9: (C1, C1), 10: (C1, FINAL),
}

WIDE1 = [[0, 1, 2, 3], [4, None, None, -1]]
WIDE2 = [[0, 1], [2, -1]]
WIDE3 = [[0], [1], [-1]]
POOL1 = [[0, 2, 1, -1]]
POOL2 = [[0, -1], [1, None]]
UP2 = [[0, 2], [1, 3], [4, -1]]
UP3 = [[0], [1], [2], [-1]]
WIDE10 = [[0], [1], [2], [3], [4], [-1]]

INPUTS = {
    1: [(WIDE1, C1)], 2: [(POOL1, C1)], 3: [(WIDE2, C2)], 4: [(POOL2, C2)], 5: [(WIDE3, C3)],
    6: [(UP3, C3), (WIDE2, C2)], 7: [(WIDE2, C2)], 8: [(UP2, C2), (WIDE1, C1)], 9: [(WIDE1, C1)],
    10: [(WIDE1, C1)],
}
COLS = {1: 4, 2: 2, 3: 2, 4: 1, 5: 1, 6: 2, 7: 2, 8: 4, 9: 4, 10: 4}
GRADS = {1: WIDE1, 2: WIDE2, 3: WIDE2, 4: WIDE3, 5: WIDE3, 6: WIDE2, 7: WIDE2, 8: WIDE1, 9: WIDE1,
         10: WIDE10}
BACKS = {
    1: [[[0, 1, 2, 3]]], 2: [[[0, 0, 1, 1]]], 3: [[[0, 1]]], 4: [[[0, 0]]], 5: [[[0]]],
    6: [[[0], [1]], [[0, 1]]], 7: [[[0, 1]]], 8: [[[0, 2], [1, 3]], [[0, 1, 2, 3]]], 9: [[[0, 1, 2, 3]]],
    10: [[[0, 1, 2, 3]]],
}


def fwd_rows(k):
    return 3 if k == 10 else 4


def fwd_shape(k):
    per_row = sum(len(segs) for segs, _ in INPUTS[k]) * LANES
    outs = COLS[k] * SHAPES[k][1]
    return (fwd_rows(k) * per_row, outs if k == 10 else 2 * outs)


def back_shape(k):
    return (2 * sum(len(s) for s in BACKS[k]) * LANES, 4 * len(GRADS[k]) * LANES)


def lanes_iota():
    return lax.broadcasted_iota(jnp.int32, (1, LANES), 1)


def dense_rows(p_ref, offset, n):
    row, lane0 = divmod(offset, LANES)
    value = p_ref[row : row + n, :]
    if lane0 == 0:
        return value
    both = jnp.where(lanes_iota() >= lane0, value, p_ref[row + 1 : row + 1 + n, :])
    return pltpu.roll(both, LANES - lane0, 1)


def load_flat(flat_ref, p_ref):
    size = flat_ref.shape[0]
    whole = size // 1024
    many = divisor(whole, 25)

    def step(i, _):
        value = flat_ref[pl.ds(pl.multiple_of(i * many * 1024, 1024), many * 1024)]
        p_ref[pl.ds(pl.multiple_of(i * many * 8, 8), many * 8), :] = value.reshape(many * 8, LANES)

    lax.fori_loop(0, whole // many, step, None)
    rest = size - whole * 1024
    if rest:
        full, part = divmod(rest, LANES)
        if full:
            value = flat_ref[pl.ds(whole * 1024, full * LANES)]
            p_ref[8 * whole : 8 * whole + full, :] = value.reshape(full, LANES)
        if part:
            p_ref[8 * whole + full : 8 * whole + full + 1, 0:part] = flat_ref[pl.ds(size - part, part)].reshape(1, part)


def flat_rows(size):
    return -(-size // 1024) * 8


def turn(value, lanes):
    lanes %= LANES
    return pltpu.roll(value, lanes, 1) if lanes else value


def natural_rows(k, p_ref, nat_ref, natural):
    ci, co = SHAPES[k]
    size = 9 * ci * co
    fill = LANES // co
    dense = dense_rows(p_ref, offset_of(k), size // LANES)
    if fill == 1:
        natural[0 : 9 * ci, :] = dense.astype(bf16)
        return
    for m in range(fill):
        nat_ref[pl.ds(m, size // LANES, stride=fill), :] = turn(dense, -co * m)
    natural[0 : 9 * ci, :] = nat_ref[0 : 9 * ci, :].astype(bf16)


def input_starts(k):
    starts = [0]
    for _, ch in INPUTS[k]:
        starts.append(starts[-1] + ch)
    return starts


def band(k, natural, places, first, ch):
    ci, co = SHAPES[k]
    zero = jnp.zeros((ch, co), bf16)
    parts = []
    for a, c in places:
        if c is not None and 0 <= a <= 2 and 0 <= c <= 2:
            row = (a * 3 + c) * ci + first
            parts.append(natural[row : row + ch, 0:co])
        else:
            parts.append(zero)
    return jnp.concatenate(parts, axis=1)


def forward_weights(k, p_ref, natural, fwd_ref, tiled_ref):
    ci, co = SHAPES[k]
    n = COLS[k]
    pair = (0,) if k == 10 else (0, 1)
    row = 0
    for j in range(fwd_rows(k)):
        for (segs, ch), first in zip(INPUTS[k], input_starts(k)):
            for seg in segs:
                for h in seg:
                    places = [(j - q, None if h is None else h - p + 1) for q in pair for p in range(n)]
                    fwd_ref[row : row + ch, :] = band(k, natural, places, first, ch) * 0.5
                    row += ch
    bias = dense_rows(p_ref, offset_of(k) + 9 * ci * co, 1)[:, :co] * 0.5
    tiled_ref[...] = jnp.concatenate([bias] * (n * len(pair)), axis=1)


def backward_weights(k, natural, back_ref):
    row = 0
    for q in (0, 1):
        for (_, ch), backs, first in zip(INPUTS[k], BACKS[k], input_starts(k)):
            for seg in backs:
                for p in seg:
                    places = [
                        (q - j + 2, None if h is None else p - h + 1) for j in range(4) for s in GRADS[k] for h in s
                    ]
                    back_ref[row : row + ch, 0 : len(GRADS[k]) * 4 * LANES] = band(k, natural, places, first, ch)
                    row += ch


def prep_first(p_ref, w_ref, tiled_ref, wide_ref):
    taps = [turn(p_ref[i * C1 // LANES : i * C1 // LANES + 1, :], -i * C1)[:, :C1] for i in range(10)]
    zero = jnp.zeros((1, C1), f32)
    wide_ref[...] = jnp.zeros(wide_ref.shape, f32)
    for m in range(6):
        for j in range(4):
            parts = []
            for q in range(2):
                for p in range(4):
                    a, c = j - q, m - p
                    parts.append(taps[a * 3 + c] if 0 <= a <= 2 and 0 <= c <= 2 else zero)
            wide_ref[4 * m + j : 4 * m + j + 1, :] = jnp.concatenate(parts, axis=1)
    w_ref[...] = wide_ref[...].astype(bf16) * 0.5
    tiled_ref[...] = jnp.concatenate([taps[9]] * 8, axis=1) * 0.5


def prep_head(p_ref, hw_ref, hwt_ref, hb_ref, nat_ref):
    wide = 1 + RAYS
    at = offset_of(11)
    for e in range(FINAL):
        nat_ref[e : e + 1, :] = dense_rows(p_ref, at + wide * e, 1)
    w = nat_ref[0:FINAL, :]
    b = dense_rows(p_ref, at + wide * FINAL, 1)
    lane = lanes_iota()
    left = right = 0.0
    for q in range(4):
        chunk = (lane >= RAYS * q) & (lane < RAYS * (q + 1))
        rows = slice(FINAL * q, FINAL * (q + 1))
        hw_ref[rows, 0:LANES] = jnp.where(chunk, turn(w, RAYS * q - 1), 0.0).astype(bf16)
        hw_ref[rows, LANES : 2 * LANES] = jnp.where(lane == RAYS * q, turn(w, RAYS * q), 0.0).astype(bf16)
        left += jnp.where(chunk, turn(b, RAYS * q - 1), 0.0)
        right += jnp.where(lane == RAYS * q, turn(b, RAYS * q), 0.0)
    hwt_ref[...] = hw_ref[...].T
    hb_ref[:, 0:LANES] = left
    hb_ref[:, LANES : 2 * LANES] = right


def prep_kernel(flat_ref, rays_hbm, *refs):
    count = 2 * len(FORWARD) + 3
    outs, scratch = refs[:count], refs[count : 2 * count]
    p_ref, nat, natural, wide, rays_ref, sems, ray_sems = refs[2 * count :]
    patches = rays_hbm.shape[0]
    loads = [pltpu.make_async_copy(rays_hbm.at[p], rays_ref.at[p], ray_sems.at[p]) for p in range(patches)]
    for copy in loads:
        copy.start()
    copies = []

    def send(*places):
        for m in places:
            copy = pltpu.make_async_copy(scratch[m], outs[m], sems.at[m])
            copy.start()
            copies.append(copy)

    last = 2 * len(FORWARD)
    load_flat(flat_ref, p_ref)
    prep_first(p_ref, scratch[last], scratch[last + 1], wide)
    send(last, last + 1)
    for i, k in enumerate(FORWARD):
        natural_rows(k, p_ref, nat, natural)
        forward_weights(k, p_ref, natural, scratch[2 * i], scratch[2 * i + 1])
        send(2 * i, 2 * i + 1)
    for p in range(patches):
        loads[p].wait()
        group_rays(rays_ref, scratch[last + 2], p)
    send(last + 2)
    for copy in copies:
        copy.wait()


def group_rays(rays_ref, out_ref, p):
    rows, rays, cols = rays_ref.shape[1:]
    per = LANES // rays
    quarter = cols // 4
    lane = lanes_iota()
    to = lax.broadcasted_iota(jnp.int32, (cols, cols), 0)
    of = lax.broadcasted_iota(jnp.int32, (cols, cols), 1)
    pick = jnp.where(of == (to % quarter) * 4 + to // quarter, 1.0, 0.0).astype(bf16)
    for r in range(rows // per):
        x = rays_ref[p, per * r : per * (r + 1)].reshape(LANES, cols).astype(f32).astype(bf16)
        turned = lax.dot_general(pick, x, (((1,), (1,)), ((), ())), preferred_element_type=f32)
        parts = [turned[quarter * q : quarter * (q + 1)] for q in range(4)]
        for e in range(per):
            total = turn(parts[0], -rays * e)
            for q in range(1, 4):
                total = jnp.where(lane >= rays * q, turn(parts[q], rays * (q - e)), total)
            out_ref[p, per * r + e] = total.astype(bf16)


def prep(flat, rays):
    count, rows, width, cols = rays.shape
    shapes = []
    for k in FORWARD:
        fs = fwd_shape(k)
        shapes += [jax.ShapeDtypeStruct(fs, bf16), jax.ShapeDtypeStruct((1, fs[1]), f32)]
    shapes += [
        jax.ShapeDtypeStruct((LANES, 2 * LANES), bf16),
        jax.ShapeDtypeStruct((1, 2 * LANES), f32),
        jax.ShapeDtypeStruct((count, rows, cols // 4, 4 * width), bf16),
    ]
    outs = pl.pallas_call(
        prep_kernel,
        out_shape=shapes,
        in_specs=[VMEM, ANY],
        out_specs=[ANY] * len(shapes),
        scratch_shapes=[pltpu.VMEM(v.shape, v.dtype) for v in shapes]
        + [
            pltpu.VMEM((flat_rows(flat.shape[0]), LANES), f32),
            pltpu.VMEM((9 * (C3 + C2), LANES), f32),
            pltpu.VMEM((9 * (C3 + C2), LANES), bf16),
            pltpu.VMEM((LANES, 2 * LANES), f32),
            pltpu.VMEM(rays.shape, jnp.int32),
            pltpu.SemaphoreType.DMA((len(shapes),)),
            pltpu.SemaphoreType.DMA((count,)),
        ],
        name="prep",
        cost_estimate=pl.CostEstimate(flops=10**9, bytes_accessed=2 * 10**7, transcendentals=0),
        compiler_params=pltpu.CompilerParams(vmem_limit_bytes=GRANT),
    )(flat, rays)
    ready = {k: tuple(outs[2 * i : 2 * i + 2]) for i, k in enumerate(FORWARD)}
    ready[0] = tuple(outs[-3:-1])
    return ready, outs[-1]


def tiles_kernel(strips, images_ref, masks_ref, out_ref):
    patches, rows, cols = images_ref.shape
    fold_ = LANES // cols
    high = rows // fold_
    below = out_ref.shape[1] - high
    total = jnp.sum(masks_ref[...].astype(f32).reshape(patches * rows, cols))
    top = jnp.floor(total * (1.0 / 16384.0))
    middle = jnp.floor((total - 16384.0 * top) * (1.0 / 128.0))
    low = total - 16384.0 * top - 128.0 * middle
    lane = lax.broadcasted_iota(jnp.int32, (below, LANES), 1)
    row = lax.broadcasted_iota(jnp.int32, (below, LANES), 0)
    digits = jnp.where(lane == 0, low, jnp.where(lane == 1, middle, jnp.where(lane == 2, top, 0.0)))
    digits = jnp.where(row == 0, digits, 0.0)
    for p in range(patches):
        x = images_ref[p]
        x = jnp.concatenate([x[high * m : high * (m + 1)] for m in range(fold_)], axis=1)
        value = jnp.concatenate([x, digits], axis=0).astype(bf16)
        for s in range(strips):
            out_ref[patches * s + p] = value


def tiles_of(images, masks, strips):
    patches, rows, cols = images.shape
    height = -(-(rows * cols // LANES + 1) // 16) * 16
    return pl.pallas_call(
        functools.partial(tiles_kernel, strips),
        out_shape=jax.ShapeDtypeStruct((strips * patches, height, LANES), bf16),
        in_specs=[VMEM] * 2,
        out_specs=VMEM,
        name="tiles",
    )(images, masks)


def layer_shapes():
    return [(3, 3, 1, C1)] + [(3, 3, *SHAPES[k]) for k in range(1, 11)] + [(FINAL, 1 + RAYS)]


def offset_of(k):
    return sum(math.prod(v) + v[-1] for v in layer_shapes()[:k])


def divisor(count, limit):
    return max(d for d in range(1, min(count, limit) + 1) if count % d == 0)


def mm(a, b):
    return lax.dot_general(a, b, (((1,), (0,)), ((), ())), preferred_element_type=f32)


def mm_t(a, b):
    return lax.dot_general(a, b, (((0,), (0,)), ((), ())), preferred_element_type=f32)


def mm_n(a, b):
    return lax.dot_general(a, b, (((1,), (1,)), ((), ())), preferred_element_type=f32)


def shifted(v):
    zero = jnp.zeros((v.shape[0], 1, v.shape[2]), v.dtype)
    left = jnp.concatenate([zero, v[:, :-1]], axis=1)
    right = jnp.concatenate([v[:, 1:], zero], axis=1)
    return left, right


def lane_of(width=LANES):
    return lax.broadcasted_iota(jnp.int32, (1, 1, width), 2)


def flat2(v):
    return v.reshape(v.shape[0] * v.shape[1], v.shape[2])


def segments(v, three):
    left, right = shifted(v)
    if three:
        return [v, right, left]
    return [v, jnp.where(lane_of() < 64, right, left)]


def rows_of(view):
    return view.reshape(view.shape[0] * 2, *view.shape[2:])


def fours_of(view):
    return view.reshape(view.shape[0] // 2, 2, *view.shape[1:])


def store(view, index, v, three):
    for s, part in enumerate(segments(v, three)):
        view[(*index, s)] = part.astype(bf16)


def lhs_parts(kind, view, base, T, j, repeat):
    segs = range(view.shape[-3])
    if kind == "up":
        at = base + (-1, 0, 0, 1)[j]
        parts = [flat2(view[pl.ds(at, T), s]) for s in segs]
        return parts[:1] + parts if repeat else parts
    p, q = divmod(j + 1, 2)
    return [flat2(view[pl.ds(base + p - 1, T), q, s]) for s in segs]


def lhs_of(sources, r, T, repeat):
    parts = []
    for j in range(4):
        for kind, view, off in sources:
            parts += lhs_parts(kind, view, r + off, T, j, repeat)
    return jnp.concatenate(parts, axis=1)


def each_block(count, T, block):
    T = min(T, count)
    for i in range(-(-count // T)):
        block(min(i * T, count - T), T)


def clear(view, start, stop):
    def step(i, _):
        view[i] = jnp.zeros(view.shape[1:], view.dtype)

    lax.fori_loop(start, stop, step, None)


def clear_outside(view, count, pad, lo, hi):
    clear(view, 0, pad + jnp.clip(lo, 0, count))
    clear(view, pad + jnp.clip(hi, 0, count), count + 2 * pad)


def silu(u):
    t = jnp.tanh(u)
    a = u * t + u
    return a, (t - a * t) + a


SLOPE_STEP = 1.0 / 26000.0
SLOPE_LOW = 0.125


def pack_slope(v):
    return (v * 13000.0 + (13000.5 + 26000.0 * SLOPE_LOW)).astype(jnp.int32).astype(jnp.int16)


def unpack_slope(v):
    return v.astype(jnp.int32).astype(f32) * SLOPE_STEP - SLOPE_LOW


def split_pair(v, T):
    g = v.shape[0] // T
    half = v.shape[1] // 2
    return [v[:, half * q : half * (q + 1)].reshape(T, g, half) for q in range(2)]


def pooled(x, level):
    lane = lane_of()
    if level == 1:
        near = x + pltpu.roll(x, LANES - C1, 2)
        far = x + pltpu.roll(x, C1, 2)
        left, right = shifted(far)
        return [jnp.where((lane & 32) == 0, near, jnp.where(lane < 64, right, left))]
    y = x + pltpu.roll(x, C2, 2)
    left, right = shifted(y)
    return [jnp.where(lane < 64, y, left), right]


def conv(sources, w, bias, out, slopes, count, lo, valid, three=False, pool=None, limit=BLOCK):
    def block(r, T):
        a, slope = silu(mm(lhs_of(sources, r, T, True), w[...]) + bias[...])
        rows, slope = split_pair(a, T), split_pair(slope, T)
        for q in range(2):
            slopes[pl.ds(r, T), q] = pack_slope(slope[q])
            store(out, (pl.ds(r + 1, T), q), rows[q], three)
        if pool:
            x = sum(v.astype(bf16).astype(f32) for v in rows) * 0.25
            for s, part in enumerate(pooled(x, pool[1])):
                pool[0][pl.ds(r + 2, T), s] = part.astype(bf16)

    each_block(count, limit, block)
    clear_outside(out, count, 1, valid[0] - lo, valid[1] - lo)
    if pool:
        clear_outside(pool[0], count, 2, valid[0] - lo, valid[1] - lo)


def first_conv(tiling, own, strip, valid, got, w_ref, bias_ref, out, slopes, xcols, x_ref, xt_ref, v_ref):
    hi, strips, across, per, width = tiling
    count = own // 2 + 22
    rows = own + 2 * HALO
    reach = -(-HALO // per)
    wide = width // across
    high = per * wide // LANES
    x_ref[...] = jnp.zeros(x_ref.shape, f32)
    for d in range(-reach, hi + reach):
        tile = strip * hi + d
        start = HALO + d * per
        first, last = max(0, -start), min(per, rows - start)

        @pl.when((tile >= 0) & (tile < strips * hi))
        def _():
            parts = [got[tile * across + c].astype(f32)[:high] for c in range(across)]
            here = [[v[:, wide * m : wide * (m + 1)] for v in parts] for m in range(LANES // wide)]
            value = jnp.concatenate([jnp.concatenate(v, axis=1) for v in here], axis=0)
            x_ref[start + first : start + last, :] = value[first:last]

    groups = width // 4
    xt_ref[0:EDGE] = jnp.zeros((EDGE, LANES), f32)
    xt_ref[EDGE + width : 2 * EDGE + width] = jnp.zeros((EDGE, LANES), f32)
    xt_ref[EDGE : EDGE + width] = x_ref[...].T
    for m in range(6):
        v_ref[m] = xt_ref[pl.ds(EDGE + m - 1, groups, stride=4), :]
    lane = lax.broadcasted_iota(jnp.int32, (1, LANES), 1)
    many = divisor(count, 6)

    def gather(i, _):
        for u in range(many):
            at = i * many + u
            total = jnp.zeros((groups, LANES), f32)
            for m in range(6):
                turned = pltpu.roll(v_ref[m], 4 * m + LANES - (2 * at + 1), 1)
                total = jnp.where((lane >= 4 * m) & (lane < 4 * m + 4), turned, total)
            xcols[at] = total.astype(bf16)

    lax.fori_loop(0, count // many, gather, None)
    def block(r, T):
        a, slope = silu(mm(flat2(xcols[pl.ds(r, T)]), w_ref[...]) + bias_ref[...])
        rows_, slope = split_pair(a, T), split_pair(slope, T)
        for q in range(2):
            slopes[pl.ds(r, T), q] = pack_slope(slope[q])
            store(out, (pl.ds(r + 1, T), q), rows_[q], False)

    each_block(count, BLOCK, block)
    clear_outside(out, count, 1, valid[0] + 11, valid[1] + 11)


def act_shapes(own, groups):
    h, h2, h3 = own // 2, own // 4, own // 8
    pairs = dict(
        a0=(h + 24, 2), s1=(h + 22, 2), p1=(h2 + 12, 1), a2=(h2 + 12, 2), s2=(h2 + 10, 2), p2=(h3 + 6, 2),
        a4=(h3 + 6, 3), t3=(h3 + 4, 3), a6=(h2 + 6, 2), t2=(h2 + 4, 2), a8=(h + 4, 2), a9=(h + 4, 2),
    )
    shapes = {k: (n, 2, segs, groups, LANES) for k, (n, segs) in pairs.items()}
    shapes["xc"] = (h + 22, groups, LANES)
    return shapes


def slope_shapes(own, groups):
    h, h2, h3 = own // 2, own // 4, own // 8
    counts = [h + 22, h + 20, h2 + 10, h2 + 8, h3 + 4, h3 + 2, h2 + 4, h2 + 2, h + 2, h + 2]
    return {f"sl{k}": (n, 2, groups, LANES) for k, n in enumerate(counts)}


def grad_shapes(own, groups):
    h, h2, h3 = own // 2, own // 4, own // 8
    pairs = {
        10: (h + 4, 6), 9: (h + 6, 2), 8: (h + 6, 2), 7: (h2 + 6, 2), 6: (h2 + 8, 2), 5: (h3 + 6, 3),
        4: (h3 + 8, 3), 3: (h2 + 12, 2), 2: (h2 + 14, 2), 1: (h + 24, 2), 0: (h + 22, 1),
    }
    return {f"g{k}": (n, 2, segs, groups, LANES) for k, (n, segs) in pairs.items()}


def loss_scales(got, tiling, pixels, scal_ref):
    _, _, across, per, width = tiling
    high = per * (width // across) // LANES
    digits = jnp.sum(got[...].astype(f32), axis=0)[high : high + 1, :]
    lane = lanes_iota()
    digits = jnp.where(lane == 0, digits, jnp.where(lane == 1, 128.0 * digits, 16384.0 * digits))
    fg = jnp.sum(jnp.where(lane < 3, digits, 0.0), axis=1, keepdims=True) * jnp.ones((1, LANES), f32)
    scal_ref[0:1] = 0.5 / fg
    scal_ref[1:2] = 0.5 / (pixels - fg)
    scal_ref[2:3] = 1.0 / (fg * RAYS)
    scal_ref[3:4] = fg


def forward_kernel(cfg, sc, got, w0, b0, *refs):
    own, tiling = cfg["own"], cfg["tiling"]
    h, h2, h3 = own // 2, own // 4, own // 8
    refs = list(refs)
    take = lambda m: [refs.pop(0) for _ in range(m)]
    w_hbm, bias = take(9), take(9)
    names = list(cfg["outs"])
    outs = dict(zip(names, take(len(names))))
    scal_ref = take(1)[0]
    here = dict(zip(names, take(len(names))))
    w_vmem = take(9)
    x_ref, xt_ref, v_ref, w_sem, out_sem = refs
    fetch = {}
    for i, k in enumerate(FORWARD):
        fetch[k] = pltpu.make_async_copy(w_hbm[i], w_vmem[i], w_sem.at[i])
        fetch[k].start()
    sent = []

    def send(*keys):
        for key in keys:
            copy = pltpu.make_async_copy(here[key], outs[key], out_sem.at[names.index(key)])
            copy.start()
            sent.append(copy)

    v1, v2, v3 = [(sc[2 * i], sc[2 * i + 1]) for i in range(3)]
    loss_scales(got, tiling, cfg["pixels"], scal_ref)
    first_conv(tiling, own, sc[6], v1, got, w0, b0, here["a0"], here["sl0"], here["xc"],
               x_ref, xt_ref, v_ref)
    send("a0", "sl0", "xc")

    def layer(k, out, sources, count, lo, valid, three=False, pool=None):
        fetch[k].wait()
        conv(sources, w_vmem[k - 1], bias[k - 1], here[out], here[f"sl{k}"], count, lo, valid, three, pool)
        send(out, f"sl{k}")

    layer(1, "s1", [("pair", here["a0"], 2)], h + 20, -10, v1, pool=(rows_of(here["p1"]), 1))
    send("p1")
    layer(2, "a2", [("pair", here["p1"], 1)], h2 + 10, -5, v2)
    layer(3, "s2", [("pair", here["a2"], 2)], h2 + 8, -4, v2, pool=(rows_of(here["p2"]), 2))
    send("p2")
    layer(4, "a4", [("pair", here["p2"], 1)], h3 + 4, -2, v3, True)
    layer(5, "t3", [("pair", here["a4"], 2)], h3 + 2, -1, v3, True)
    layer(6, "a6", [("up", rows_of(here["t3"]), 2), ("pair", here["s2"], 3)], h2 + 4, -2, v2)
    layer(7, "t2", [("pair", here["a6"], 2)], h2 + 2, -1, v2)
    layer(8, "a8", [("up", rows_of(here["t2"]), 3), ("pair", here["s1"], 10)], h + 2, -1, v1)
    layer(9, "a9", [("pair", here["a8"], 1)], h + 2, -1, v1)
    for copy in sent:
        copy.wait()


def forward(sc, got, ready, own, tiling, pixels):
    groups = tiling[-1] // 4
    shapes = {k: jax.ShapeDtypeStruct(v, bf16) for k, v in act_shapes(own, groups).items()}
    shapes |= {k: jax.ShapeDtypeStruct(v, jnp.int16) for k, v in slope_shapes(own, groups).items()}
    weights = [ready[k][0] for k in FORWARD]
    biases = [ready[k][1] for k in FORWARD]
    width = tiling[-1]
    outs = pl.pallas_call(
        functools.partial(forward_kernel, dict(own=own, tiling=tiling, outs=tuple(shapes), pixels=float(pixels))),
        out_shape=[*shapes.values(), jax.ShapeDtypeStruct((8, LANES), f32)],
        in_specs=[SMEM] + [VMEM] * 3 + [ANY] * 9 + [VMEM] * 9,
        out_specs=[ANY] * len(shapes) + [VMEM],
        scratch_shapes=[pltpu.VMEM(v.shape, v.dtype) for v in shapes.values()]
        + [pltpu.VMEM(w.shape, bf16) for w in weights]
        + [
            pltpu.VMEM((LANES, width), f32),
            pltpu.VMEM((width + 2 * EDGE, LANES), f32),
            pltpu.VMEM((6, groups, LANES), f32),
            pltpu.SemaphoreType.DMA((9,)),
            pltpu.SemaphoreType.DMA((len(shapes),)),
        ],
        name="forward",
        cost_estimate=pl.CostEstimate(flops=2 * 10**10, bytes_accessed=5 * 10**7, transcendentals=10**7),
        compiler_params=pltpu.CompilerParams(vmem_limit_bytes=GRANT),
    )(sc, got, *ready[0], *weights, *biases)
    return dict(zip(shapes, outs)), outs[-1]


def sum_back(k, acc):
    ci, co = SHAPES[k]
    n = COLS[k]
    pieces = {}
    for a in range(3):
        value = acc(a)
        base = start = 0
        for segs, ch in INPUTS[k]:
            if segs is UP2:
                unique = [[(0, 1), (2, 3)], [(4,), (-1,)]]
            elif segs is UP3:
                unique = [[(0, 1)], [(2,)], [(-1,)]]
            else:
                unique = [[() if c is None else (c,) for c in seg] for seg in segs]
            uses = {}
            for seg in unique:
                for columns in seg:
                    for col in columns:
                        for p in range(n):
                            c = col - p + 1
                            if 0 <= c <= 2:
                                uses.setdefault(c, []).append((base, p))
                    base += ch
            for c, places in uses.items():
                total = None
                for row, p in places:
                    piece = value[row : row + ch, p * co : (p + 1) * co]
                    total = piece if total is None else total + piece
                pieces[(a * 3 + c) * ci + start] = total
            start += ch
    return pieces


def place(out, value, offset):
    out, base = out
    row, lane0 = divmod(offset - base * LANES, LANES)
    n = value.shape[0]
    if lane0 == 0:
        out[row : row + n, :] += value
        return
    lane = lax.broadcasted_iota(jnp.int32, (1, LANES), 1)
    turned = pltpu.roll(value, lane0, 1)
    out[row : row + n, :] += jnp.where(lane >= lane0, turned, 0.0)
    out[row + 1 : row + 1 + n, :] += jnp.where(lane < lane0, turned, 0.0)


def fold(row, co):
    total = row[:, 0:LANES]
    for m in range(1, row.shape[1] // LANES):
        total = total + row[:, LANES * m : LANES * (m + 1)]
    width = LANES
    while width > co:
        width //= 2
        total = total + pltpu.roll(total, width, 1)
    lane = lax.broadcasted_iota(jnp.int32, (1, LANES), 1)
    return jnp.where(lane < co, total, 0.0)


def place_layer(k, pieces, db, nat, out):
    ci, co = SHAPES[k]
    n = 9 * ci * co // LANES
    fill = LANES // co
    for row, total in pieces.items():
        nat[row : row + total.shape[0], 0:co] = total
    if fill == 1:
        value = nat[0:n, :]
    else:
        value = jnp.concatenate([nat[pl.ds(m, n, stride=fill), :][:, :co] for m in range(fill)], axis=1)
    place(out, value, offset_of(k))
    place(out, fold(db, co), offset_of(k) + 9 * ci * co)


def head_part(own, scal, x, w, bias, hw, hwt, hb, rays, grad, acc, dhead, nat, out):
    _, cols, per = rays.shape[:3]
    x, grad = rows_of(x), rows_of(grad)
    groups = x.shape[2]
    T = divisor(math.gcd(own, per), HEAD_ROWS)
    M = T * groups
    fg_scale, bg_scale, ray_scale_ = scal[0:1], scal[1:2], scal[2:3]
    lane = lax.broadcasted_iota(jnp.int32, (1, LANES), 1)
    is_logit = (lane & 31) == 0
    ones = jnp.ones((8, M), bf16)
    dhead[...] = jnp.zeros(dhead.shape, f32)

    def block(i, carry):
        dbh, fg_loss, bg_loss, ray_loss = carry
        r = i * T
        slabs = [
            jnp.concatenate([flat2(x[pl.ds(r + 4 + d, T), s]) for s in range(2)], axis=1) for d in (-1, 0, 1)
        ]
        a, slope = silu(mm(jnp.concatenate(slabs, axis=1), w[...]) + bias[...])
        slope = 0.5 + 0.5 * slope
        feat = a.astype(bf16)
        head = mm(feat, hw[...]) + hb[...]
        dist, logit = head[:, :LANES], head[:, LANES:]
        part, first = r // per, r % per
        ray = jnp.concatenate([rays[part, c, pl.ds(first, T)] for c in range(cols)], axis=1)
        ray = flat2(ray.astype(f32))
        y = jnp.where(ray > 0.0, 1.0, 0.0)
        diff = dist - ray * (1.0 / ray_scale)
        smooth = jnp.sqrt(diff * diff + 1.0)
        g_dist = diff / smooth * (y * ray_scale_)
        cross = jnp.maximum(logit, 0.0) - logit * y + jnp.log(1.0 + jnp.exp(-jnp.abs(logit)))
        cross = jnp.where(is_logit, cross, 0.0)
        sig = 1.0 / (1.0 + jnp.exp(-logit))
        g_logit = jnp.where(is_logit, (sig - y) * (y * fg_scale + (1.0 - y) * bg_scale), 0.0)
        fg_loss += jnp.sum((cross * y).reshape(M // 8, 8, LANES), axis=0)
        bg_loss += jnp.sum((cross * (1.0 - y)).reshape(M // 8, 8, LANES), axis=0)
        ray_loss += jnp.sum((smooth * y).reshape(M // 8, 8, LANES), axis=0)
        g_head = jnp.concatenate([g_dist, g_logit], axis=1).astype(bf16)
        dhead[...] += mm_t(feat, g_head)
        gz = mm(g_head, hwt[...]) * slope
        center = gz.astype(bf16)
        for s in range(4):
            grad[pl.ds(r + 4, T), s] = center[:, LANES * s : LANES * (s + 1)].reshape(T, groups, LANES)
        left = shifted(gz[:, 3 * LANES :].reshape(T, groups, LANES))[0]
        right = shifted(gz[:, :LANES].reshape(T, groups, LANES))[1]
        grad[pl.ds(r + 4, T), 4] = right.astype(bf16)
        grad[pl.ds(r + 4, T), 5] = left.astype(bf16)
        return dbh + mm(ones, g_head), fg_loss, bg_loss, ray_loss

    zero = jnp.zeros((8, LANES), f32)
    start = (jnp.zeros((8, 2 * LANES), f32), zero, zero, zero)
    carry = start
    for i in range(own // T):
        carry = block(i, carry)
    dbh, *losses = carry
    clear(grad, 0, 4)
    clear(grad, own + 4, own + 8)
    g = jnp.concatenate([flat2(grad[pl.ds(4, own), s]) for s in range(4)], axis=1)
    for a in range(3):
        acc[a] = mm_t(jnp.concatenate([flat2(x[pl.ds(3 + a, own), s]) for s in range(2)], axis=1), g)
    db = mm(jnp.ones((8, own * groups), bf16), g)
    place_layer(10, sum_back(10, lambda a: acc[a]), db[0:1], nat, out)
    both = jnp.zeros((FINAL, LANES), f32)
    for q in range(4):
        rows = dhead[FINAL * q : FINAL * (q + 1), :]
        piece, first = rows[:, :LANES], rows[:, LANES:]
        if q:
            piece = pltpu.roll(piece, LANES - RAYS * q, 1)
            first = pltpu.roll(first, LANES - RAYS * q, 1)
        both += jnp.where(lane == 0, first, pltpu.roll(piece, 1, 1))
    wide = 1 + RAYS
    nat[0:FINAL, :] = jnp.where(lane < wide, both, 0.0)
    at = offset_of(11)
    flat, base = out
    for e in range(FINAL):
        row, lane0 = divmod(at - base * LANES + wide * e, LANES)
        value = pltpu.roll(nat[e : e + 1, :], lane0, 1) if lane0 else nat[e : e + 1, :]
        if lane0 + wide <= LANES:
            flat[row : row + 1, :] += value
        else:
            flat[row : row + 1, :] += jnp.where(lane >= lane0, value, 0.0)
            flat[row + 1 : row + 2, :] += jnp.where(lane < lane0, value, 0.0)
    dist_sum, logit_sum = fold(dbh[0:1, :LANES], RAYS), fold(dbh[0:1, LANES:], RAYS)
    value = jnp.where(lane == 0, logit_sum, pltpu.roll(dist_sum, 1, 1))
    place(out, jnp.where(lane < wide, value, 0.0), at + FINAL * wide)
    terms = jnp.zeros((1, LANES), f32)
    for m, part in enumerate(losses):
        terms = jnp.where(lane == m, jnp.sum(part), terms)
    place(out, terms, offset_of(12))


def weight_grad(k, sources, grad, count, acc, nat, out):
    rows = sum(v.shape[-3] for _, v, _ in sources) * LANES
    groups = grad.shape[3]
    g = jnp.concatenate([flat2(grad[pl.ds(2, count), q, 0]) for q in range(2)], axis=1)
    for j in range(4):
        parts = []
        for kind, view, off in sources:
            parts += lhs_parts(kind, view, off, count, j, False)
        acc[j, 0:rows] = mm_t(jnp.concatenate(parts, axis=1), g)
    db = mm(jnp.ones((8, count * groups), bf16), g)
    pieces = sum_back(k, lambda a: acc[a, 0:rows, 0:LANES] + acc[a + 1, 0:rows, LANES : 2 * LANES])
    place_layer(k, pieces, db[0:1], nat, out)


def input_grad(mode, grad, goff, w, slopes, out, count, valid, lo, three=False, extra=None, side=None, limit=BLOCK):
    def block(r, T):
        groups = grad.shape[3]
        acc = mm_n(lhs_of([("pair", grad, goff)], r, T, False), w[...])
        if mode == "join":
            parts = [acc[:, LANES * m : LANES * (m + 1)].reshape(T, groups, LANES) for m in range(6)]
            gz = ((parts[0] + parts[1]) + (parts[3] + parts[4])) * unpack_slope(slopes[pl.ds(r, T)])
            store(out, (pl.ds(r + 4, T),), gz, three)
            for q in range(2):
                side[0][pl.ds(r + side[1], T), q] = parts[2 + 3 * q]
            return
        vals = split_pair(acc, T)
        for q in range(2):
            if mode == "pool":
                for e in range(2):
                    total = vals[q] * 0.25 + extra[pl.ds(r, T), q, e]
                    store(out, (pl.ds(r + 1, T), q, e), total * unpack_slope(slopes[pl.ds(r, T), q, e]), three)
                continue
            gz = vals[q] * unpack_slope(slopes[pl.ds(r, T), q])
            if mode == "last":
                out[pl.ds(r, T), q, 0] = gz.astype(bf16)
            else:
                store(out, (pl.ds(r + 2, T), q), gz, three)

    if mode == "join":
        side[0][...] = jnp.zeros(side[0].shape, f32)
    each_block(count, limit, block)
    low, high = valid[0] - lo, valid[1] - lo
    if mode == "plain":
        clear_outside(out, count, 2, low, high)
    elif mode == "last":
        clear_outside(out, count, 0, low, high)
    elif mode == "join":
        clear_outside(out, count, 4, low, high)
    else:
        clear_outside(out, count, 1, low // 2, high // 2)


def first_grad(grad, xcols, count, out, tmp):
    groups = grad.shape[3]

    def block(r, T, carry):
        g = jnp.concatenate([flat2(grad[pl.ds(r, T), q, 0]) for q in range(2)], axis=1)
        return carry[0] + mm_t(flat2(xcols[pl.ds(r, T)]), g), carry[1] + mm(jnp.ones((8, T * groups), bf16), g)

    T = divisor(count, 18)
    start = (jnp.zeros((LANES, 2 * LANES), f32), jnp.zeros((8, 2 * LANES), f32))
    dw, db = lax.fori_loop(0, count // T, lambda i, c: block(i * T, T, c), start)
    tmp[...] = jnp.zeros(tmp.shape, f32)
    for a in range(3):
        for c in range(3):
            total = None
            for q in range(2):
                for p in range(4):
                    m, j = p + c, a + q
                    at = (q * 4 + p) * C1
                    piece = dw[4 * m + j : 4 * m + j + 1, at : at + C1]
                    total = piece if total is None else total + piece
            row, at = divmod((a * 3 + c) * C1, LANES)
            tmp[row : row + 1, at : at + C1] = total
    place(out, tmp[...], 0)
    place(out, fold(db[0:1], C1), 9 * C1)


def arena_plan(own, groups, places):
    sizes = act_shapes(own, groups) | grad_shapes(own, groups)
    tiles = {k: math.prod(v[:-2]) for k, v in sizes.items()}
    at, top = {}, 0
    for lists in places:
        ends = []
        for names in lists:
            spot = top
            for name in names:
                at[name] = spot
                spot += tiles[name]
            ends.append(spot)
        top = max(ends)
    return sizes, tiles, at, top


SLOTS = {k: "x" if k in (8, 6) else "y" for k in SHAPES}
DEEP = dict(
    acts=("a9", "a8", "t2", "s1", "a6", "t3", "s2", "a4", "p2"),
    slopes=("sl9", "sl8", "sl7", "sl6", "sl5", "sl4"),
    layers=(10, 9, 8, 7, 6, 5),
    places=([["g10"]], [["g9"], ["g7"], ["g5"]], [["g8"], ["g6"], ["g4"]], [["a9", "a8"]], [["t2", "s1"]],
            [["a6", "t3", "s2", "a4", "p2"]]),
)
MIDDLE = dict(
    acts=("a2", "p1"),
    slopes=("sl3", "sl2", "sl1"),
    layers=(4, 3, 2),
    places=([["g4"]], [["g3"]], [["g2"]], [["g1"]], [["a2", "p1"]]),
)
FIRST = dict(
    acts=("a0", "xc"),
    slopes=("sl0",),
    layers=(1,),
    places=([["g1"]], [["g0"]], [["a0", "xc"]]),
)
SPLIT = 504
STRIPS = 4


def split_rows():
    plane, strips = lax.axis_size("hi") * lax.axis_size("half"), lax.axis_size("strip")
    share = 16 * plane
    low = -(-offset_of(4) // (LANES * share)) * share
    share *= strips
    return -(-(offset_of(12) + 3 - SPLIT * LANES) // (LANES * share)) * share, low


class Part:
    def __init__(self, stage, plan, arena, slopes, slots, hbm, sems, p_ref, nat, natural):
        self.stage, self.arena, self.slopes, self.hbm, self.sems = stage, arena, slopes, hbm, sems
        self.sizes, self.tiles, self.at, _ = plan
        self.slots, self.p_ref, self.nat, self.natural = slots, p_ref, nat, natural
        self.copies = {}

    def view(self, name):
        return self.arena.at[pl.ds(self.at[name], self.tiles[name])].reshape(*self.sizes[name])

    def fetch(self, key, target=None):
        if target is None:
            target = self.slopes[key] if key in self.slopes else self.view(key)
        copy = pltpu.make_async_copy(self.hbm[key], target, self.sems.at[list(self.hbm).index(key)])
        copy.start()
        self.copies[key] = copy

    def need(self, *keys):
        for key in keys:
            self.copies[key].wait()

    def weight(self, k):
        rows, lanes = back_shape(k)
        ref = self.slots[SLOTS[k]].at[pl.ds(0, rows), pl.ds(0, lanes)]
        natural_rows(k, self.p_ref, self.nat, self.natural)
        backward_weights(k, self.natural, ref)
        return ref


def deep_kernel(cfg, sc, scal, flat_ref, *refs):
    own, groups = cfg["own"], cfg["groups"]
    h, h2, h3 = own // 2, own // 4, own // 8
    refs = list(refs)
    take = lambda m: [refs.pop(0) for _ in range(m)]
    names = DEEP["acts"] + DEEP["slopes"] + ("rays",)
    hbm = dict(zip(names, take(len(names))))
    keep_hbm, send_hbm, g4_hbm, gs1_hbm, gs2_hbm = take(5)
    arena = take(1)[0]
    slopes = dict(zip(DEEP["slopes"], take(len(DEEP["slopes"]))))
    slots = dict(zip("yx", take(2)))
    p_ref, w10, bias10, hw, hwt, hb, rays, gs1, gs2, acc, acc10, dhead, nat, natural, flat, sems, out_sems = refs
    part = Part(DEEP, cfg["plan"], arena, slopes, slots, hbm, sems, p_ref, nat, natural)
    view, need = part.view, part.need
    part.fetch("a9")
    part.fetch("rays", rays)
    for key in ("sl9", "a8", "sl8", "t2", "s1", "sl7", "a6", "sl6", "t3", "s2", "sl5", "a4", "sl4", "p2"):
        part.fetch(key)
    out = (flat, SPLIT)
    flat[...] = jnp.zeros(flat.shape, f32)
    v1, v2, v3 = [(sc[2 * i], sc[2 * i + 1]) for i in range(3)]
    load_flat(flat_ref, p_ref)
    natural_rows(10, p_ref, nat, natural)
    forward_weights(10, p_ref, natural, w10, bias10)
    prep_head(p_ref, hw, hwt, hb, nat)
    need("a9", "rays")
    head_part(own, scal, view("a9"), w10, bias10, hw, hwt, hb, rays, view("g10"), acc10, dhead, nat, out)

    weight = part.weight(10)
    need("sl9")
    input_grad("plain", view("g10"), 1, weight, slopes["sl9"], view("g9"), h + 2, v1, -1)

    need("a8", "sl8")
    weight_grad(9, [("pair", view("a8"), 1)], view("g9"), h + 2, acc, nat, out)
    weight = part.weight(9)
    input_grad("plain", view("g9"), 2, weight, slopes["sl8"], view("g8"), h + 2, v1, -1)

    need("t2", "s1", "sl7")
    weight_grad(8, [("up", rows_of(view("t2")), 3), ("pair", view("s1"), 10)], view("g8"), h + 2, acc, nat, out)
    weight = part.weight(8)
    input_grad("join", view("g8"), 1, weight, rows_of(slopes["sl7"]), rows_of(view("g7")), h + 4, v1, -2,
               side=(gs1, 8))
    outs = [pltpu.make_async_copy(gs1, gs1_hbm, out_sems.at[0])]
    outs[0].start()

    need("a6", "sl6")
    weight_grad(7, [("pair", view("a6"), 2)], view("g7"), h2 + 2, acc, nat, out)
    weight = part.weight(7)
    input_grad("plain", view("g7"), 1, weight, slopes["sl6"], view("g6"), h2 + 4, v2, -2)

    need("t3", "s2", "sl5")
    weight_grad(6, [("up", rows_of(view("t3")), 2), ("pair", view("s2"), 3)], view("g6"), h2 + 4, acc, nat, out)
    weight = part.weight(6)
    input_grad("join", view("g6"), 2, weight, rows_of(slopes["sl5"]), rows_of(view("g5")), h2 + 4, v2, -2,
               three=True, side=(gs2, 2))
    outs.append(pltpu.make_async_copy(gs2, gs2_hbm, out_sems.at[1]))
    outs[-1].start()

    need("a4", "sl4")
    weight_grad(5, [("pair", view("a4"), 2)], view("g5"), h3 + 2, acc, nat, out)
    weight = part.weight(5)
    input_grad("plain", view("g5"), 1, weight, slopes["sl4"], view("g4"), h3 + 4, v3, -2, three=True)

    outs.append(pltpu.make_async_copy(view("g4"), g4_hbm, out_sems.at[2]))
    outs[-1].start()

    need("p2")
    weight_grad(4, [("pair", view("p2"), 1)], view("g4"), h3 + 4, acc, nat, out)
    half = flat.shape[0] // 2
    for m, (core, target) in enumerate(((sc[7], keep_hbm), (1 - sc[7], send_hbm))):
        rows = pl.ds(pl.multiple_of(core * half, 8), half)
        outs.append(pltpu.make_async_copy(flat.at[rows], target, out_sems.at[3 + m]))
        outs[-1].start()
    for copy in outs:
        copy.wait()


def stage_scratch(stage, own, groups, plan, params):
    def slot(s):
        return tuple(max([back_shape(k)[d] for k in stage["layers"] if SLOTS[k] == s] + [8]) for d in (0, 1))

    slopes = slope_shapes(own, groups)
    return (
        [pltpu.VMEM((plan[3], groups, LANES), bf16)]
        + [pltpu.VMEM(slopes[k], jnp.int16) for k in stage["slopes"]]
        + [pltpu.VMEM(slot(s), bf16) for s in "yx" if any(SLOTS[k] == s for k in stage["layers"])]
        + [pltpu.VMEM((flat_rows(params.shape[0]), LANES), f32)]
    )


def deep(sc, scal, params, kept, rays, own, groups):
    plan = arena_plan(own, groups, DEEP["places"])
    h, h2 = own // 2, own // 4
    args = [kept[k] for k in DEEP["acts"] + DEEP["slopes"]] + [rays]
    rows = split_rows()[0]
    gs1, gs2 = (h + 20, 2, groups, LANES), (h2 + 8, 2, groups, LANES)
    return pl.pallas_call(
        functools.partial(deep_kernel, dict(own=own, groups=groups, plan=plan)),
        out_shape=[
            jax.ShapeDtypeStruct((rows // 2, LANES), f32),
            jax.ShapeDtypeStruct((rows // 2, LANES), f32),
            jax.ShapeDtypeStruct(grad_shapes(own, groups)["g4"], bf16),
            jax.ShapeDtypeStruct(gs1, f32),
            jax.ShapeDtypeStruct(gs2, f32),
        ],
        in_specs=[SMEM, VMEM, VMEM] + [ANY] * len(args),
        out_specs=[ANY] * 5,
        scratch_shapes=stage_scratch(DEEP, own, groups, plan, params)
        + [
            pltpu.VMEM(fwd_shape(10), bf16),
            pltpu.VMEM((1, fwd_shape(10)[1]), f32),
            pltpu.VMEM((4 * FINAL, 2 * LANES), bf16),
            pltpu.VMEM((2 * LANES, 4 * FINAL), bf16),
            pltpu.VMEM((1, 2 * LANES), f32),
            pltpu.VMEM(rays.shape, bf16),
            pltpu.VMEM(gs1, f32),
            pltpu.VMEM(gs2, f32),
            pltpu.VMEM((4, 5 * LANES, 2 * LANES), f32),
            pltpu.VMEM((3, 2 * LANES, 4 * FINAL), f32),
            pltpu.VMEM((4 * FINAL, 2 * LANES), f32),
            pltpu.VMEM((9 * (C3 + C2), LANES), f32),
            pltpu.VMEM((9 * (C3 + C2), LANES), bf16),
            pltpu.VMEM((rows, LANES), f32),
            pltpu.SemaphoreType.DMA((len(args),)),
            pltpu.SemaphoreType.DMA((5,)),
        ],
        name="deep",
        cost_estimate=pl.CostEstimate(flops=5 * 10**10, bytes_accessed=5 * 10**7, transcendentals=10**7),
        compiler_params=pltpu.CompilerParams(vmem_limit_bytes=GRANT),
    )(sc, scal, params, *args)


def middle_kernel(cfg, sc, flat_ref, *refs):
    own, groups = cfg["own"], cfg["groups"]
    h, h2, h3 = own // 2, own // 4, own // 8
    refs = list(refs)
    take = lambda m: [refs.pop(0) for _ in range(m)]
    names = MIDDLE["acts"] + MIDDLE["slopes"] + ("g4", "gs1", "gs2")
    hbm = dict(zip(names, take(len(names))))
    flat, g1_hbm, arena = take(3)
    slopes = dict(zip(MIDDLE["slopes"], take(len(MIDDLE["slopes"]))))
    slots = dict(zip("y", take(1)))
    p_ref, gs1, gs2, acc, nat, natural, sems, out_sem = refs
    part = Part(MIDDLE, cfg["plan"], arena, slopes, slots, hbm, sems, p_ref, nat, natural)
    view, need = part.view, part.need
    for key in ("g4", "sl3"):
        part.fetch(key)
    part.fetch("gs2", gs2)
    for key in ("a2", "sl2", "p1", "sl1"):
        part.fetch(key)
    part.fetch("gs1", gs1)
    out = (flat, 0)
    flat[...] = jnp.zeros(flat.shape, f32)
    load_flat(flat_ref, p_ref)
    v1, v2 = [(sc[2 * i], sc[2 * i + 1]) for i in range(2)]
    weight = part.weight(4)
    need("g4", "sl3", "gs2")
    input_grad("pool", view("g4"), 2, weight, fours_of(slopes["sl3"]), fours_of(view("g3")), h3 + 4, v2, -4,
               extra=fours_of(gs2))

    need("a2", "sl2")
    weight_grad(3, [("pair", view("a2"), 2)], view("g3"), h2 + 8, acc, nat, out)
    weight = part.weight(3)
    input_grad("plain", view("g3"), 1, weight, slopes["sl2"], view("g2"), h2 + 10, v2, -5)

    need("p1", "sl1", "gs1")
    weight = part.weight(2)
    input_grad("pool", view("g2"), 2, weight, fours_of(slopes["sl1"]), fours_of(view("g1")), h2 + 10, v1, -10,
               extra=fours_of(gs1))
    copy = pltpu.make_async_copy(view("g1"), g1_hbm, out_sem)
    copy.start()
    weight_grad(2, [("pair", view("p1"), 1)], view("g2"), h2 + 10, acc, nat, out)
    copy.wait()


def middle(sc, params, kept, g4, gs1, gs2, own, groups):
    plan = arena_plan(own, groups, MIDDLE["places"])
    args = [kept[k] for k in MIDDLE["acts"] + MIDDLE["slopes"]] + [g4, gs1, gs2]
    return pl.pallas_call(
        functools.partial(middle_kernel, dict(own=own, groups=groups, plan=plan)),
        out_shape=[
            jax.ShapeDtypeStruct((split_rows()[1], LANES), f32),
            jax.ShapeDtypeStruct(grad_shapes(own, groups)["g1"], bf16),
        ],
        in_specs=[SMEM, VMEM] + [ANY] * len(args),
        out_specs=[VMEM, ANY],
        scratch_shapes=stage_scratch(MIDDLE, own, groups, plan, params)
        + [
            pltpu.VMEM(gs1.shape, f32),
            pltpu.VMEM(gs2.shape, f32),
            pltpu.VMEM((4, 2 * LANES, 2 * LANES), f32),
            pltpu.VMEM((9 * C3, LANES), f32),
            pltpu.VMEM((9 * C3, LANES), bf16),
            pltpu.SemaphoreType.DMA((len(args),)),
            pltpu.SemaphoreType.DMA,
        ],
        name="middle",
        cost_estimate=pl.CostEstimate(flops=10**10, bytes_accessed=2 * 10**7, transcendentals=10**7),
        compiler_params=pltpu.CompilerParams(vmem_limit_bytes=GRANT),
    )(sc, params, *args)


def first_kernel(cfg, sc, flat_ref, low_ref, *refs):
    own, groups = cfg["own"], cfg["groups"]
    h = own // 2
    refs = list(refs)
    take = lambda m: [refs.pop(0) for _ in range(m)]
    names = FIRST["acts"] + FIRST["slopes"] + ("g1",)
    hbm = dict(zip(names, take(len(names))))
    flat, arena = take(2)
    slopes = dict(zip(FIRST["slopes"], take(len(FIRST["slopes"]))))
    slots = dict(zip("y", take(1)))
    p_ref, acc, nat, natural, tmp, sems = refs
    part = Part(FIRST, cfg["plan"], arena, slopes, slots, hbm, sems, p_ref, nat, natural)
    view, need = part.view, part.need
    for key in ("g1", "sl0", "a0", "xc"):
        part.fetch(key)
    out = (flat, 0)
    flat[...] = low_ref[...]
    load_flat(flat_ref, p_ref)
    v1 = (sc[0], sc[1])
    weight = part.weight(1)
    need("g1", "sl0")
    input_grad("last", view("g1"), 1, weight, slopes["sl0"], view("g0"), h + 22, v1, -11)
    need("a0", "xc")
    weight_grad(1, [("pair", view("a0"), 2)], view("g1"), h + 20, acc, nat, out)
    first_grad(view("g0"), view("xc"), h + 22, out, tmp)


def first(sc, params, low, kept, g1, own, groups):
    plan = arena_plan(own, groups, FIRST["places"])
    args = [kept[k] for k in FIRST["acts"] + FIRST["slopes"]] + [g1]
    return pl.pallas_call(
        functools.partial(first_kernel, dict(own=own, groups=groups, plan=plan)),
        out_shape=jax.ShapeDtypeStruct(low.shape, f32),
        in_specs=[SMEM, VMEM, VMEM] + [ANY] * len(args),
        out_specs=VMEM,
        scratch_shapes=stage_scratch(FIRST, own, groups, plan, params)
        + [
            pltpu.VMEM((4, 2 * LANES, 2 * LANES), f32),
            pltpu.VMEM((9 * C1, LANES), f32),
            pltpu.VMEM((9 * C1, LANES), bf16),
            pltpu.VMEM((8, LANES), f32),
            pltpu.SemaphoreType.DMA((len(args),)),
        ],
        name="first",
        cost_estimate=pl.CostEstimate(flops=10**10, bytes_accessed=2 * 10**7, transcendentals=10**7),
        compiler_params=pltpu.CompilerParams(vmem_limit_bytes=GRANT),
    )(sc, params, low, *args)


def add_up(value, n):
    return value.reshape(n, -1, LANES).sum(0)


def gather_up(value, axes, n):
    return lax.all_to_all(jnp.tile(value, (n, 1)), axes, 0, 0, tiled=True)


def from_others(value):
    strips = lax.axis_size("strip")
    if strips != STRIPS:
        whole = gather_up(value, ("strip",), strips).reshape(strips, *value.shape)
        return [whole[t] for t in range(strips)]
    swaps = [[(i, i ^ x) for i in range(strips)] for x in range(1, strips)]
    return [value] + [lax.ppermute(value, "strip", swap) for swap in swaps]


def tree_sum(values):
    while len(values) > 1:
        values = [a + b for a, b in zip(values[::2], values[1::2])] + values[len(values) // 2 * 2 :]
    return values[0]


def sum_all(keep, send, middle_of, first_of):
    strips = lax.axis_size("strip")
    plane = lax.axis_size("hi") * lax.axis_size("half")
    swap = [(0, 1), (1, 0)]
    part = keep + lax.ppermute(send, "core", swap)
    part = lax.all_to_all(part, ("hi", "half"), 0, 0, tiled=True)
    part, made = lax.optimization_barrier((part, middle_of()))
    part = lax.all_to_all(add_up(part, plane), ("strip",), 0, 0, tiled=True)
    part, low = lax.optimization_barrier((part, first_of(*made)))
    low = lax.all_to_all(low, ("core", "hi", "half"), 0, 0, tiled=True)
    high = from_others(add_up(part, strips))
    high, low = lax.optimization_barrier((high, low))
    low = tree_sum(from_others(add_up(low, 2 * plane)))
    part = gather_up(jnp.concatenate([*high, low], axis=0), ("hi", "half"), plane)
    return part, lax.ppermute(part, "core", swap)


def adam_kernel(chunks, low_rows, sc, mine, other, weights, first, second, *refs):
    outs, info, grads, news, sems = refs[:3], refs[3], refs[4], refs[5:8], refs[8]
    size = weights.shape[0]
    plane, strips = chunks
    low_share = low_rows // (2 * plane)
    step_ = mine.shape[0] // plane
    share = (step_ - low_share) // strips
    for c, parts in enumerate(((mine, other), (other, mine))):

        @pl.when(sc[7] == c)
        def _():
            for m, ref in enumerate(parts):
                for n in range(plane):
                    for t in range(strips):
                        slot = sc[6] ^ t if strips == STRIPS else t
                        row = SPLIT + ((m * plane + n) * strips + t) * share
                        grads[row : row + share] = ref[pl.ds(pl.multiple_of(n * step_ + slot * share, 8), share)]
            for m, ref in enumerate(parts):
                for n in range(plane):
                    start = n * step_ + strips * share
                    row = (m * plane + n) * low_share
                    same = min(max(SPLIT - row, 0), low_share)
                    if same:
                        grads[row : row + same] = ref[start : start + same]
                    if same < low_share:
                        grads[row + same : row + low_share] += ref[start + same : start + low_share]

    whole = size // 1024
    many = divisor(whole, 25)
    steps = whole // many

    def square(i, total):
        g = grads[pl.ds(pl.multiple_of(i * many * 8, 8), many * 8), :]
        return total + jnp.sum((g * g).reshape(many, 8, LANES), axis=0)

    total = lax.fori_loop(0, steps, square, jnp.zeros((8, LANES), f32))
    last = grads[8 * whole : 8 * whole + 8, :]
    index = lax.broadcasted_iota(jnp.int32, (8, LANES), 0) * LANES + lax.broadcasted_iota(jnp.int32, (8, LANES), 1)
    total += jnp.where(index < size - 1024 * whole, last * last, 0.0)
    norm = jnp.sqrt(jnp.sum(total, axis=(0, 1), keepdims=True))
    info[...] = jnp.concatenate([norm * jnp.ones((8, LANES), f32), last], axis=0)
    scale = jnp.minimum(1.0, clip_limit / (norm + 1e-06))

    def update(where, g):
        clipped = g * scale[0, 0]
        one = beta_one * first[where] + (1.0 - beta_one) * clipped
        two = beta_two * second[where] + (1.0 - beta_two) * clipped * clipped
        first_hat = one / (1.0 - beta_one**step_count)
        second_hat = two / (1.0 - beta_two**step_count)
        w = weights[where]
        news[0][where] = w - learn_rate * (first_hat / (jnp.sqrt(second_hat) + adam_eps) + decay_rate * w)
        news[1][where] = one
        news[2][where] = two

    copies = []

    def send(n, where):
        for m in range(3):
            copy = pltpu.make_async_copy(news[m].at[where], outs[m].at[where], sems.at[n, m])
            copy.start()
            copies.append(copy)

    groups = 4
    for n in range(groups):
        first_step, last_step = steps * n // groups, steps * (n + 1) // groups

        def step(i, _):
            g = grads[pl.ds(pl.multiple_of(i * many * 8, 8), many * 8), :].reshape(many * 1024)
            update(pl.ds(pl.multiple_of(i * many * 1024, 1024), many * 1024), g)

        lax.fori_loop(first_step, last_step, step, None)
        if n < groups - 1:
            send(n, pl.ds(first_step * many * 1024, (last_step - first_step) * many * 1024))
    rest = size - 1024 * whole
    if rest:
        update(pl.ds(1024 * whole, rest), last.reshape(1024)[:rest])
    start = steps * (groups - 1) // groups * many * 1024
    send(groups - 1, pl.ds(start, size - start))
    for copy in copies:
        copy.wait()


def adam(sc, mine, other, params, first, second):
    chunks = (lax.axis_size("hi") * lax.axis_size("half"), lax.axis_size("strip"))
    low_rows = split_rows()[1]
    flat = jax.ShapeDtypeStruct(params.shape, f32)
    return pl.pallas_call(
        functools.partial(adam_kernel, chunks, low_rows),
        out_shape=[flat, flat, flat, jax.ShapeDtypeStruct((16, LANES), f32)],
        in_specs=[SMEM] + [VMEM] * 5,
        out_specs=[ANY] * 3 + [VMEM],
        scratch_shapes=[pltpu.VMEM((SPLIT + 2 * mine.shape[0] - low_rows, LANES), f32)]
        + [pltpu.VMEM(params.shape, f32)] * 3
        + [pltpu.SemaphoreType.DMA((4, 3))],
        name="adam",
        cost_estimate=pl.CostEstimate(flops=10**7, bytes_accessed=14 * 10**6, transcendentals=10**6),
        compiler_params=pltpu.CompilerParams(vmem_limit_bytes=12 * 2**20),
    )(sc, mine, other, params, first, second)


AXES = ("strip", "hi", "half", "core")
GROUP = ("hi", "half", "core")


def body(patch, images, fg_masks, ray_targets, params, moment_one, moment_two):
    strips, hi, half, core = (lax.axis_size(a) for a in AXES)
    cols = half * core
    count, rows_here, cols_here = images.shape
    own = rows_here * hi
    strip = lax.axis_index("strip")

    got = lax.all_to_all(tiles_of(images, fg_masks, strips), AXES, 0, 0, tiled=True)
    ready, rays = prep(params, jnp.transpose(ray_targets, (0, 1, 3, 2)))
    rays = lax.all_to_all(rays, GROUP, 0, 0, tiled=True)
    rays = rays.reshape(hi, cols, rows_here, cols_here // 4, 4 * RAYS)

    bounds = [
        jnp.stack([-strip * (own // d), patch // d - strip * (own // d)]).astype(jnp.int32)
        for d in (2, 4, 8)
    ]
    sc = jnp.concatenate([*bounds, jnp.stack([strip, lax.axis_index("core")]).astype(jnp.int32)])
    tiling = (hi, strips, cols, rows_here, patch)
    kept, scal = forward(sc, got, ready, own, tiling, count * patch * patch)
    groups = patch // 4
    keep, send, g4, gs1, gs2 = deep(sc, scal, params, kept, rays, own, groups)
    mine, other = sum_all(
        keep,
        send,
        lambda: middle(sc, params, kept, g4, gs1, gs2, own, groups),
        lambda low, g1: first(sc, params, low, kept, g1, own, groups),
    )
    new_params, new_one, new_two, info = adam(sc, mine, other, params, moment_one, moment_two)
    at = params.shape[0] % 1024
    loss_terms = info[8:].reshape(-1)[at : at + 3]
    return (new_params, new_one, new_two, loss_terms, scal[3, 0], info[0, 0])


def solution(mesh):
    rows, cols = mesh.shape["rows"], mesh.shape["cols"]
    patches = 8
    hi = patches // cols
    split = Mesh(mesh.devices.reshape(rows // hi, hi, cols // 2, 2), AXES)
    tiled = P(None, ("strip", "hi"), ("half", "core"))
    in_specs = (tiled, tiled, P(None, ("strip", "hi"), ("half", "core"), None), P(), P(), P())
    out_specs = (P(),) * 6

    def step(images, *rest):
        if images.shape[0] != patches:
            raise ValueError("eight patches")
        part = functools.partial(body, images.shape[1])
        return jax.shard_map(part, mesh=split, in_specs=in_specs, out_specs=out_specs, check_vma=False)(
            images, *rest
        )

    return step
```

```python
import functools
import math

import jax
import jax.numpy as jnp
from jax import lax
from jax.experimental import pallas as pl
from jax.experimental.pallas import tpu as pltpu
from jax.sharding import Mesh, PartitionSpec as P

C1 = 32
C2 = 64
C3 = 128
FINAL = 128
RAYS = 32

beta_one = 0.9
beta_two = 0.999
learn_rate = 0.05
decay_rate = 0.01
adam_eps = 1e-08
clip_limit = 0.005
step_count = 10.0
ray_scale = 16.0

bf16 = jnp.bfloat16
f32 = jnp.float32

LANES = 128
PAIR, PLAIN, POOL, LAST, JOIN = "pair", "plain", "pool", "last", "join"
STRIP, HI, SIDE, CORE = "strip", "hi", "half", "core"
FORWARD = range(1, 10)
GRANT = 60 * 2**20
BLOCK = 4
HEAD_ROWS = 8
HALO = 24
EDGE = 8
VMEM = pl.BlockSpec(memory_space=pltpu.VMEM)
SMEM = pl.BlockSpec(memory_space=pltpu.SMEM)
ANY = pl.BlockSpec(memory_space=pl.ANY)

SHAPES = {
    1: (C1, C1), 2: (C1, C2), 3: (C2, C2), 4: (C2, C3), 5: (C3, C3),
    6: (C3 + C2, C2), 7: (C2, C2), 8: (C2 + C1, C1), 9: (C1, C1), 10: (C1, FINAL),
}

WIDE1 = [[0, 1, 2, 3], [4, None, None, -1]]
WIDE2 = [[0, 1], [2, -1]]
WIDE3 = [[0], [1], [-1]]
POOL1 = [[0, 2, 1, -1]]
POOL2 = [[0, -1], [1, None]]
UP2 = [[0, 2], [1, 3], [4, -1]]
UP3 = [[0], [1], [2], [-1]]
WIDE10 = [[0], [1], [2], [3], [4], [-1]]

INPUTS = {
    1: [(WIDE1, C1)], 2: [(POOL1, C1)], 3: [(WIDE2, C2)], 4: [(POOL2, C2)], 5: [(WIDE3, C3)],
    6: [(UP3, C3), (WIDE2, C2)], 7: [(WIDE2, C2)], 8: [(UP2, C2), (WIDE1, C1)], 9: [(WIDE1, C1)],
    10: [(WIDE1, C1)],
}
COLS = {1: 4, 2: 2, 3: 2, 4: 1, 5: 1, 6: 2, 7: 2, 8: 4, 9: 4, 10: 4}
GRADS = {1: WIDE1, 2: WIDE2, 3: WIDE2, 4: WIDE3, 5: WIDE3, 6: WIDE2, 7: WIDE2, 8: WIDE1, 9: WIDE1,
         10: WIDE10}
BACKS = {
    1: [[[0, 1, 2, 3]]], 2: [[[0, 0, 1, 1]]], 3: [[[0, 1]]], 4: [[[0, 0]]], 5: [[[0]]],
    6: [[[0], [1]], [[0, 1]]], 7: [[[0, 1]]], 8: [[[0, 2], [1, 3]], [[0, 1, 2, 3]]], 9: [[[0, 1, 2, 3]]],
    10: [[[0, 1, 2, 3]]],
}


def fwd_rows(k):
    return 3 if k == 10 else 4


def fwd_shape(k):
    per_row = sum(len(segs) for segs, _ in INPUTS[k]) * LANES
    outs = COLS[k] * SHAPES[k][1]
    return (fwd_rows(k) * per_row, outs if k == 10 else 2 * outs)


def back_shape(k):
    return (2 * sum(len(s) for s in BACKS[k]) * LANES, 4 * len(GRADS[k]) * LANES)


def lanes_iota():
    return lax.broadcasted_iota(jnp.int32, (1, LANES), 1)


def dense_rows(p_ref, offset, n):
    row, lane0 = divmod(offset, LANES)
    value = p_ref[row : row + n, :]
    if lane0 == 0:
        return value
    both = jnp.where(lanes_iota() >= lane0, value, p_ref[row + 1 : row + 1 + n, :])
    return pltpu.roll(both, LANES - lane0, 1)


def load_flat(flat_ref, p_ref, base=0):
    size = flat_ref.shape[0]
    whole = size // 1024
    many = divisor(whole, 25)
    row = base // LANES

    def step(i, _):
        value = flat_ref[pl.ds(pl.multiple_of(i * many * 1024, 1024), many * 1024)]
        p_ref[pl.ds(pl.multiple_of(row + i * many * 8, 8), many * 8), :] = value.reshape(many * 8, LANES)

    lax.fori_loop(0, whole // many, step, None)
    rest = size - whole * 1024
    if rest:
        row += 8 * whole
        full, part = divmod(rest, LANES)
        if full:
            value = flat_ref[pl.ds(whole * 1024, full * LANES)]
            p_ref[row : row + full, :] = value.reshape(full, LANES)
        if part:
            p_ref[row + full : row + full + 1, 0:part] = flat_ref[pl.ds(size - part, part)].reshape(1, part)


def flat_range(layers, size):
    start = offset_of(min(layers)) // 1024 * 1024
    stop = -(-offset_of(max(layers) + 1) // 1024) * 1024
    return start, min(stop, size) - start


def flat_rows(size):
    return -(-size // 1024) * 8


def turn(value, lanes):
    lanes %= LANES
    return pltpu.roll(value, lanes, 1) if lanes else value


def natural_rows(k, p_ref, nat_ref, natural):
    ci, co = SHAPES[k]
    size = 9 * ci * co
    fill = LANES // co
    dense = dense_rows(p_ref, offset_of(k), size // LANES)
    if fill == 1:
        natural[0 : 9 * ci, :] = dense.astype(bf16)
        return
    for m in range(fill):
        nat_ref[pl.ds(m, size // LANES, stride=fill), :] = turn(dense, -co * m)
    natural[0 : 9 * ci, :] = nat_ref[0 : 9 * ci, :].astype(bf16)


def input_starts(k):
    starts = [0]
    for _, ch in INPUTS[k]:
        starts.append(starts[-1] + ch)
    return starts


def band(k, natural, places, first, ch):
    ci, co = SHAPES[k]
    zero = jnp.zeros((ch, co), bf16)
    parts = []
    for a, c in places:
        if c is not None and 0 <= a <= 2 and 0 <= c <= 2:
            row = (a * 3 + c) * ci + first
            parts.append(natural[row : row + ch, 0:co])
        else:
            parts.append(zero)
    return jnp.concatenate(parts, axis=1)


def forward_weights(k, p_ref, natural, fwd_ref, tiled_ref):
    ci, co = SHAPES[k]
    n = COLS[k]
    pair = (0,) if k == 10 else (0, 1)
    row = 0
    for j in range(fwd_rows(k)):
        for (segs, ch), first in zip(INPUTS[k], input_starts(k)):
            for seg in segs:
                for h in seg:
                    places = [(j - q, None if h is None else h - p + 1) for q in pair for p in range(n)]
                    fwd_ref[row : row + ch, :] = band(k, natural, places, first, ch) * 0.5
                    row += ch
    bias = dense_rows(p_ref, offset_of(k) + 9 * ci * co, 1)[:, :co] * 0.5
    tiled_ref[...] = jnp.concatenate([bias] * (n * len(pair)), axis=1)


def backward_weights(k, natural, back_ref):
    row = 0
    for q in (0, 1):
        for (_, ch), backs, first in zip(INPUTS[k], BACKS[k], input_starts(k)):
            for seg in backs:
                for p in seg:
                    places = [
                        (q - j + 2, None if h is None else p - h + 1) for j in range(4) for s in GRADS[k] for h in s
                    ]
                    back_ref[row : row + ch, 0 : len(GRADS[k]) * 4 * LANES] = band(k, natural, places, first, ch)
                    row += ch


def prep_first(p_ref, w_ref, tiled_ref, wide_ref):
    taps = [turn(p_ref[i * C1 // LANES : i * C1 // LANES + 1, :], -i * C1)[:, :C1] for i in range(10)]
    zero = jnp.zeros((1, C1), f32)
    wide_ref[...] = jnp.zeros(wide_ref.shape, f32)
    for m in range(6):
        for j in range(4):
            parts = []
            for q in range(2):
                for p in range(4):
                    a, c = j - q, m - p
                    parts.append(taps[a * 3 + c] if 0 <= a <= 2 and 0 <= c <= 2 else zero)
            wide_ref[4 * m + j : 4 * m + j + 1, :] = jnp.concatenate(parts, axis=1)
    w_ref[...] = wide_ref[...].astype(bf16) * 0.5
    tiled_ref[...] = jnp.concatenate([taps[9]] * 8, axis=1) * 0.5


def prep_head(p_ref, hw_ref, hwt_ref, hb_ref, nat_ref):
    wide = 1 + RAYS
    at = offset_of(11)
    for e in range(FINAL):
        nat_ref[e : e + 1, :] = dense_rows(p_ref, at + wide * e, 1)
    w = nat_ref[0:FINAL, :]
    b = dense_rows(p_ref, at + wide * FINAL, 1)
    lane = lanes_iota()
    left = right = 0.0
    for q in range(4):
        chunk = (lane >= RAYS * q) & (lane < RAYS * (q + 1))
        rows = slice(FINAL * q, FINAL * (q + 1))
        hw_ref[rows, 0:LANES] = jnp.where(chunk, turn(w, RAYS * q - 1), 0.0).astype(bf16)
        hw_ref[rows, LANES : 2 * LANES] = jnp.where(lane == RAYS * q, turn(w, RAYS * q), 0.0).astype(bf16)
        left += jnp.where(chunk, turn(b, RAYS * q - 1), 0.0)
        right += jnp.where(lane == RAYS * q, turn(b, RAYS * q), 0.0)
    hwt_ref[...] = hw_ref[...].T
    hb_ref[:, 0:LANES] = left
    hb_ref[:, LANES : 2 * LANES] = right


def prep_kernel(flat_ref, rays_hbm, *refs):
    count = 2 * len(FORWARD) + 3
    outs, scratch = refs[:count], refs[count : 2 * count]
    p_ref, nat, natural, wide, rays_ref, sems, ray_sems = refs[2 * count :]
    patches = rays_hbm.shape[0]
    loads = [pltpu.make_async_copy(rays_hbm.at[p], rays_ref.at[p], ray_sems.at[p]) for p in range(patches)]
    for copy in loads:
        copy.start()
    copies = []

    def send(*places):
        for m in places:
            copy = pltpu.make_async_copy(scratch[m], outs[m], sems.at[m])
            copy.start()
            copies.append(copy)

    last = 2 * len(FORWARD)
    load_flat(flat_ref, p_ref)
    prep_first(p_ref, scratch[last], scratch[last + 1], wide)
    send(last, last + 1)
    for i, k in enumerate(FORWARD):
        natural_rows(k, p_ref, nat, natural)
        forward_weights(k, p_ref, natural, scratch[2 * i], scratch[2 * i + 1])
        send(2 * i, 2 * i + 1)
    for p in range(patches):
        loads[p].wait()
        group_rays(rays_ref, scratch[last + 2], p)
    send(last + 2)
    for copy in copies:
        copy.wait()


def group_rays(rays_ref, out_ref, p):
    rows, rays, cols = rays_ref.shape[1:]
    per = LANES // rays
    quarter = cols // 4
    lane = lanes_iota()
    to = lax.broadcasted_iota(jnp.int32, (cols, cols), 0)
    of = lax.broadcasted_iota(jnp.int32, (cols, cols), 1)
    pick = jnp.where(of == (to % quarter) * 4 + to // quarter, 1.0, 0.0).astype(bf16)
    for r in range(rows // per):
        x = rays_ref[p, per * r : per * (r + 1)].reshape(LANES, cols).astype(f32).astype(bf16)
        turned = lax.dot_general(pick, x, (((1,), (1,)), ((), ())), preferred_element_type=f32)
        parts = [turned[quarter * q : quarter * (q + 1)] for q in range(4)]
        for e in range(per):
            total = turn(parts[0], -rays * e)
            for q in range(1, 4):
                total = jnp.where(lane >= rays * q, turn(parts[q], rays * (q - e)), total)
            out_ref[p, per * r + e] = total.astype(bf16)


def prep(flat, rays):
    count, rows, width, cols = rays.shape
    shapes = []
    for k in FORWARD:
        fs = fwd_shape(k)
        shapes += [jax.ShapeDtypeStruct(fs, bf16), jax.ShapeDtypeStruct((1, fs[1]), f32)]
    shapes += [
        jax.ShapeDtypeStruct((LANES, 2 * LANES), bf16),
        jax.ShapeDtypeStruct((1, 2 * LANES), f32),
        jax.ShapeDtypeStruct((count, rows, cols // 4, 4 * width), bf16),
    ]
    outs = pl.pallas_call(
        prep_kernel,
        out_shape=shapes,
        in_specs=[VMEM, ANY],
        out_specs=[ANY] * len(shapes),
        scratch_shapes=[pltpu.VMEM(v.shape, v.dtype) for v in shapes]
        + [
            pltpu.VMEM((flat_rows(flat.shape[0]), LANES), f32),
            pltpu.VMEM((9 * (C3 + C2), LANES), f32),
            pltpu.VMEM((9 * (C3 + C2), LANES), bf16),
            pltpu.VMEM((LANES, 2 * LANES), f32),
            pltpu.VMEM(rays.shape, jnp.int32),
            pltpu.SemaphoreType.DMA((len(shapes),)),
            pltpu.SemaphoreType.DMA((count,)),
        ],
        name="prep",
        cost_estimate=pl.CostEstimate(flops=10**9, bytes_accessed=2 * 10**7, transcendentals=0),
        compiler_params=pltpu.CompilerParams(vmem_limit_bytes=GRANT),
    )(flat, rays)
    ready = {k: tuple(outs[2 * i : 2 * i + 2]) for i, k in enumerate(FORWARD)}
    ready[0] = tuple(outs[-3:-1])
    return ready, outs[-1]


def tiles_kernel(strips, images_ref, masks_ref, out_ref):
    patches, rows, cols = images_ref.shape
    fold_ = LANES // cols
    high = rows // fold_
    below = out_ref.shape[1] - high
    total = jnp.sum(masks_ref[...].astype(f32).reshape(patches * rows, cols))
    top = jnp.floor(total * (1.0 / 16384.0))
    middle = jnp.floor((total - 16384.0 * top) * (1.0 / 128.0))
    low = total - 16384.0 * top - 128.0 * middle
    lane = lax.broadcasted_iota(jnp.int32, (below, LANES), 1)
    row = lax.broadcasted_iota(jnp.int32, (below, LANES), 0)
    digits = jnp.where(lane == 0, low, jnp.where(lane == 1, middle, jnp.where(lane == 2, top, 0.0)))
    digits = jnp.where(row == 0, digits, 0.0)
    for p in range(patches):
        x = images_ref[p]
        x = jnp.concatenate([x[high * m : high * (m + 1)] for m in range(fold_)], axis=1)
        value = jnp.concatenate([x, digits], axis=0).astype(bf16)
        for s in range(strips):
            out_ref[patches * s + p] = value


def tiles_of(images, masks, strips):
    patches, rows, cols = images.shape
    height = -(-(rows * cols // LANES + 1) // 16) * 16
    return pl.pallas_call(
        functools.partial(tiles_kernel, strips),
        out_shape=jax.ShapeDtypeStruct((strips * patches, height, LANES), bf16),
        in_specs=[VMEM] * 2,
        out_specs=VMEM,
        name="tiles",
    )(images, masks)


def layer_shapes():
    return [(3, 3, 1, C1)] + [(3, 3, *SHAPES[k]) for k in range(1, 11)] + [(FINAL, 1 + RAYS)]


def offset_of(k):
    return sum(math.prod(v) + v[-1] for v in layer_shapes()[:k])


def divisor(count, limit):
    return max(d for d in range(1, min(count, limit) + 1) if count % d == 0)


def mm(a, b):
    return lax.dot_general(a, b, (((1,), (0,)), ((), ())), preferred_element_type=f32)


def mm_t(a, b):
    return lax.dot_general(a, b, (((0,), (0,)), ((), ())), preferred_element_type=f32)


def mm_n(a, b):
    return lax.dot_general(a, b, (((1,), (1,)), ((), ())), preferred_element_type=f32)


def shifted(v):
    zero = jnp.zeros((v.shape[0], 1, v.shape[2]), v.dtype)
    left = jnp.concatenate([zero, v[:, :-1]], axis=1)
    right = jnp.concatenate([v[:, 1:], zero], axis=1)
    return left, right


def lane_of(width=LANES):
    return lax.broadcasted_iota(jnp.int32, (1, 1, width), 2)


def flat2(v):
    return v.reshape(v.shape[0] * v.shape[1], v.shape[2])


def segments(v, three):
    left, right = shifted(v)
    if three:
        return [v, right, left]
    return [v, jnp.where(lane_of() < 64, right, left)]


def rows_of(view):
    return view.reshape(view.shape[0] * 2, *view.shape[2:])


def fours_of(view):
    return view.reshape(view.shape[0] // 2, 2, *view.shape[1:])


def store(view, index, v, three):
    for s, part in enumerate(segments(v, three)):
        view[(*index, s)] = part.astype(bf16)


def lhs_parts(kind, view, base, T, j, repeat):
    segs = range(view.shape[-3])
    if kind == "up":
        at = base + (-1, 0, 0, 1)[j]
        parts = [flat2(view[pl.ds(at, T), s]) for s in segs]
        return parts[:1] + parts if repeat else parts
    p, q = divmod(j + 1, 2)
    return [flat2(view[pl.ds(base + p - 1, T), q, s]) for s in segs]


def lhs_of(sources, r, T, repeat):
    parts = []
    for j in range(4):
        for kind, view, off in sources:
            parts += lhs_parts(kind, view, r + off, T, j, repeat)
    return jnp.concatenate(parts, axis=1)


def each_block(first, last, T, block):
    T = min(T, last - first)
    for i in range(-(-(last - first) // T)):
        block(min(first + i * T, last - T), T)


def clear(view, start, stop):
    def step(i, _):
        view[i] = jnp.zeros(view.shape[1:], view.dtype)

    lax.fori_loop(start, stop, step, None)


def clear_outside(view, count, pad, lo, hi):
    clear(view, 0, pad + jnp.clip(lo, 0, count))
    clear(view, pad + jnp.clip(hi, 0, count), count + 2 * pad)


def silu(u):
    t = jnp.tanh(u)
    a = u * t + u
    return a, (t - a * t) + a


SLOPE_STEP = 1.0 / 26000.0
SLOPE_LOW = 0.125


def pack_slope(v):
    return (v * 13000.0 + (13000.5 + 26000.0 * SLOPE_LOW)).astype(jnp.int32).astype(jnp.int16)


def unpack_slope(v):
    return v.astype(jnp.int32).astype(f32) * SLOPE_STEP - SLOPE_LOW


def split_pair(v, T):
    g = v.shape[0] // T
    half = v.shape[1] // 2
    return [v[:, half * q : half * (q + 1)].reshape(T, g, half) for q in range(2)]


def pooled(x, level):
    lane = lane_of()
    if level == 1:
        near = x + pltpu.roll(x, LANES - C1, 2)
        far = x + pltpu.roll(x, C1, 2)
        left, right = shifted(far)
        return [jnp.where((lane & 32) == 0, near, jnp.where(lane < 64, right, left))]
    y = x + pltpu.roll(x, C2, 2)
    left, right = shifted(y)
    return [jnp.where(lane < 64, y, left), right]


def conv(sources, w, bias, out, slopes, count, lo, valid, three=False, pool=None, limit=BLOCK):
    def block(r, T):
        a, slope = silu(mm(lhs_of(sources, r, T, True), w[...]) + bias[...])
        rows, slope = split_pair(a, T), split_pair(slope, T)
        for q in range(2):
            slopes[pl.ds(r, T), q] = pack_slope(slope[q])
            store(out, (pl.ds(r + 1, T), q), rows[q], three)
        if pool:
            x = sum(v.astype(bf16).astype(f32) for v in rows) * 0.25
            for s, part in enumerate(pooled(x, pool[1])):
                pool[0][pl.ds(r + 2, T), s] = part.astype(bf16)

    each_block(0, count, limit, block)
    clear_outside(out, count, 1, valid[0] - lo, valid[1] - lo)
    if pool:
        clear_outside(pool[0], count, 2, valid[0] - lo, valid[1] - lo)


def first_conv(tiling, own, strip, valid, got, w_ref, bias_ref, out, slopes, xcols, x_ref, xt_ref, v_ref):
    hi, strips, across, per, width = tiling
    count = own // 2 + 22
    rows = own + 2 * HALO
    reach = -(-HALO // per)
    wide = width // across
    high = per * wide // LANES
    x_ref[...] = jnp.zeros(x_ref.shape, f32)
    for d in range(-reach, hi + reach):
        tile = strip * hi + d
        start = HALO + d * per
        first, last = max(0, -start), min(per, rows - start)

        @pl.when((tile >= 0) & (tile < strips * hi))
        def _():
            parts = [got[tile * across + c].astype(f32)[:high] for c in range(across)]
            here = [[v[:, wide * m : wide * (m + 1)] for v in parts] for m in range(LANES // wide)]
            value = jnp.concatenate([jnp.concatenate(v, axis=1) for v in here], axis=0)
            x_ref[start + first : start + last, :] = value[first:last]

    groups = width // 4
    xt_ref[0:EDGE] = jnp.zeros((EDGE, LANES), f32)
    xt_ref[EDGE + width : 2 * EDGE + width] = jnp.zeros((EDGE, LANES), f32)
    xt_ref[EDGE : EDGE + width] = x_ref[...].T
    for m in range(6):
        v_ref[m] = xt_ref[pl.ds(EDGE + m - 1, groups, stride=4), :]
    lane = lax.broadcasted_iota(jnp.int32, (1, LANES), 1)
    many = divisor(count, 6)

    def gather(i, _):
        for u in range(many):
            at = i * many + u
            total = jnp.zeros((groups, LANES), f32)
            for m in range(6):
                turned = pltpu.roll(v_ref[m], 4 * m + LANES - (2 * at + 1), 1)
                total = jnp.where((lane >= 4 * m) & (lane < 4 * m + 4), turned, total)
            xcols[at] = total.astype(bf16)

    lax.fori_loop(0, count // many, gather, None)
    def block(r, T):
        a, slope = silu(mm(flat2(xcols[pl.ds(r, T)]), w_ref[...]) + bias_ref[...])
        rows_, slope = split_pair(a, T), split_pair(slope, T)
        for q in range(2):
            slopes[pl.ds(r, T), q] = pack_slope(slope[q])
            store(out, (pl.ds(r + 1, T), q), rows_[q], False)

    each_block(0, count, BLOCK, block)
    clear_outside(out, count, 1, valid[0] + 11, valid[1] + 11)


def act_shapes(own, groups):
    h, h2, h3 = own // 2, own // 4, own // 8
    pairs = dict(
        a0=(h + 24, 2), s1=(h + 22, 2), p1=(h2 + 12, 1), a2=(h2 + 12, 2), s2=(h2 + 10, 2), p2=(h3 + 6, 2),
        a4=(h3 + 6, 3), t3=(h3 + 4, 3), a6=(h2 + 6, 2), t2=(h2 + 4, 2), a8=(h + 4, 2), a9=(h + 4, 2),
    )
    shapes = {k: (n, 2, segs, groups, LANES) for k, (n, segs) in pairs.items()}
    shapes["xc"] = (h + 22, groups, LANES)
    return shapes


def slope_shapes(own, groups):
    h, h2, h3 = own // 2, own // 4, own // 8
    counts = [h + 22, h + 20, h2 + 10, h2 + 8, h3 + 4, h3 + 2, h2 + 4, h2 + 2, h + 2, h + 2]
    return {f"sl{k}": (n, 2, groups, LANES) for k, n in enumerate(counts)}


def grad_shapes(own, groups):
    h, h2, h3 = own // 2, own // 4, own // 8
    pairs = {
        10: (h + 4, 6), 9: (h + 6, 2), 8: (h + 6, 2), 7: (h2 + 6, 2), 6: (h2 + 8, 2), 5: (h3 + 6, 3),
        4: (h3 + 8, 3), 3: (h2 + 12, 2), 2: (h2 + 14, 2), 1: (h + 24, 2), 0: (h + 22, 1),
    }
    return {f"g{k}": (n, 2, segs, groups, LANES) for k, (n, segs) in pairs.items()}


def loss_scales(got, tiling, pixels, scal_ref):
    _, _, across, per, width = tiling
    high = per * (width // across) // LANES
    digits = jnp.sum(got[...].astype(f32), axis=0)[high : high + 1, :]
    lane = lanes_iota()
    digits = jnp.where(lane == 0, digits, jnp.where(lane == 1, 128.0 * digits, 16384.0 * digits))
    fg = jnp.sum(jnp.where(lane < 3, digits, 0.0), axis=1, keepdims=True) * jnp.ones((1, LANES), f32)
    scal_ref[0:1] = 0.5 / fg
    scal_ref[1:2] = 0.5 / (pixels - fg)
    scal_ref[2:3] = 1.0 / (fg * RAYS)
    scal_ref[3:4] = fg


def forward_kernel(cfg, sc, got, w0, b0, *refs):
    own, tiling = cfg["own"], cfg["tiling"]
    h, h2, h3 = own // 2, own // 4, own // 8
    refs = list(refs)
    take = lambda m: [refs.pop(0) for _ in range(m)]
    w_hbm, bias = take(9), take(9)
    names = list(cfg["outs"])
    outs = dict(zip(names, take(len(names))))
    scal_ref = take(1)[0]
    here = dict(zip(names, take(len(names))))
    w_vmem = take(9)
    x_ref, xt_ref, v_ref, w_sem, out_sem = refs
    fetch = {}
    for i, k in enumerate(FORWARD):
        fetch[k] = pltpu.make_async_copy(w_hbm[i], w_vmem[i], w_sem.at[i])
        fetch[k].start()
    sent = []

    def send(*keys):
        for key in keys:
            copy = pltpu.make_async_copy(here[key], outs[key], out_sem.at[names.index(key)])
            copy.start()
            sent.append(copy)

    v1, v2, v3 = [(sc[2 * i], sc[2 * i + 1]) for i in range(3)]
    loss_scales(got, tiling, cfg["pixels"], scal_ref)
    first_conv(tiling, own, sc[6], v1, got, w0, b0, here["a0"], here["sl0"], here["xc"],
               x_ref, xt_ref, v_ref)
    send("a0", "sl0", "xc")

    def layer(k, out, sources, count, lo, valid, three=False, pool=None):
        fetch[k].wait()
        conv(sources, w_vmem[k - 1], bias[k - 1], here[out], here[f"sl{k}"], count, lo, valid, three, pool)
        send(out, f"sl{k}")

    layer(1, "s1", [(PAIR, here["a0"], 2)], h + 20, -10, v1, pool=(rows_of(here["p1"]), 1))
    send("p1")
    layer(2, "a2", [(PAIR, here["p1"], 1)], h2 + 10, -5, v2)
    layer(3, "s2", [(PAIR, here["a2"], 2)], h2 + 8, -4, v2, pool=(rows_of(here["p2"]), 2))
    send("p2")
    layer(4, "a4", [(PAIR, here["p2"], 1)], h3 + 4, -2, v3, True)
    layer(5, "t3", [(PAIR, here["a4"], 2)], h3 + 2, -1, v3, True)
    layer(6, "a6", [("up", rows_of(here["t3"]), 2), (PAIR, here["s2"], 3)], h2 + 4, -2, v2)
    layer(7, "t2", [(PAIR, here["a6"], 2)], h2 + 2, -1, v2)
    layer(8, "a8", [("up", rows_of(here["t2"]), 3), (PAIR, here["s1"], 10)], h + 2, -1, v1)
    layer(9, "a9", [(PAIR, here["a8"], 1)], h + 2, -1, v1)
    for copy in sent:
        copy.wait()


def forward(sc, got, ready, own, tiling, pixels):
    groups = tiling[-1] // 4
    shapes = {k: jax.ShapeDtypeStruct(v, bf16) for k, v in act_shapes(own, groups).items()}
    shapes |= {k: jax.ShapeDtypeStruct(v, jnp.int16) for k, v in slope_shapes(own, groups).items()}
    weights = [ready[k][0] for k in FORWARD]
    biases = [ready[k][1] for k in FORWARD]
    width = tiling[-1]
    outs = pl.pallas_call(
        functools.partial(forward_kernel, dict(own=own, tiling=tiling, outs=tuple(shapes), pixels=float(pixels))),
        out_shape=[*shapes.values(), jax.ShapeDtypeStruct((8, LANES), f32)],
        in_specs=[SMEM] + [VMEM] * 3 + [ANY] * 9 + [VMEM] * 9,
        out_specs=[ANY] * len(shapes) + [VMEM],
        scratch_shapes=[pltpu.VMEM(v.shape, v.dtype) for v in shapes.values()]
        + [pltpu.VMEM(w.shape, bf16) for w in weights]
        + [
            pltpu.VMEM((LANES, width), f32),
            pltpu.VMEM((width + 2 * EDGE, LANES), f32),
            pltpu.VMEM((6, groups, LANES), f32),
            pltpu.SemaphoreType.DMA((9,)),
            pltpu.SemaphoreType.DMA((len(shapes),)),
        ],
        name="forward",
        cost_estimate=pl.CostEstimate(flops=2 * 10**10, bytes_accessed=5 * 10**7, transcendentals=10**7),
        compiler_params=pltpu.CompilerParams(vmem_limit_bytes=GRANT),
    )(sc, got, *ready[0], *weights, *biases)
    return dict(zip(shapes, outs)), outs[-1]


def sum_back(k, acc):
    ci, co = SHAPES[k]
    n = COLS[k]
    pieces = {}
    for a in range(3):
        value = acc(a)
        base = start = 0
        for segs, ch in INPUTS[k]:
            if segs is UP2:
                unique = [[(0, 1), (2, 3)], [(4,), (-1,)]]
            elif segs is UP3:
                unique = [[(0, 1)], [(2,)], [(-1,)]]
            else:
                unique = [[() if c is None else (c,) for c in seg] for seg in segs]
            uses = {}
            for seg in unique:
                for columns in seg:
                    for col in columns:
                        for p in range(n):
                            c = col - p + 1
                            if 0 <= c <= 2:
                                uses.setdefault(c, []).append((base, p))
                    base += ch
            for c, places in uses.items():
                total = None
                for row, p in places:
                    piece = value[row : row + ch, p * co : (p + 1) * co]
                    total = piece if total is None else total + piece
                pieces[(a * 3 + c) * ci + start] = total
            start += ch
    return pieces


def place(out, value, offset):
    out, base = out
    row, lane0 = divmod(offset - base * LANES, LANES)
    n = value.shape[0]
    if lane0 == 0:
        out[row : row + n, :] += value
        return
    lane = lax.broadcasted_iota(jnp.int32, (1, LANES), 1)
    turned = pltpu.roll(value, lane0, 1)
    out[row : row + n, :] += jnp.where(lane >= lane0, turned, 0.0)
    out[row + 1 : row + 1 + n, :] += jnp.where(lane < lane0, turned, 0.0)


def fold(row, co):
    total = row[:, 0:LANES]
    for m in range(1, row.shape[1] // LANES):
        total = total + row[:, LANES * m : LANES * (m + 1)]
    width = LANES
    while width > co:
        width //= 2
        total = total + pltpu.roll(total, width, 1)
    lane = lax.broadcasted_iota(jnp.int32, (1, LANES), 1)
    return jnp.where(lane < co, total, 0.0)


def place_layer(k, pieces, db, nat, out):
    ci, co = SHAPES[k]
    n = 9 * ci * co // LANES
    fill = LANES // co
    for row, total in pieces.items():
        nat[row : row + total.shape[0], 0:co] = total
    if fill == 1:
        value = nat[0:n, :]
    else:
        value = jnp.concatenate([nat[pl.ds(m, n, stride=fill), :][:, :co] for m in range(fill)], axis=1)
    place(out, value, offset_of(k))
    place(out, fold(db, co), offset_of(k) + 9 * ci * co)


def head_part(own, scal, x, w, bias, hw, hwt, hb, rays, grad, acc, dhead, nat, out):
    _, cols, per = rays.shape[:3]
    x, grad = rows_of(x), rows_of(grad)
    groups = x.shape[2]
    T = divisor(math.gcd(own, per), HEAD_ROWS)
    M = T * groups
    fg_scale, bg_scale, ray_scale_ = scal[0:1], scal[1:2], scal[2:3]
    lane = lax.broadcasted_iota(jnp.int32, (1, LANES), 1)
    is_logit = (lane & 31) == 0
    ones = jnp.ones((8, M), bf16)
    dhead[...] = jnp.zeros(dhead.shape, f32)

    def block(i, carry):
        dbh, fg_loss, bg_loss, ray_loss = carry
        r = i * T
        slabs = [
            jnp.concatenate([flat2(x[pl.ds(r + 4 + d, T), s]) for s in range(2)], axis=1) for d in (-1, 0, 1)
        ]
        a, slope = silu(mm(jnp.concatenate(slabs, axis=1), w[...]) + bias[...])
        slope = 0.5 + 0.5 * slope
        feat = a.astype(bf16)
        head = mm(feat, hw[...]) + hb[...]
        dist, logit = head[:, :LANES], head[:, LANES:]
        part, first = r // per, r % per
        ray = jnp.concatenate([rays[part, c, pl.ds(first, T)] for c in range(cols)], axis=1)
        ray = flat2(ray.astype(f32))
        y = jnp.where(ray > 0.0, 1.0, 0.0)
        diff = dist - ray * (1.0 / ray_scale)
        smooth = jnp.sqrt(diff * diff + 1.0)
        g_dist = diff / smooth * (y * ray_scale_)
        cross = jnp.maximum(logit, 0.0) - logit * y + jnp.log(1.0 + jnp.exp(-jnp.abs(logit)))
        cross = jnp.where(is_logit, cross, 0.0)
        sig = 1.0 / (1.0 + jnp.exp(-logit))
        g_logit = jnp.where(is_logit, (sig - y) * (y * fg_scale + (1.0 - y) * bg_scale), 0.0)
        fg_loss += jnp.sum((cross * y).reshape(M // 8, 8, LANES), axis=0)
        bg_loss += jnp.sum((cross * (1.0 - y)).reshape(M // 8, 8, LANES), axis=0)
        ray_loss += jnp.sum((smooth * y).reshape(M // 8, 8, LANES), axis=0)
        g_head = jnp.concatenate([g_dist, g_logit], axis=1).astype(bf16)
        dhead[...] += mm_t(feat, g_head)
        gz = mm(g_head, hwt[...]) * slope
        center = gz.astype(bf16)
        for s in range(4):
            grad[pl.ds(r + 4, T), s] = center[:, LANES * s : LANES * (s + 1)].reshape(T, groups, LANES)
        left = shifted(gz[:, 3 * LANES :].reshape(T, groups, LANES))[0]
        right = shifted(gz[:, :LANES].reshape(T, groups, LANES))[1]
        grad[pl.ds(r + 4, T), 4] = right.astype(bf16)
        grad[pl.ds(r + 4, T), 5] = left.astype(bf16)
        return dbh + mm(ones, g_head), fg_loss, bg_loss, ray_loss

    zero = jnp.zeros((8, LANES), f32)
    start = (jnp.zeros((8, 2 * LANES), f32), zero, zero, zero)
    carry = start
    for i in range(own // T):
        carry = block(i, carry)
    dbh, *losses = carry
    clear(grad, 0, 4)
    clear(grad, own + 4, own + 8)
    g = jnp.concatenate([flat2(grad[pl.ds(4, own), s]) for s in range(4)], axis=1)
    for a in range(3):
        acc[a] = mm_t(jnp.concatenate([flat2(x[pl.ds(3 + a, own), s]) for s in range(2)], axis=1), g)
    db = mm(jnp.ones((8, own * groups), bf16), g)
    place_layer(10, sum_back(10, lambda a: acc[a]), db[0:1], nat, out)
    both = jnp.zeros((FINAL, LANES), f32)
    for q in range(4):
        rows = dhead[FINAL * q : FINAL * (q + 1), :]
        piece, first = rows[:, :LANES], rows[:, LANES:]
        if q:
            piece = pltpu.roll(piece, LANES - RAYS * q, 1)
            first = pltpu.roll(first, LANES - RAYS * q, 1)
        both += jnp.where(lane == 0, first, pltpu.roll(piece, 1, 1))
    wide = 1 + RAYS
    nat[0:FINAL, :] = jnp.where(lane < wide, both, 0.0)
    at = offset_of(11)
    flat, base = out
    for e in range(FINAL):
        row, lane0 = divmod(at - base * LANES + wide * e, LANES)
        value = pltpu.roll(nat[e : e + 1, :], lane0, 1) if lane0 else nat[e : e + 1, :]
        if lane0 + wide <= LANES:
            flat[row : row + 1, :] += value
        else:
            flat[row : row + 1, :] += jnp.where(lane >= lane0, value, 0.0)
            flat[row + 1 : row + 2, :] += jnp.where(lane < lane0, value, 0.0)
    dist_sum, logit_sum = fold(dbh[0:1, :LANES], RAYS), fold(dbh[0:1, LANES:], RAYS)
    value = jnp.where(lane == 0, logit_sum, pltpu.roll(dist_sum, 1, 1))
    place(out, jnp.where(lane < wide, value, 0.0), at + FINAL * wide)
    terms = jnp.zeros((1, LANES), f32)
    for m, part in enumerate(losses):
        terms = jnp.where(lane == m, jnp.sum(part), terms)
    place(out, terms, offset_of(12))


def weight_grad(k, sources, grad, count, acc, nat, out):
    rows = sum(v.shape[-3] for _, v, _ in sources) * LANES
    groups = grad.shape[3]
    g = jnp.concatenate([flat2(grad[pl.ds(2, count), q, 0]) for q in range(2)], axis=1)
    for j in range(4):
        parts = []
        for kind, view, off in sources:
            parts += lhs_parts(kind, view, off, count, j, False)
        acc[j, 0:rows] = mm_t(jnp.concatenate(parts, axis=1), g)
    db = mm(jnp.ones((8, count * groups), bf16), g)
    pieces = sum_back(k, lambda a: acc[a, 0:rows, 0:LANES] + acc[a + 1, 0:rows, LANES : 2 * LANES])
    place_layer(k, pieces, db[0:1], nat, out)


def input_grad(mode, grad, goff, w, slopes, out, count, valid, lo, three=False, extra=None, side=None, limit=BLOCK):
    def block(r, T):
        groups = grad.shape[3]
        acc = mm_n(lhs_of([(PAIR, grad, goff)], r, T, False), w[...])
        if mode == JOIN:
            parts = [acc[:, LANES * m : LANES * (m + 1)].reshape(T, groups, LANES) for m in range(6)]
            gz = ((parts[0] + parts[1]) + (parts[3] + parts[4])) * unpack_slope(slopes[pl.ds(r, T)])
            store(out, (pl.ds(r + 4, T),), gz, three)
            for q in range(2):
                side[pl.ds(r, T), q] = parts[2 + 3 * q]
            return
        vals = split_pair(acc, T)
        for q in range(2):
            if mode == POOL:
                for e in range(2):
                    total = vals[q] * 0.25
                    if start <= r < stop:
                        total += extra[pl.ds(r - start, T), q, e]
                    store(out, (pl.ds(r + 1, T), q, e), total * unpack_slope(slopes[pl.ds(r, T), q, e]), three)
                continue
            gz = vals[q] * unpack_slope(slopes[pl.ds(r, T), q])
            if mode == LAST:
                out[pl.ds(r, T), q, 0] = gz.astype(bf16)
            else:
                store(out, (pl.ds(r + 2, T), q), gz, three)

    start = stop = 0
    if mode == POOL:
        start = (count - extra.shape[0]) // 2
        stop = start + extra.shape[0]
    for first, last in ((0, start), (start, stop), (stop, count)):
        if first < last:
            each_block(first, last, limit, block)
    low, high = valid[0] - lo, valid[1] - lo
    if mode == PLAIN:
        clear_outside(out, count, 2, low, high)
    elif mode == LAST:
        clear_outside(out, count, 0, low, high)
    elif mode == JOIN:
        clear_outside(out, count, 4, low, high)
    else:
        clear_outside(out, count, 1, low // 2, high // 2)


def first_grad(grad, xcols, count, out, tmp):
    groups = grad.shape[3]

    def block(r, T, carry):
        g = jnp.concatenate([flat2(grad[pl.ds(r, T), q, 0]) for q in range(2)], axis=1)
        return carry[0] + mm_t(flat2(xcols[pl.ds(r, T)]), g), carry[1] + mm(jnp.ones((8, T * groups), bf16), g)

    T = divisor(count, 18)
    start = (jnp.zeros((LANES, 2 * LANES), f32), jnp.zeros((8, 2 * LANES), f32))
    dw, db = lax.fori_loop(0, count // T, lambda i, c: block(i * T, T, c), start)
    tmp[...] = jnp.zeros(tmp.shape, f32)
    for a in range(3):
        for c in range(3):
            total = None
            for q in range(2):
                for p in range(4):
                    m, j = p + c, a + q
                    at = (q * 4 + p) * C1
                    piece = dw[4 * m + j : 4 * m + j + 1, at : at + C1]
                    total = piece if total is None else total + piece
            row, at = divmod((a * 3 + c) * C1, LANES)
            tmp[row : row + 1, at : at + C1] = total
    place(out, tmp[...], 0)
    place(out, fold(db[0:1], C1), 9 * C1)


def arena_plan(own, groups, places):
    sizes = act_shapes(own, groups) | grad_shapes(own, groups)
    tiles = {k: math.prod(v[:-2]) for k, v in sizes.items()}
    at, top = {}, 0
    for lists in places:
        ends = []
        for names in lists:
            spot = top
            for name in names:
                at[name] = spot
                spot += tiles[name]
            ends.append(spot)
        top = max(ends)
    return sizes, tiles, at, top


SLOTS = {k: "x" if k in (8, 6) else "y" for k in SHAPES}
DEEP = dict(
    acts=("a9", "a8", "t2", "s1", "a6", "t3", "s2", "a4", "p2"),
    slopes=("sl9", "sl8", "sl7", "sl6", "sl5", "sl4"),
    layers=(10, 9, 8, 7, 6, 5),
    places=([["g10"]], [["g9"], ["g7"], ["g5"]], [["g8"], ["g6"], ["g4"]], [["a9", "a8"]], [["t2", "s1"]],
            [["a6", "t3", "s2", "a4", "p2"]]),
)
SHALLOW = dict(
    acts=("a2", "p1", "a0", "xc"),
    slopes=("sl3", "sl2", "sl1", "sl0"),
    layers=(4, 3, 2, 1),
    places=([["g4"]], [["g3"]], [["g2"]], [["g1"]], [["g0"]], [["a2", "p1", "a0", "xc"]]),
)
SPLIT = 504
STRIPS = 4


def split_rows():
    plane, strips = lax.axis_size(HI) * lax.axis_size(SIDE), lax.axis_size(STRIP)
    share = 16 * plane
    low = -(-offset_of(4) // (LANES * share)) * share
    share *= strips
    return -(-(offset_of(12) + 3 - SPLIT * LANES) // (LANES * share)) * share, low


class Part:
    def __init__(self, stage, plan, arena, slopes, slots, hbm, sems, p_ref, nat, natural):
        self.stage, self.arena, self.slopes, self.hbm, self.sems = stage, arena, slopes, hbm, sems
        self.sizes, self.tiles, self.at, _ = plan
        self.slots, self.p_ref, self.nat, self.natural = slots, p_ref, nat, natural
        self.copies = {}

    def view(self, name):
        return self.arena.at[pl.ds(self.at[name], self.tiles[name])].reshape(*self.sizes[name])

    def fetch(self, key, target=None):
        if target is None:
            target = self.slopes[key] if key in self.slopes else self.view(key)
        copy = pltpu.make_async_copy(self.hbm[key], target, self.sems.at[list(self.hbm).index(key)])
        copy.start()
        self.copies[key] = copy

    def need(self, *keys):
        for key in keys:
            self.copies[key].wait()

    def weight(self, k):
        rows, lanes = back_shape(k)
        ref = self.slots[SLOTS[k]].at[pl.ds(0, rows), pl.ds(0, lanes)]
        natural_rows(k, self.p_ref, self.nat, self.natural)
        backward_weights(k, self.natural, ref)
        return ref


def deep_kernel(cfg, sc, scal, flat_ref, *refs):
    own, groups = cfg["own"], cfg["groups"]
    h, h2, h3 = own // 2, own // 4, own // 8
    refs = list(refs)
    take = lambda m: [refs.pop(0) for _ in range(m)]
    names = DEEP["acts"] + DEEP["slopes"] + ("rays",)
    hbm = dict(zip(names, take(len(names))))
    keep_hbm, send_hbm, g4_hbm, gs1_hbm, gs2_hbm = take(5)
    arena = take(1)[0]
    slopes = dict(zip(DEEP["slopes"], take(len(DEEP["slopes"]))))
    slots = dict(zip("yx", take(2)))
    p_ref, w10, bias10, hw, hwt, hb, rays, gs1, gs2, acc, acc10, dhead, nat, natural, flat, sems, out_sems = refs
    part = Part(DEEP, cfg["plan"], arena, slopes, slots, hbm, sems, p_ref, nat, natural)
    view, need = part.view, part.need
    part.fetch("a9")
    part.fetch("rays", rays)
    for key in ("sl9", "a8", "sl8", "t2", "s1", "sl7", "a6", "sl6", "t3", "s2", "sl5", "a4", "sl4", "p2"):
        part.fetch(key)
    out = (flat, SPLIT)
    flat[...] = jnp.zeros(flat.shape, f32)
    v1, v2, v3 = [(sc[2 * i], sc[2 * i + 1]) for i in range(3)]
    load_flat(flat_ref, p_ref)
    natural_rows(10, p_ref, nat, natural)
    forward_weights(10, p_ref, natural, w10, bias10)
    prep_head(p_ref, hw, hwt, hb, nat)
    need("a9", "rays")
    head_part(own, scal, view("a9"), w10, bias10, hw, hwt, hb, rays, view("g10"), acc10, dhead, nat, out)

    weight = part.weight(10)
    need("sl9")
    input_grad(PLAIN, view("g10"), 1, weight, slopes["sl9"], view("g9"), h + 2, v1, -1)

    need("a8", "sl8")
    weight_grad(9, [(PAIR, view("a8"), 1)], view("g9"), h + 2, acc, nat, out)
    weight = part.weight(9)
    input_grad(PLAIN, view("g9"), 2, weight, slopes["sl8"], view("g8"), h + 2, v1, -1)

    need("t2", "s1", "sl7")
    weight_grad(8, [("up", rows_of(view("t2")), 3), (PAIR, view("s1"), 10)], view("g8"), h + 2, acc, nat, out)
    weight = part.weight(8)
    input_grad(JOIN, view("g8"), 1, weight, rows_of(slopes["sl7"]), rows_of(view("g7")), h + 4, v1, -2,
               side=gs1)
    outs = [pltpu.make_async_copy(gs1, gs1_hbm, out_sems.at[0])]
    outs[0].start()

    need("a6", "sl6")
    weight_grad(7, [(PAIR, view("a6"), 2)], view("g7"), h2 + 2, acc, nat, out)
    weight = part.weight(7)
    input_grad(PLAIN, view("g7"), 1, weight, slopes["sl6"], view("g6"), h2 + 4, v2, -2)

    need("t3", "s2", "sl5")
    weight_grad(6, [("up", rows_of(view("t3")), 2), (PAIR, view("s2"), 3)], view("g6"), h2 + 4, acc, nat, out)
    weight = part.weight(6)
    input_grad(JOIN, view("g6"), 2, weight, rows_of(slopes["sl5"]), rows_of(view("g5")), h2 + 4, v2, -2,
               three=True, side=gs2)
    outs.append(pltpu.make_async_copy(gs2, gs2_hbm, out_sems.at[1]))
    outs[-1].start()

    need("a4", "sl4")
    weight_grad(5, [(PAIR, view("a4"), 2)], view("g5"), h3 + 2, acc, nat, out)
    weight = part.weight(5)
    input_grad(PLAIN, view("g5"), 1, weight, slopes["sl4"], view("g4"), h3 + 4, v3, -2, three=True)

    outs.append(pltpu.make_async_copy(view("g4"), g4_hbm, out_sems.at[2]))
    outs[-1].start()

    need("p2")
    weight_grad(4, [(PAIR, view("p2"), 1)], view("g4"), h3 + 4, acc, nat, out)
    half = flat.shape[0] // 2
    for m, (core, target) in enumerate(((sc[7], keep_hbm), (1 - sc[7], send_hbm))):
        rows = pl.ds(pl.multiple_of(core * half, 8), half)
        outs.append(pltpu.make_async_copy(flat.at[rows], target, out_sems.at[3 + m]))
        outs[-1].start()
    for copy in outs:
        copy.wait()


def stage_scratch(stage, own, groups, plan, params):
    def slot(s):
        return tuple(max([back_shape(k)[d] for k in stage["layers"] if SLOTS[k] == s] + [8]) for d in (0, 1))

    slopes = slope_shapes(own, groups)
    return (
        [pltpu.VMEM((plan[3], groups, LANES), bf16)]
        + [pltpu.VMEM(slopes[k], jnp.int16) for k in stage["slopes"]]
        + [pltpu.VMEM(slot(s), bf16) for s in "yx" if any(SLOTS[k] == s for k in stage["layers"])]
        + [pltpu.VMEM((flat_rows(params.shape[0]), LANES), f32)]
    )


def deep(sc, scal, params, kept, rays, own, groups):
    plan = arena_plan(own, groups, DEEP["places"])
    h, h2 = own // 2, own // 4
    args = [kept[k] for k in DEEP["acts"] + DEEP["slopes"]] + [rays]
    rows = split_rows()[0]
    gs1, gs2 = (h + 4, 2, groups, LANES), (h2 + 4, 2, groups, LANES)
    return pl.pallas_call(
        functools.partial(deep_kernel, dict(own=own, groups=groups, plan=plan)),
        out_shape=[
            jax.ShapeDtypeStruct((rows // 2, LANES), f32),
            jax.ShapeDtypeStruct((rows // 2, LANES), f32),
            jax.ShapeDtypeStruct(grad_shapes(own, groups)["g4"], bf16),
            jax.ShapeDtypeStruct(gs1, f32),
            jax.ShapeDtypeStruct(gs2, f32),
        ],
        in_specs=[SMEM, VMEM, VMEM] + [ANY] * len(args),
        out_specs=[ANY] * 5,
        scratch_shapes=stage_scratch(DEEP, own, groups, plan, params)
        + [
            pltpu.VMEM(fwd_shape(10), bf16),
            pltpu.VMEM((1, fwd_shape(10)[1]), f32),
            pltpu.VMEM((4 * FINAL, 2 * LANES), bf16),
            pltpu.VMEM((2 * LANES, 4 * FINAL), bf16),
            pltpu.VMEM((1, 2 * LANES), f32),
            pltpu.VMEM(rays.shape, bf16),
            pltpu.VMEM(gs1, f32),
            pltpu.VMEM(gs2, f32),
            pltpu.VMEM((4, 5 * LANES, 2 * LANES), f32),
            pltpu.VMEM((3, 2 * LANES, 4 * FINAL), f32),
            pltpu.VMEM((4 * FINAL, 2 * LANES), f32),
            pltpu.VMEM((9 * (C3 + C2), LANES), f32),
            pltpu.VMEM((9 * (C3 + C2), LANES), bf16),
            pltpu.VMEM((rows, LANES), f32),
            pltpu.SemaphoreType.DMA((len(args),)),
            pltpu.SemaphoreType.DMA((5,)),
        ],
        name="deep",
        cost_estimate=pl.CostEstimate(flops=5 * 10**10, bytes_accessed=5 * 10**7, transcendentals=10**7),
        compiler_params=pltpu.CompilerParams(vmem_limit_bytes=GRANT),
    )(sc, scal, params, *args)


def shallow_kernel(cfg, sc, flat_ref, *refs):
    own, groups = cfg["own"], cfg["groups"]
    h, h2, h3 = own // 2, own // 4, own // 8
    refs = list(refs)
    take = lambda m: [refs.pop(0) for _ in range(m)]
    names = SHALLOW["acts"] + SHALLOW["slopes"] + ("g4", "gs1", "gs2")
    hbm = dict(zip(names, take(len(names))))
    flat, arena = take(2)
    slopes = dict(zip(SHALLOW["slopes"], take(len(SHALLOW["slopes"]))))
    slots = dict(zip("y", take(1)))
    p_ref, gs1, gs2, acc, nat, natural, tmp, sems = refs
    part = Part(SHALLOW, cfg["plan"], arena, slopes, slots, hbm, sems, p_ref, nat, natural)
    view, need = part.view, part.need
    part.fetch("g4")
    part.fetch("sl3")
    part.fetch("gs2", gs2)
    for key in ("a2", "sl2", "p1", "sl1"):
        part.fetch(key)
    part.fetch("gs1", gs1)
    for key in ("a0", "sl0", "xc"):
        part.fetch(key)
    out = (flat, 0)
    flat[...] = jnp.zeros(flat.shape, f32)
    v1, v2 = [(sc[2 * i], sc[2 * i + 1]) for i in range(2)]
    load_flat(flat_ref, p_ref)
    weight = part.weight(4)
    need("g4", "sl3", "gs2")
    input_grad(POOL, view("g4"), 2, weight, fours_of(slopes["sl3"]), fours_of(view("g3")), h3 + 4, v2, -4,
               extra=fours_of(gs2))

    need("a2", "sl2")
    weight_grad(3, [(PAIR, view("a2"), 2)], view("g3"), h2 + 8, acc, nat, out)
    weight = part.weight(3)
    input_grad(PLAIN, view("g3"), 1, weight, slopes["sl2"], view("g2"), h2 + 10, v2, -5)

    need("p1", "sl1", "gs1")
    weight_grad(2, [(PAIR, view("p1"), 1)], view("g2"), h2 + 10, acc, nat, out)
    weight = part.weight(2)
    input_grad(POOL, view("g2"), 2, weight, fours_of(slopes["sl1"]), fours_of(view("g1")), h2 + 10, v1, -10,
               extra=fours_of(gs1))

    need("a0", "sl0", "xc")
    weight_grad(1, [(PAIR, view("a0"), 2)], view("g1"), h + 20, acc, nat, out)
    weight = part.weight(1)
    input_grad(LAST, view("g1"), 1, weight, slopes["sl0"], view("g0"), h + 22, v1, -11)
    first_grad(view("g0"), view("xc"), h + 22, out, tmp)


def shallow(sc, params, kept, g4, gs1, gs2, own, groups):
    plan = arena_plan(own, groups, SHALLOW["places"])
    args = [kept[k] for k in SHALLOW["acts"] + SHALLOW["slopes"]] + [g4, gs1, gs2]
    span = flat_range(SHALLOW["layers"], params.shape[0])
    return pl.pallas_call(
        functools.partial(shallow_kernel, dict(own=own, groups=groups, plan=plan, range=span)),
        out_shape=jax.ShapeDtypeStruct((split_rows()[1], LANES), f32),
        in_specs=[SMEM, VMEM] + [ANY] * len(args),
        out_specs=VMEM,
        scratch_shapes=stage_scratch(SHALLOW, own, groups, plan, params)
        + [
            pltpu.VMEM(gs1.shape, f32),
            pltpu.VMEM(gs2.shape, f32),
            pltpu.VMEM((4, 2 * LANES, 2 * LANES), f32),
            pltpu.VMEM((9 * C3, LANES), f32),
            pltpu.VMEM((9 * C3, LANES), bf16),
            pltpu.VMEM((8, LANES), f32),
            pltpu.SemaphoreType.DMA((len(args),)),
        ],
        name="shallow",
        cost_estimate=pl.CostEstimate(flops=2 * 10**10, bytes_accessed=2 * 10**7, transcendentals=10**7),
        compiler_params=pltpu.CompilerParams(vmem_limit_bytes=GRANT),
    )(sc, params, *args)


def add_up(value, n):
    return value.reshape(n, -1, LANES).sum(0)


def gather_up(value, axes, n):
    return lax.all_to_all(jnp.tile(value, (n, 1)), axes, 0, 0, tiled=True)


def from_others(value):
    strips = lax.axis_size(STRIP)
    if strips != STRIPS:
        whole = gather_up(value, (STRIP,), strips).reshape(strips, *value.shape)
        return [whole[t] for t in range(strips)]
    swaps = [[(i, i ^ x) for i in range(strips)] for x in range(1, strips)]
    return [value] + [lax.ppermute(value, STRIP, swap) for swap in swaps]


def tree_sum(values):
    while len(values) > 1:
        values = [a + b for a, b in zip(values[::2], values[1::2])] + values[len(values) // 2 * 2 :]
    return values[0]


def scatter_up(value):
    strips = lax.axis_size(STRIP)
    if strips != STRIPS:
        return add_up(lax.all_to_all(value, (STRIP,), 0, 0, tiled=True), strips)
    strip = lax.axis_index(STRIP)
    share = value.shape[0] // strips
    parts = [lax.dynamic_slice_in_dim(value, (strip ^ x) * share, share) for x in range(strips)]
    swaps = [[(i, i ^ x) for i in range(strips)] for x in range(strips)]
    return tree_sum(parts[:1] + [lax.ppermute(parts[x], STRIP, swaps[x]) for x in range(1, strips)])


def sum_all(keep, send, low_of):
    plane = lax.axis_size(HI) * lax.axis_size(SIDE)
    swap = [(0, 1), (1, 0)]
    part = keep + lax.ppermute(send, CORE, swap)
    part = lax.all_to_all(part, (HI, SIDE), 0, 0, tiled=True)
    part, low = lax.optimization_barrier((part, low_of()))
    low = lax.all_to_all(low, (CORE, HI, SIDE), 0, 0, tiled=True)
    high = from_others(scatter_up(add_up(part, plane)))
    high, low = lax.optimization_barrier((high, low))
    low = tree_sum(from_others(add_up(low, 2 * plane)))
    part = gather_up(jnp.concatenate([*high, low], axis=0), (HI, SIDE), plane)
    return part, lax.ppermute(part, CORE, swap)


def adam_kernel(chunks, low_rows, sc, mine, other, weights, first, second, *refs):
    outs, info, grads, news, sems = refs[:3], refs[3], refs[4], refs[5:8], refs[8]
    size = weights.shape[0]
    plane, strips = chunks
    low_share = low_rows // (2 * plane)
    step_ = mine.shape[0] // plane
    share = (step_ - low_share) // strips
    for c, parts in enumerate(((mine, other), (other, mine))):

        @pl.when(sc[7] == c)
        def _():
            for m, ref in enumerate(parts):
                for n in range(plane):
                    for t in range(strips):
                        slot = sc[6] ^ t if strips == STRIPS else t
                        row = SPLIT + ((m * plane + n) * strips + t) * share
                        grads[row : row + share] = ref[pl.ds(pl.multiple_of(n * step_ + slot * share, 8), share)]
            for m, ref in enumerate(parts):
                for n in range(plane):
                    start = n * step_ + strips * share
                    row = (m * plane + n) * low_share
                    same = min(max(SPLIT - row, 0), low_share)
                    if same:
                        grads[row : row + same] = ref[start : start + same]
                    if same < low_share:
                        grads[row + same : row + low_share] += ref[start + same : start + low_share]

    whole = size // 1024
    many = divisor(whole, 25)
    steps = whole // many

    def square(i, total):
        g = grads[pl.ds(pl.multiple_of(i * many * 8, 8), many * 8), :]
        return total + jnp.sum((g * g).reshape(many, 8, LANES), axis=0)

    total = lax.fori_loop(0, steps, square, jnp.zeros((8, LANES), f32))
    last = grads[8 * whole : 8 * whole + 8, :]
    index = lax.broadcasted_iota(jnp.int32, (8, LANES), 0) * LANES + lax.broadcasted_iota(jnp.int32, (8, LANES), 1)
    total += jnp.where(index < size - 1024 * whole, last * last, 0.0)
    norm = jnp.sqrt(jnp.sum(total, axis=(0, 1), keepdims=True))
    info[...] = jnp.concatenate([norm * jnp.ones((8, LANES), f32), last], axis=0)
    scale = jnp.minimum(1.0, clip_limit / (norm + 1e-06))

    def update(where, g):
        clipped = g * scale[0, 0]
        one = beta_one * first[where] + (1.0 - beta_one) * clipped
        two = beta_two * second[where] + (1.0 - beta_two) * clipped * clipped
        first_hat = one / (1.0 - beta_one**step_count)
        second_hat = two / (1.0 - beta_two**step_count)
        w = weights[where]
        news[0][where] = w - learn_rate * (first_hat / (jnp.sqrt(second_hat) + adam_eps) + decay_rate * w)
        news[1][where] = one
        news[2][where] = two

    copies = []

    def send(n, where):
        for m in range(3):
            copy = pltpu.make_async_copy(news[m].at[where], outs[m].at[where], sems.at[n, m])
            copy.start()
            copies.append(copy)

    groups = 4
    for n in range(groups):
        first_step, last_step = steps * n // groups, steps * (n + 1) // groups

        def step(i, _):
            g = grads[pl.ds(pl.multiple_of(i * many * 8, 8), many * 8), :].reshape(many * 1024)
            update(pl.ds(pl.multiple_of(i * many * 1024, 1024), many * 1024), g)

        lax.fori_loop(first_step, last_step, step, None)
        if n < groups - 1:
            send(n, pl.ds(first_step * many * 1024, (last_step - first_step) * many * 1024))
    rest = size - 1024 * whole
    if rest:
        update(pl.ds(1024 * whole, rest), last.reshape(1024)[:rest])
    start = steps * (groups - 1) // groups * many * 1024
    send(groups - 1, pl.ds(start, size - start))
    for copy in copies:
        copy.wait()


def adam(sc, mine, other, params, first, second):
    chunks = (lax.axis_size(HI) * lax.axis_size(SIDE), lax.axis_size(STRIP))
    low_rows = split_rows()[1]
    flat = jax.ShapeDtypeStruct(params.shape, f32)
    return pl.pallas_call(
        functools.partial(adam_kernel, chunks, low_rows),
        out_shape=[flat, flat, flat, jax.ShapeDtypeStruct((16, LANES), f32)],
        in_specs=[SMEM] + [VMEM] * 5,
        out_specs=[ANY] * 3 + [VMEM],
        scratch_shapes=[pltpu.VMEM((SPLIT + 2 * mine.shape[0] - low_rows, LANES), f32)]
        + [pltpu.VMEM(params.shape, f32)] * 3
        + [pltpu.SemaphoreType.DMA((4, 3))],
        name="adam",
        cost_estimate=pl.CostEstimate(flops=10**7, bytes_accessed=14 * 10**6, transcendentals=10**6),
        compiler_params=pltpu.CompilerParams(vmem_limit_bytes=12 * 2**20),
    )(sc, mine, other, params, first, second)


AXES = (STRIP, HI, SIDE, CORE)
GROUP = (HI, SIDE, CORE)


def body(patch, images, fg_masks, ray_targets, params, moment_one, moment_two):
    strips, hi, half, core = (lax.axis_size(a) for a in AXES)
    cols = half * core
    count, rows_here, cols_here = images.shape
    own = rows_here * hi
    strip = lax.axis_index(STRIP)

    got = lax.all_to_all(tiles_of(images, fg_masks, strips), AXES, 0, 0, tiled=True)
    ready, rays = prep(params, jnp.transpose(ray_targets, (0, 1, 3, 2)))
    rays = lax.all_to_all(rays, GROUP, 0, 0, tiled=True)
    rays = rays.reshape(hi, cols, rows_here, cols_here // 4, 4 * RAYS)

    bounds = [
        jnp.stack([-strip * (own // d), patch // d - strip * (own // d)]).astype(jnp.int32)
        for d in (2, 4, 8)
    ]
    sc = jnp.concatenate([*bounds, jnp.stack([strip, lax.axis_index(CORE)]).astype(jnp.int32)])
    tiling = (hi, strips, cols, rows_here, patch)
    kept, scal = forward(sc, got, ready, own, tiling, count * patch * patch)
    groups = patch // 4
    keep, send, g4, gs1, gs2 = deep(sc, scal, params, kept, rays, own, groups)
    mine, other = sum_all(keep, send, lambda: shallow(sc, params, kept, g4, gs1, gs2, own, groups))
    new_params, new_one, new_two, info = adam(sc, mine, other, params, moment_one, moment_two)
    at = params.shape[0] % 1024
    loss_terms = info[8:].reshape(-1)[at : at + 3]
    return (new_params, new_one, new_two, loss_terms, scal[3, 0], info[0, 0])


def solution(mesh):
    rows, cols = mesh.shape["rows"], mesh.shape["cols"]
    patches = 8
    hi = patches // cols
    split = Mesh(mesh.devices.reshape(rows // hi, hi, cols // 2, 2), AXES)
    tiled = P(None, (STRIP, HI), (SIDE, CORE))
    in_specs = (tiled, tiled, P(None, (STRIP, HI), (SIDE, CORE), None), P(), P(), P())
    out_specs = (P(),) * 6

    def step(images, *rest):
        if images.shape[0] != patches:
            raise ValueError("eight patches")
        part = functools.partial(body, images.shape[1])
        return jax.shard_map(part, mesh=split, in_specs=in_specs, out_specs=out_specs, check_vma=False)(
            images, *rest
        )

    return step
```

```python
import functools
import math

import jax
import jax.numpy as jnp
from jax import lax
from jax.experimental import pallas as pl
from jax.experimental.pallas import tpu as pltpu
from jax.sharding import Mesh, PartitionSpec as P

C1 = 32
C2 = 64
C3 = 128
FINAL = 128
RAYS = 32

beta_one = 0.9
beta_two = 0.999
learn_rate = 0.05
decay_rate = 0.01
adam_eps = 1e-08
clip_limit = 0.005
step_count = 10.0
ray_scale = 16.0

bf16 = jnp.bfloat16
f32 = jnp.float32

LANES = 128
PAIR, PLAIN, POOL, LAST, JOIN = "pair", "plain", "pool", "last", "join"
STRIP, HI, SIDE, CORE = "strip", "hi", "half", "core"
FORWARD = range(1, 10)
GRANT = 60 * 2**20
BLOCK = 4
HEAD_ROWS = 8
HALO = 24
EDGE = 8
VMEM = pl.BlockSpec(memory_space=pltpu.VMEM)
SMEM = pl.BlockSpec(memory_space=pltpu.SMEM)
ANY = pl.BlockSpec(memory_space=pl.ANY)

SHAPES = {
    1: (C1, C1), 2: (C1, C2), 3: (C2, C2), 4: (C2, C3), 5: (C3, C3),
    6: (C3 + C2, C2), 7: (C2, C2), 8: (C2 + C1, C1), 9: (C1, C1), 10: (C1, FINAL),
}

WIDE1 = [[0, 1, 2, 3], [4, None, None, -1]]
WIDE2 = [[0, 1], [2, -1]]
WIDE3 = [[0], [1], [-1]]
POOL1 = [[0, 2, 1, -1]]
POOL2 = [[0, -1], [1, None]]
UP2 = [[0, 2], [1, 3], [4, -1]]
UP3 = [[0], [1], [2], [-1]]
WIDE10 = [[0], [1], [2], [3], [4], [-1]]

INPUTS = {
    1: [(WIDE1, C1)], 2: [(POOL1, C1)], 3: [(WIDE2, C2)], 4: [(POOL2, C2)], 5: [(WIDE3, C3)],
    6: [(UP3, C3), (WIDE2, C2)], 7: [(WIDE2, C2)], 8: [(UP2, C2), (WIDE1, C1)], 9: [(WIDE1, C1)],
    10: [(WIDE1, C1)],
}
COLS = {1: 4, 2: 2, 3: 2, 4: 1, 5: 1, 6: 2, 7: 2, 8: 4, 9: 4, 10: 4}
GRADS = {1: WIDE1, 2: WIDE2, 3: WIDE2, 4: WIDE3, 5: WIDE3, 6: WIDE2, 7: WIDE2, 8: WIDE1, 9: WIDE1,
         10: WIDE10}
BACKS = {
    1: [[[0, 1, 2, 3]]], 2: [[[0, 0, 1, 1]]], 3: [[[0, 1]]], 4: [[[0, 0]]], 5: [[[0]]],
    6: [[[0], [1]], [[0, 1]]], 7: [[[0, 1]]], 8: [[[0, 2], [1, 3]], [[0, 1, 2, 3]]], 9: [[[0, 1, 2, 3]]],
    10: [[[0, 1, 2, 3]]],
}


def fwd_rows(k):
    return 3 if k == 10 else 4


def fwd_shape(k):
    per_row = sum(len(segs) for segs, _ in INPUTS[k]) * LANES
    outs = COLS[k] * SHAPES[k][1]
    return (fwd_rows(k) * per_row, outs if k == 10 else 2 * outs)


def back_shape(k):
    return (2 * sum(len(s) for s in BACKS[k]) * LANES, 4 * len(GRADS[k]) * LANES)


def lanes_iota():
    return lax.broadcasted_iota(jnp.int32, (1, LANES), 1)


def dense_rows(p_ref, offset, n):
    row, lane0 = divmod(offset, LANES)
    value = p_ref[row : row + n, :]
    if lane0 == 0:
        return value
    both = jnp.where(lanes_iota() >= lane0, value, p_ref[row + 1 : row + 1 + n, :])
    return pltpu.roll(both, LANES - lane0, 1)


def load_flat(flat_ref, p_ref, base=0):
    size = flat_ref.shape[0]
    whole = size // 1024
    many = divisor(whole, 25)
    row = base // LANES

    def step(i, _):
        value = flat_ref[pl.ds(pl.multiple_of(i * many * 1024, 1024), many * 1024)]
        p_ref[pl.ds(pl.multiple_of(row + i * many * 8, 8), many * 8), :] = value.reshape(many * 8, LANES)

    lax.fori_loop(0, whole // many, step, None)
    rest = size - whole * 1024
    if rest:
        row += 8 * whole
        full, part = divmod(rest, LANES)
        if full:
            value = flat_ref[pl.ds(whole * 1024, full * LANES)]
            p_ref[row : row + full, :] = value.reshape(full, LANES)
        if part:
            p_ref[row + full : row + full + 1, 0:part] = flat_ref[pl.ds(size - part, part)].reshape(1, part)


def flat_range(layers, size):
    start = offset_of(min(layers)) // 1024 * 1024
    stop = -(-offset_of(max(layers) + 1) // 1024) * 1024
    return start, min(stop, size) - start


def flat_rows(size):
    return -(-size // 1024) * 8


def turn(value, lanes):
    lanes %= LANES
    return pltpu.roll(value, lanes, 1) if lanes else value


def natural_rows(k, p_ref, nat_ref, natural):
    ci, co = SHAPES[k]
    size = 9 * ci * co
    fill = LANES // co
    dense = dense_rows(p_ref, offset_of(k), size // LANES)
    if fill == 1:
        natural[0 : 9 * ci, :] = dense.astype(bf16)
        return
    for m in range(fill):
        nat_ref[pl.ds(m, size // LANES, stride=fill), :] = turn(dense, -co * m)
    natural[0 : 9 * ci, :] = nat_ref[0 : 9 * ci, :].astype(bf16)


def input_starts(k):
    starts = [0]
    for _, ch in INPUTS[k]:
        starts.append(starts[-1] + ch)
    return starts


def band(k, natural, places, first, ch):
    ci, co = SHAPES[k]
    zero = jnp.zeros((ch, co), bf16)
    parts = []
    for a, c in places:
        if c is not None and 0 <= a <= 2 and 0 <= c <= 2:
            row = (a * 3 + c) * ci + first
            parts.append(natural[row : row + ch, 0:co])
        else:
            parts.append(zero)
    return jnp.concatenate(parts, axis=1)


def forward_weights(k, p_ref, natural, fwd_ref, tiled_ref):
    ci, co = SHAPES[k]
    n = COLS[k]
    pair = (0,) if k == 10 else (0, 1)
    row = 0
    for j in range(fwd_rows(k)):
        for (segs, ch), first in zip(INPUTS[k], input_starts(k)):
            for seg in segs:
                for h in seg:
                    places = [(j - q, None if h is None else h - p + 1) for q in pair for p in range(n)]
                    fwd_ref[row : row + ch, :] = band(k, natural, places, first, ch) * 0.5
                    row += ch
    bias = dense_rows(p_ref, offset_of(k) + 9 * ci * co, 1)[:, :co] * 0.5
    tiled_ref[...] = jnp.concatenate([bias] * (n * len(pair)), axis=1)


def backward_weights(k, natural, back_ref):
    half = back_shape(k)[0] // 2
    per = len(GRADS[k]) * LANES
    row = 0
    for (_, ch), backs, first in zip(INPUTS[k], BACKS[k], input_starts(k)):
        for seg in backs:
            for p in seg:
                places = [(2 - j, None if h is None else p - h + 1) for j in range(3) for s in GRADS[k] for h in s]
                value = band(k, natural, places, first, ch)
                zero = jnp.zeros((ch, per), bf16)
                back_ref[row : row + ch, 0 : 3 * per] = value
                back_ref[row : row + ch, 3 * per : 4 * per] = zero
                back_ref[half + row : half + row + ch, 0:per] = zero
                back_ref[half + row : half + row + ch, per : 4 * per] = value
                row += ch


def prep_first(p_ref, w_ref, tiled_ref, wide_ref):
    taps = [turn(p_ref[i * C1 // LANES : i * C1 // LANES + 1, :], -i * C1)[:, :C1] for i in range(10)]
    zero = jnp.zeros((1, C1), f32)
    wide_ref[...] = jnp.zeros(wide_ref.shape, f32)
    for m in range(6):
        for j in range(4):
            parts = []
            for q in range(2):
                for p in range(4):
                    a, c = j - q, m - p
                    parts.append(taps[a * 3 + c] if 0 <= a <= 2 and 0 <= c <= 2 else zero)
            wide_ref[4 * m + j : 4 * m + j + 1, :] = jnp.concatenate(parts, axis=1)
    w_ref[...] = wide_ref[...].astype(bf16) * 0.5
    tiled_ref[...] = jnp.concatenate([taps[9]] * 8, axis=1) * 0.5


def prep_head(p_ref, hw_ref, hwt_ref, hb_ref, nat_ref):
    wide = 1 + RAYS
    at = offset_of(11)
    for e in range(FINAL):
        nat_ref[e : e + 1, :] = dense_rows(p_ref, at + wide * e, 1)
    w = nat_ref[0:FINAL, :]
    b = dense_rows(p_ref, at + wide * FINAL, 1)
    lane = lanes_iota()
    left = right = 0.0
    for q in range(4):
        chunk = (lane >= RAYS * q) & (lane < RAYS * (q + 1))
        rows = slice(FINAL * q, FINAL * (q + 1))
        hw_ref[rows, 0:LANES] = jnp.where(chunk, turn(w, RAYS * q - 1), 0.0).astype(bf16)
        hw_ref[rows, LANES : 2 * LANES] = jnp.where(lane == RAYS * q, turn(w, RAYS * q), 0.0).astype(bf16)
        left += jnp.where(chunk, turn(b, RAYS * q - 1), 0.0)
        right += jnp.where(lane == RAYS * q, turn(b, RAYS * q), 0.0)
    hwt_ref[...] = hw_ref[...].T
    hb_ref[:, 0:LANES] = left
    hb_ref[:, LANES : 2 * LANES] = right


def prep_kernel(flat_ref, rays_hbm, *refs):
    count = 2 * len(FORWARD) + 3
    outs, scratch = refs[:count], refs[count : 2 * count]
    p_ref, nat, natural, wide, rays_ref, sems, ray_sems = refs[2 * count :]
    patches = rays_hbm.shape[0]
    loads = [pltpu.make_async_copy(rays_hbm.at[p], rays_ref.at[p], ray_sems.at[p]) for p in range(patches)]
    for copy in loads:
        copy.start()
    copies = []

    def send(*places):
        for m in places:
            copy = pltpu.make_async_copy(scratch[m], outs[m], sems.at[m])
            copy.start()
            copies.append(copy)

    last = 2 * len(FORWARD)
    load_flat(flat_ref, p_ref)
    prep_first(p_ref, scratch[last], scratch[last + 1], wide)
    send(last, last + 1)
    for i, k in enumerate(FORWARD):
        natural_rows(k, p_ref, nat, natural)
        forward_weights(k, p_ref, natural, scratch[2 * i], scratch[2 * i + 1])
        send(2 * i, 2 * i + 1)
    for p in range(patches):
        loads[p].wait()
        group_rays(rays_ref, scratch[last + 2], p)
    send(last + 2)
    for copy in copies:
        copy.wait()


def group_rays(rays_ref, out_ref, p):
    rows, rays, cols = rays_ref.shape[1:]
    per = LANES // rays
    quarter = cols // 4
    lane = lanes_iota()
    to = lax.broadcasted_iota(jnp.int32, (cols, cols), 0)
    of = lax.broadcasted_iota(jnp.int32, (cols, cols), 1)
    pick = jnp.where(of == (to % quarter) * 4 + to // quarter, 1.0, 0.0).astype(bf16)
    for r in range(rows // per):
        x = rays_ref[p, per * r : per * (r + 1)].reshape(LANES, cols).astype(f32).astype(bf16)
        turned = lax.dot_general(pick, x, (((1,), (1,)), ((), ())), preferred_element_type=f32)
        parts = [turned[quarter * q : quarter * (q + 1)] for q in range(4)]
        for e in range(per):
            total = turn(parts[0], -rays * e)
            for q in range(1, 4):
                total = jnp.where(lane >= rays * q, turn(parts[q], rays * (q - e)), total)
            out_ref[p, per * r + e] = total.astype(bf16)


def prep(flat, rays):
    count, rows, width, cols = rays.shape
    shapes = []
    for k in FORWARD:
        fs = fwd_shape(k)
        shapes += [jax.ShapeDtypeStruct(fs, bf16), jax.ShapeDtypeStruct((1, fs[1]), f32)]
    shapes += [
        jax.ShapeDtypeStruct((LANES, 2 * LANES), bf16),
        jax.ShapeDtypeStruct((1, 2 * LANES), f32),
        jax.ShapeDtypeStruct((count, rows, cols // 4, 4 * width), bf16),
    ]
    outs = pl.pallas_call(
        prep_kernel,
        out_shape=shapes,
        in_specs=[VMEM, ANY],
        out_specs=[ANY] * len(shapes),
        scratch_shapes=[pltpu.VMEM(v.shape, v.dtype) for v in shapes]
        + [
            pltpu.VMEM((flat_rows(flat.shape[0]), LANES), f32),
            pltpu.VMEM((9 * (C3 + C2), LANES), f32),
            pltpu.VMEM((9 * (C3 + C2), LANES), bf16),
            pltpu.VMEM((LANES, 2 * LANES), f32),
            pltpu.VMEM(rays.shape, jnp.int32),
            pltpu.SemaphoreType.DMA((len(shapes),)),
            pltpu.SemaphoreType.DMA((count,)),
        ],
        name="prep",
        cost_estimate=pl.CostEstimate(flops=10**9, bytes_accessed=2 * 10**7, transcendentals=0),
        compiler_params=pltpu.CompilerParams(vmem_limit_bytes=GRANT),
    )(flat, rays)
    ready = {k: tuple(outs[2 * i : 2 * i + 2]) for i, k in enumerate(FORWARD)}
    ready[0] = tuple(outs[-3:-1])
    return ready, outs[-1]


def tiles_kernel(strips, images_ref, masks_ref, out_ref):
    patches, rows, cols = images_ref.shape
    fold_ = LANES // cols
    high = rows // fold_
    below = out_ref.shape[1] - high
    total = jnp.sum(masks_ref[...].astype(f32).reshape(patches * rows, cols))
    top = jnp.floor(total * (1.0 / 16384.0))
    middle = jnp.floor((total - 16384.0 * top) * (1.0 / 128.0))
    low = total - 16384.0 * top - 128.0 * middle
    lane = lax.broadcasted_iota(jnp.int32, (below, LANES), 1)
    row = lax.broadcasted_iota(jnp.int32, (below, LANES), 0)
    digits = jnp.where(lane == 0, low, jnp.where(lane == 1, middle, jnp.where(lane == 2, top, 0.0)))
    digits = jnp.where(row == 0, digits, 0.0)
    for p in range(patches):
        x = images_ref[p]
        x = jnp.concatenate([x[high * m : high * (m + 1)] for m in range(fold_)], axis=1)
        value = jnp.concatenate([x, digits], axis=0).astype(bf16)
        for s in range(strips):
            out_ref[patches * s + p] = value


def tiles_of(images, masks, strips):
    patches, rows, cols = images.shape
    height = -(-(rows * cols // LANES + 1) // 16) * 16
    return pl.pallas_call(
        functools.partial(tiles_kernel, strips),
        out_shape=jax.ShapeDtypeStruct((strips * patches, height, LANES), bf16),
        in_specs=[VMEM] * 2,
        out_specs=VMEM,
        name="tiles",
    )(images, masks)


def layer_shapes():
    return [(3, 3, 1, C1)] + [(3, 3, *SHAPES[k]) for k in range(1, 11)] + [(FINAL, 1 + RAYS)]


def offset_of(k):
    return sum(math.prod(v) + v[-1] for v in layer_shapes()[:k])


def divisor(count, limit):
    return max(d for d in range(1, min(count, limit) + 1) if count % d == 0)


def mm(a, b):
    return lax.dot_general(a, b, (((1,), (0,)), ((), ())), preferred_element_type=f32)


def mm_t(a, b):
    return lax.dot_general(a, b, (((0,), (0,)), ((), ())), preferred_element_type=f32)


def mm_n(a, b):
    return lax.dot_general(a, b, (((1,), (1,)), ((), ())), preferred_element_type=f32)


def shifted(v):
    zero = jnp.zeros((v.shape[0], 1, v.shape[2]), v.dtype)
    left = jnp.concatenate([zero, v[:, :-1]], axis=1)
    right = jnp.concatenate([v[:, 1:], zero], axis=1)
    return left, right


def lane_of(width=LANES):
    return lax.broadcasted_iota(jnp.int32, (1, 1, width), 2)


def flat2(v):
    return v.reshape(v.shape[0] * v.shape[1], v.shape[2])


def segments(v, three):
    left, right = shifted(v)
    if three:
        return [v, right, left]
    return [v, jnp.where(lane_of() < 64, right, left)]


def rows_of(view):
    return view.reshape(view.shape[0] * 2, *view.shape[2:])


def fours_of(view):
    return view.reshape(view.shape[0] // 2, 2, *view.shape[1:])


def store(view, index, v, three):
    for s, part in enumerate(segments(v, three)):
        view[(*index, s)] = part.astype(bf16)


def lhs_parts(kind, view, base, T, j, repeat):
    segs = range(view.shape[-3])
    if kind == "up":
        at = base + (-1, 0, 0, 1)[j]
        parts = [flat2(view[pl.ds(at, T), s]) for s in segs]
        return parts[:1] + parts if repeat else parts
    p, q = divmod(j + 1, 2)
    return [flat2(view[pl.ds(base + p - 1, T), q, s]) for s in segs]


def lhs_of(sources, r, T, repeat):
    parts = []
    for j in range(4):
        for kind, view, off in sources:
            parts += lhs_parts(kind, view, r + off, T, j, repeat)
    return jnp.concatenate(parts, axis=1)


def each_block(first, last, T, block):
    T = min(T, last - first)
    for i in range(-(-(last - first) // T)):
        block(min(first + i * T, last - T), T)


def clear(view, start, stop):
    def step(i, _):
        view[i] = jnp.zeros(view.shape[1:], view.dtype)

    lax.fori_loop(start, stop, step, None)


def clear_outside(view, count, pad, lo, hi):
    clear(view, 0, pad + jnp.clip(lo, 0, count))
    clear(view, pad + jnp.clip(hi, 0, count), count + 2 * pad)


def silu(u):
    t = jnp.tanh(u)
    a = u * t + u
    return a, (t - a * t) + a


SLOPE_STEP = 1.0 / 26000.0
SLOPE_LOW = 0.125


def pack_slope(v):
    return (v * 13000.0 + (13000.5 + 26000.0 * SLOPE_LOW)).astype(jnp.int32).astype(jnp.int16)


def unpack_slope(v):
    return v.astype(jnp.int32).astype(f32) * SLOPE_STEP - SLOPE_LOW


def split_pair(v, T):
    g = v.shape[0] // T
    half = v.shape[1] // 2
    return [v[:, half * q : half * (q + 1)].reshape(T, g, half) for q in range(2)]


def pooled(x, level):
    lane = lane_of()
    if level == 1:
        near = x + pltpu.roll(x, LANES - C1, 2)
        far = x + pltpu.roll(x, C1, 2)
        left, right = shifted(far)
        return [jnp.where((lane & 32) == 0, near, jnp.where(lane < 64, right, left))]
    y = x + pltpu.roll(x, C2, 2)
    left, right = shifted(y)
    return [jnp.where(lane < 64, y, left), right]


def conv(sources, w, bias, out, slopes, count, lo, valid, three=False, pool=None, limit=BLOCK):
    def block(r, T):
        a, slope = silu(mm(lhs_of(sources, r, T, True), w[...]) + bias[...])
        rows, slope = split_pair(a, T), split_pair(slope, T)
        for q in range(2):
            slopes[pl.ds(r, T), q] = pack_slope(slope[q])
            store(out, (pl.ds(r + 1, T), q), rows[q], three)
        if pool:
            x = sum(v.astype(bf16).astype(f32) for v in rows) * 0.25
            for s, part in enumerate(pooled(x, pool[1])):
                pool[0][pl.ds(r + 2, T), s] = part.astype(bf16)

    each_block(0, count, limit, block)
    clear_outside(out, count, 1, valid[0] - lo, valid[1] - lo)
    if pool:
        clear_outside(pool[0], count, 2, valid[0] - lo, valid[1] - lo)


def first_conv(tiling, own, strip, valid, got, w_ref, bias_ref, out, slopes, xcols, x_ref, xt_ref, v_ref):
    hi, strips, across, per, width = tiling
    count = own // 2 + 22
    rows = own + 2 * HALO
    reach = -(-HALO // per)
    wide = width // across
    high = per * wide // LANES
    x_ref[...] = jnp.zeros(x_ref.shape, f32)
    for d in range(-reach, hi + reach):
        tile = strip * hi + d
        start = HALO + d * per
        first, last = max(0, -start), min(per, rows - start)

        @pl.when((tile >= 0) & (tile < strips * hi))
        def _():
            parts = [got[tile * across + c].astype(f32)[:high] for c in range(across)]
            here = [[v[:, wide * m : wide * (m + 1)] for v in parts] for m in range(LANES // wide)]
            value = jnp.concatenate([jnp.concatenate(v, axis=1) for v in here], axis=0)
            x_ref[start + first : start + last, :] = value[first:last]

    groups = width // 4
    xt_ref[0:EDGE] = jnp.zeros((EDGE, LANES), f32)
    xt_ref[EDGE + width : 2 * EDGE + width] = jnp.zeros((EDGE, LANES), f32)
    xt_ref[EDGE : EDGE + width] = x_ref[...].T
    for m in range(6):
        v_ref[m] = xt_ref[pl.ds(EDGE + m - 1, groups, stride=4), :]
    lane = lax.broadcasted_iota(jnp.int32, (1, LANES), 1)
    many = divisor(count, 6)

    def gather(i, _):
        for u in range(many):
            at = i * many + u
            total = jnp.zeros((groups, LANES), f32)
            for m in range(6):
                turned = pltpu.roll(v_ref[m], 4 * m + LANES - (2 * at + 1), 1)
                total = jnp.where((lane >= 4 * m) & (lane < 4 * m + 4), turned, total)
            xcols[at] = total.astype(bf16)

    lax.fori_loop(0, count // many, gather, None)
    def block(r, T):
        a, slope = silu(mm(flat2(xcols[pl.ds(r, T)]), w_ref[...]) + bias_ref[...])
        rows_, slope = split_pair(a, T), split_pair(slope, T)
        for q in range(2):
            slopes[pl.ds(r, T), q] = pack_slope(slope[q])
            store(out, (pl.ds(r + 1, T), q), rows_[q], False)

    each_block(0, count, BLOCK, block)
    clear_outside(out, count, 1, valid[0] + 11, valid[1] + 11)


def act_shapes(own, groups):
    h, h2, h3 = own // 2, own // 4, own // 8
    pairs = dict(
        a0=(h + 24, 2), s1=(h + 22, 2), p1=(h2 + 12, 1), a2=(h2 + 12, 2), s2=(h2 + 10, 2), p2=(h3 + 6, 2),
        a4=(h3 + 6, 3), t3=(h3 + 4, 3), a6=(h2 + 6, 2), t2=(h2 + 4, 2), a8=(h + 4, 2), a9=(h + 4, 2),
    )
    shapes = {k: (n, 2, segs, groups, LANES) for k, (n, segs) in pairs.items()}
    shapes["xc"] = (h + 22, groups, LANES)
    return shapes


def slope_shapes(own, groups):
    h, h2, h3 = own // 2, own // 4, own // 8
    counts = [h + 22, h + 20, h2 + 10, h2 + 8, h3 + 4, h3 + 2, h2 + 4, h2 + 2, h + 2, h + 2]
    return {f"sl{k}": (n, 2, groups, LANES) for k, n in enumerate(counts)}


def grad_shapes(own, groups):
    h, h2, h3 = own // 2, own // 4, own // 8
    pairs = {
        10: (h + 4, 6), 9: (h + 6, 2), 8: (h + 6, 2), 7: (h2 + 6, 2), 6: (h2 + 8, 2), 5: (h3 + 6, 3),
        4: (h3 + 8, 3), 3: (h2 + 12, 2), 2: (h2 + 14, 2), 1: (h + 24, 2), 0: (h + 22, 1),
    }
    return {f"g{k}": (n, 2, segs, groups, LANES) for k, (n, segs) in pairs.items()}


def loss_scales(got, tiling, pixels, scal_ref):
    _, _, across, per, width = tiling
    high = per * (width // across) // LANES
    digits = jnp.sum(got[...].astype(f32), axis=0)[high : high + 1, :]
    lane = lanes_iota()
    digits = jnp.where(lane == 0, digits, jnp.where(lane == 1, 128.0 * digits, 16384.0 * digits))
    fg = jnp.sum(jnp.where(lane < 3, digits, 0.0), axis=1, keepdims=True) * jnp.ones((1, LANES), f32)
    scal_ref[0:1] = 0.5 / fg
    scal_ref[1:2] = 0.5 / (pixels - fg)
    scal_ref[2:3] = 1.0 / (fg * RAYS)
    scal_ref[3:4] = fg


def forward_kernel(cfg, sc, got, w0, b0, *refs):
    own, tiling = cfg["own"], cfg["tiling"]
    h, h2, h3 = own // 2, own // 4, own // 8
    refs = list(refs)
    take = lambda m: [refs.pop(0) for _ in range(m)]
    w_hbm, bias = take(9), take(9)
    names = list(cfg["outs"])
    outs = dict(zip(names, take(len(names))))
    scal_ref = take(1)[0]
    here = dict(zip(names, take(len(names))))
    w_vmem = take(9)
    x_ref, xt_ref, v_ref, w_sem, out_sem = refs
    fetch = {}
    for i, k in enumerate(FORWARD):
        fetch[k] = pltpu.make_async_copy(w_hbm[i], w_vmem[i], w_sem.at[i])
        fetch[k].start()
    sent = []

    def send(*keys):
        for key in keys:
            copy = pltpu.make_async_copy(here[key], outs[key], out_sem.at[names.index(key)])
            copy.start()
            sent.append(copy)

    v1, v2, v3 = [(sc[2 * i], sc[2 * i + 1]) for i in range(3)]
    loss_scales(got, tiling, cfg["pixels"], scal_ref)
    first_conv(tiling, own, sc[6], v1, got, w0, b0, here["a0"], here["sl0"], here["xc"],
               x_ref, xt_ref, v_ref)
    send("a0", "sl0", "xc")

    def layer(k, out, sources, count, lo, valid, three=False, pool=None):
        fetch[k].wait()
        conv(sources, w_vmem[k - 1], bias[k - 1], here[out], here[f"sl{k}"], count, lo, valid, three, pool)
        send(out, f"sl{k}")

    layer(1, "s1", [(PAIR, here["a0"], 2)], h + 20, -10, v1, pool=(rows_of(here["p1"]), 1))
    send("p1")
    layer(2, "a2", [(PAIR, here["p1"], 1)], h2 + 10, -5, v2)
    layer(3, "s2", [(PAIR, here["a2"], 2)], h2 + 8, -4, v2, pool=(rows_of(here["p2"]), 2))
    send("p2")
    layer(4, "a4", [(PAIR, here["p2"], 1)], h3 + 4, -2, v3, True)
    layer(5, "t3", [(PAIR, here["a4"], 2)], h3 + 2, -1, v3, True)
    layer(6, "a6", [("up", rows_of(here["t3"]), 2), (PAIR, here["s2"], 3)], h2 + 4, -2, v2)
    layer(7, "t2", [(PAIR, here["a6"], 2)], h2 + 2, -1, v2)
    layer(8, "a8", [("up", rows_of(here["t2"]), 3), (PAIR, here["s1"], 10)], h + 2, -1, v1)
    layer(9, "a9", [(PAIR, here["a8"], 1)], h + 2, -1, v1)
    for copy in sent:
        copy.wait()


def forward(sc, got, ready, own, tiling, pixels):
    groups = tiling[-1] // 4
    shapes = {k: jax.ShapeDtypeStruct(v, bf16) for k, v in act_shapes(own, groups).items()}
    shapes |= {k: jax.ShapeDtypeStruct(v, jnp.int16) for k, v in slope_shapes(own, groups).items()}
    weights = [ready[k][0] for k in FORWARD]
    biases = [ready[k][1] for k in FORWARD]
    width = tiling[-1]
    outs = pl.pallas_call(
        functools.partial(forward_kernel, dict(own=own, tiling=tiling, outs=tuple(shapes), pixels=float(pixels))),
        out_shape=[*shapes.values(), jax.ShapeDtypeStruct((8, LANES), f32)],
        in_specs=[SMEM] + [VMEM] * 3 + [ANY] * 9 + [VMEM] * 9,
        out_specs=[ANY] * len(shapes) + [VMEM],
        scratch_shapes=[pltpu.VMEM(v.shape, v.dtype) for v in shapes.values()]
        + [pltpu.VMEM(w.shape, bf16) for w in weights]
        + [
            pltpu.VMEM((LANES, width), f32),
            pltpu.VMEM((width + 2 * EDGE, LANES), f32),
            pltpu.VMEM((6, groups, LANES), f32),
            pltpu.SemaphoreType.DMA((9,)),
            pltpu.SemaphoreType.DMA((len(shapes),)),
        ],
        name="forward",
        cost_estimate=pl.CostEstimate(flops=2 * 10**10, bytes_accessed=5 * 10**7, transcendentals=10**7),
        compiler_params=pltpu.CompilerParams(vmem_limit_bytes=GRANT),
    )(sc, got, *ready[0], *weights, *biases)
    return dict(zip(shapes, outs)), outs[-1]


def sum_back(k, acc):
    ci, co = SHAPES[k]
    n = COLS[k]
    pieces = {}
    for a in range(3):
        value = acc(a)
        base = start = 0
        for segs, ch in INPUTS[k]:
            if segs is UP2:
                unique = [[(0, 1), (2, 3)], [(4,), (-1,)]]
            elif segs is UP3:
                unique = [[(0, 1)], [(2,)], [(-1,)]]
            else:
                unique = [[() if c is None else (c,) for c in seg] for seg in segs]
            uses = {}
            for seg in unique:
                for columns in seg:
                    for col in columns:
                        for p in range(n):
                            c = col - p + 1
                            if 0 <= c <= 2:
                                uses.setdefault(c, []).append((base, p))
                    base += ch
            for c, places in uses.items():
                total = None
                for row, p in places:
                    piece = value[row : row + ch, p * co : (p + 1) * co]
                    total = piece if total is None else total + piece
                pieces[(a * 3 + c) * ci + start] = total
            start += ch
    return pieces


def place(out, value, offset):
    out, base = out
    row, lane0 = divmod(offset - base * LANES, LANES)
    n = value.shape[0]
    if lane0 == 0:
        out[row : row + n, :] += value
        return
    lane = lax.broadcasted_iota(jnp.int32, (1, LANES), 1)
    turned = pltpu.roll(value, lane0, 1)
    out[row : row + n, :] += jnp.where(lane >= lane0, turned, 0.0)
    out[row + 1 : row + 1 + n, :] += jnp.where(lane < lane0, turned, 0.0)


def fold(row, co):
    total = row[:, 0:LANES]
    for m in range(1, row.shape[1] // LANES):
        total = total + row[:, LANES * m : LANES * (m + 1)]
    width = LANES
    while width > co:
        width //= 2
        total = total + pltpu.roll(total, width, 1)
    lane = lax.broadcasted_iota(jnp.int32, (1, LANES), 1)
    return jnp.where(lane < co, total, 0.0)


def place_layer(k, pieces, db, nat, out):
    ci, co = SHAPES[k]
    n = 9 * ci * co // LANES
    fill = LANES // co
    for row, total in pieces.items():
        nat[row : row + total.shape[0], 0:co] = total
    if fill == 1:
        value = nat[0:n, :]
    else:
        value = jnp.concatenate([nat[pl.ds(m, n, stride=fill), :][:, :co] for m in range(fill)], axis=1)
    place(out, value, offset_of(k))
    place(out, fold(db, co), offset_of(k) + 9 * ci * co)


def head_part(own, scal, x, w, bias, hw, hwt, hb, rays, grad, acc, dhead, nat, out):
    _, cols, per = rays.shape[:3]
    x, grad = rows_of(x), rows_of(grad)
    groups = x.shape[2]
    T = divisor(math.gcd(own, per), HEAD_ROWS)
    M = T * groups
    fg_scale, bg_scale, ray_scale_ = scal[0:1], scal[1:2], scal[2:3]
    lane = lax.broadcasted_iota(jnp.int32, (1, LANES), 1)
    is_logit = (lane & 31) == 0
    ones = jnp.ones((8, M), bf16)
    dhead[...] = jnp.zeros(dhead.shape, f32)

    def block(i, carry):
        dbh, fg_loss, bg_loss, ray_loss = carry
        r = i * T
        slabs = [
            jnp.concatenate([flat2(x[pl.ds(r + 4 + d, T), s]) for s in range(2)], axis=1) for d in (-1, 0, 1)
        ]
        a, slope = silu(mm(jnp.concatenate(slabs, axis=1), w[...]) + bias[...])
        slope = 0.5 + 0.5 * slope
        feat = a.astype(bf16)
        head = mm(feat, hw[...]) + hb[...]
        dist, logit = head[:, :LANES], head[:, LANES:]
        part, first = r // per, r % per
        ray = jnp.concatenate([rays[part, c, pl.ds(first, T)] for c in range(cols)], axis=1)
        ray = flat2(ray.astype(f32))
        y = jnp.where(ray > 0.0, 1.0, 0.0)
        diff = dist - ray * (1.0 / ray_scale)
        smooth = jnp.sqrt(diff * diff + 1.0)
        g_dist = diff / smooth * (y * ray_scale_)
        cross = jnp.maximum(logit, 0.0) - logit * y + jnp.log(1.0 + jnp.exp(-jnp.abs(logit)))
        cross = jnp.where(is_logit, cross, 0.0)
        sig = 1.0 / (1.0 + jnp.exp(-logit))
        g_logit = jnp.where(is_logit, (sig - y) * (y * fg_scale + (1.0 - y) * bg_scale), 0.0)
        fg_loss += jnp.sum((cross * y).reshape(M // 8, 8, LANES), axis=0)
        bg_loss += jnp.sum((cross * (1.0 - y)).reshape(M // 8, 8, LANES), axis=0)
        ray_loss += jnp.sum((smooth * y).reshape(M // 8, 8, LANES), axis=0)
        g_head = jnp.concatenate([g_dist, g_logit], axis=1).astype(bf16)
        dhead[...] += mm_t(feat, g_head)
        gz = mm(g_head, hwt[...]) * slope
        center = gz.astype(bf16)
        for s in range(4):
            grad[pl.ds(r + 4, T), s] = center[:, LANES * s : LANES * (s + 1)].reshape(T, groups, LANES)
        left = shifted(gz[:, 3 * LANES :].reshape(T, groups, LANES))[0]
        right = shifted(gz[:, :LANES].reshape(T, groups, LANES))[1]
        grad[pl.ds(r + 4, T), 4] = right.astype(bf16)
        grad[pl.ds(r + 4, T), 5] = left.astype(bf16)
        return dbh + mm(ones, g_head), fg_loss, bg_loss, ray_loss

    zero = jnp.zeros((8, LANES), f32)
    start = (jnp.zeros((8, 2 * LANES), f32), zero, zero, zero)
    carry = start
    for i in range(own // T):
        carry = block(i, carry)
    dbh, *losses = carry
    clear(grad, 0, 4)
    clear(grad, own + 4, own + 8)
    g = jnp.concatenate([flat2(grad[pl.ds(4, own), s]) for s in range(4)], axis=1)
    for a in range(3):
        acc[a] = mm_t(jnp.concatenate([flat2(x[pl.ds(3 + a, own), s]) for s in range(2)], axis=1), g)
    db = mm(jnp.ones((8, own * groups), bf16), g)
    place_layer(10, sum_back(10, lambda a: acc[a]), db[0:1], nat, out)
    both = jnp.zeros((FINAL, LANES), f32)
    for q in range(4):
        rows = dhead[FINAL * q : FINAL * (q + 1), :]
        piece, first = rows[:, :LANES], rows[:, LANES:]
        if q:
            piece = pltpu.roll(piece, LANES - RAYS * q, 1)
            first = pltpu.roll(first, LANES - RAYS * q, 1)
        both += jnp.where(lane == 0, first, pltpu.roll(piece, 1, 1))
    wide = 1 + RAYS
    nat[0:FINAL, :] = jnp.where(lane < wide, both, 0.0)
    at = offset_of(11)
    flat, base = out
    for e in range(FINAL):
        row, lane0 = divmod(at - base * LANES + wide * e, LANES)
        value = pltpu.roll(nat[e : e + 1, :], lane0, 1) if lane0 else nat[e : e + 1, :]
        if lane0 + wide <= LANES:
            flat[row : row + 1, :] += value
        else:
            flat[row : row + 1, :] += jnp.where(lane >= lane0, value, 0.0)
            flat[row + 1 : row + 2, :] += jnp.where(lane < lane0, value, 0.0)
    dist_sum, logit_sum = fold(dbh[0:1, :LANES], RAYS), fold(dbh[0:1, LANES:], RAYS)
    value = jnp.where(lane == 0, logit_sum, pltpu.roll(dist_sum, 1, 1))
    place(out, jnp.where(lane < wide, value, 0.0), at + FINAL * wide)
    terms = jnp.zeros((1, LANES), f32)
    for m, part in enumerate(losses):
        terms = jnp.where(lane == m, jnp.sum(part), terms)
    place(out, terms, offset_of(12))


def weight_grad(k, sources, grad, count, acc, nat, out):
    rows = sum(v.shape[-3] for _, v, _ in sources) * LANES
    groups = grad.shape[3]
    g = jnp.concatenate([flat2(grad[pl.ds(2, count), q, 0]) for q in range(2)], axis=1)
    for j in range(4):
        parts = []
        for kind, view, off in sources:
            parts += lhs_parts(kind, view, off, count, j, False)
        acc[j, 0:rows] = mm_t(jnp.concatenate(parts, axis=1), g)
    db = mm(jnp.ones((8, count * groups), bf16), g)
    pieces = sum_back(k, lambda a: acc[a, 0:rows, 0:LANES] + acc[a + 1, 0:rows, LANES : 2 * LANES])
    place_layer(k, pieces, db[0:1], nat, out)


def input_grad(mode, grad, goff, w, slopes, out, count, valid, lo, three=False, extra=None, side=None, limit=BLOCK):
    def block(r, T):
        groups = grad.shape[3]
        acc = mm_n(lhs_of([(PAIR, grad, goff)], r, T, False), w[...])
        if mode == JOIN:
            parts = [acc[:, LANES * m : LANES * (m + 1)].reshape(T, groups, LANES) for m in range(6)]
            gz = ((parts[0] + parts[1]) + (parts[3] + parts[4])) * unpack_slope(slopes[pl.ds(r, T)])
            store(out, (pl.ds(r + 4, T),), gz, three)
            for q in range(2):
                side[pl.ds(r, T), q] = parts[2 + 3 * q]
            return
        vals = split_pair(acc, T)
        for q in range(2):
            if mode == POOL:
                for e in range(2):
                    total = vals[q] * 0.25
                    if start <= r < stop:
                        total += extra[pl.ds(r - start, T), q, e]
                    store(out, (pl.ds(r + 1, T), q, e), total * unpack_slope(slopes[pl.ds(r, T), q, e]), three)
                continue
            gz = vals[q] * unpack_slope(slopes[pl.ds(r, T), q])
            if mode == LAST:
                out[pl.ds(r, T), q, 0] = gz.astype(bf16)
            else:
                store(out, (pl.ds(r + 2, T), q), gz, three)

    start = stop = 0
    if mode == POOL:
        start = (count - extra.shape[0]) // 2
        stop = start + extra.shape[0]
    for first, last in ((0, start), (start, stop), (stop, count)):
        if first < last:
            each_block(first, last, limit, block)
    low, high = valid[0] - lo, valid[1] - lo
    if mode == PLAIN:
        clear_outside(out, count, 2, low, high)
    elif mode == LAST:
        clear_outside(out, count, 0, low, high)
    elif mode == JOIN:
        clear_outside(out, count, 4, low, high)
    else:
        clear_outside(out, count, 1, low // 2, high // 2)


def first_grad(grad, xcols, count, out, tmp):
    groups = grad.shape[3]

    def block(r, T, carry):
        g = jnp.concatenate([flat2(grad[pl.ds(r, T), q, 0]) for q in range(2)], axis=1)
        return carry[0] + mm_t(flat2(xcols[pl.ds(r, T)]), g), carry[1] + mm(jnp.ones((8, T * groups), bf16), g)

    T = divisor(count, 18)
    start = (jnp.zeros((LANES, 2 * LANES), f32), jnp.zeros((8, 2 * LANES), f32))
    dw, db = lax.fori_loop(0, count // T, lambda i, c: block(i * T, T, c), start)
    tmp[...] = jnp.zeros(tmp.shape, f32)
    for a in range(3):
        for c in range(3):
            total = None
            for q in range(2):
                for p in range(4):
                    m, j = p + c, a + q
                    at = (q * 4 + p) * C1
                    piece = dw[4 * m + j : 4 * m + j + 1, at : at + C1]
                    total = piece if total is None else total + piece
            row, at = divmod((a * 3 + c) * C1, LANES)
            tmp[row : row + 1, at : at + C1] = total
    place(out, tmp[...], 0)
    place(out, fold(db[0:1], C1), 9 * C1)


def arena_plan(own, groups, places):
    sizes = act_shapes(own, groups) | grad_shapes(own, groups)
    tiles = {k: math.prod(v[:-2]) for k, v in sizes.items()}
    at, top = {}, 0
    for lists in places:
        ends = []
        for names in lists:
            spot = top
            for name in names:
                at[name] = spot
                spot += tiles[name]
            ends.append(spot)
        top = max(ends)
    return sizes, tiles, at, top


SLOTS = {k: "x" if k in (8, 6) else "y" for k in SHAPES}
DEEP = dict(
    acts=("a9", "a8", "t2", "s1", "a6", "t3", "s2", "a4", "p2"),
    slopes=("sl9", "sl8", "sl7", "sl6", "sl5", "sl4"),
    layers=(10, 9, 8, 7, 6, 5),
    places=([["g10"]], [["g9"], ["g7"], ["g5"]], [["g8"], ["g6"], ["g4"]], [["a9", "a8"]], [["t2", "s1"]],
            [["a6", "t3", "s2", "a4", "p2"]]),
)
SHALLOW = dict(
    acts=("a2", "p1", "a0", "xc"),
    slopes=("sl3", "sl2", "sl1", "sl0"),
    layers=(4, 3, 2, 1),
    places=([["g4"]], [["g3"]], [["g2"]], [["g1"]], [["g0"]], [["a2", "p1", "a0", "xc"]]),
)
SPLIT = 504
STRIPS = 4


def split_rows():
    plane, strips = lax.axis_size(HI) * lax.axis_size(SIDE), lax.axis_size(STRIP)
    share = 16 * plane
    low = -(-offset_of(4) // (LANES * share)) * share
    share *= strips
    return -(-(offset_of(12) + 3 - SPLIT * LANES) // (LANES * share)) * share, low


class Part:
    def __init__(self, stage, plan, arena, slopes, slots, hbm, sems, p_ref, nat, natural):
        self.stage, self.arena, self.slopes, self.hbm, self.sems = stage, arena, slopes, hbm, sems
        self.sizes, self.tiles, self.at, _ = plan
        self.slots, self.p_ref, self.nat, self.natural = slots, p_ref, nat, natural
        self.copies = {}

    def view(self, name):
        return self.arena.at[pl.ds(self.at[name], self.tiles[name])].reshape(*self.sizes[name])

    def fetch(self, key, target=None):
        if target is None:
            target = self.slopes[key] if key in self.slopes else self.view(key)
        copy = pltpu.make_async_copy(self.hbm[key], target, self.sems.at[list(self.hbm).index(key)])
        copy.start()
        self.copies[key] = copy

    def need(self, *keys):
        for key in keys:
            self.copies[key].wait()

    def weight(self, k):
        rows, lanes = back_shape(k)
        ref = self.slots[SLOTS[k]].at[pl.ds(0, rows), pl.ds(0, lanes)]
        natural_rows(k, self.p_ref, self.nat, self.natural)
        backward_weights(k, self.natural, ref)
        return ref


def deep_kernel(cfg, sc, scal, flat_ref, *refs):
    own, groups = cfg["own"], cfg["groups"]
    h, h2, h3 = own // 2, own // 4, own // 8
    refs = list(refs)
    take = lambda m: [refs.pop(0) for _ in range(m)]
    names = DEEP["acts"] + DEEP["slopes"]
    hbm = dict(zip(names, take(len(names))))
    rays = take(1)[0]
    keep_hbm, send_hbm, g4_hbm, gs1_hbm, gs2_hbm = take(5)
    arena = take(1)[0]
    slopes = dict(zip(DEEP["slopes"], take(len(DEEP["slopes"]))))
    slots = dict(zip("yx", take(2)))
    p_ref, w10, bias10, hw, hwt, hb, gs1, gs2, acc, acc10, dhead, nat, natural, flat, sems, out_sems = refs
    part = Part(DEEP, cfg["plan"], arena, slopes, slots, hbm, sems, p_ref, nat, natural)
    view, need = part.view, part.need
    part.fetch("a9")
    for key in ("sl9", "a8", "sl8", "t2", "s1", "sl7", "a6", "sl6", "t3", "s2", "sl5", "a4", "sl4", "p2"):
        part.fetch(key)
    out = (flat, SPLIT)
    flat[...] = jnp.zeros(flat.shape, f32)
    v1, v2, v3 = [(sc[2 * i], sc[2 * i + 1]) for i in range(3)]
    load_flat(flat_ref, p_ref)
    natural_rows(10, p_ref, nat, natural)
    forward_weights(10, p_ref, natural, w10, bias10)
    prep_head(p_ref, hw, hwt, hb, nat)
    need("a9")
    head_part(own, scal, view("a9"), w10, bias10, hw, hwt, hb, rays, view("g10"), acc10, dhead, nat, out)

    weight = part.weight(10)
    need("sl9")
    input_grad(PLAIN, view("g10"), 1, weight, slopes["sl9"], view("g9"), h + 2, v1, -1)

    need("a8", "sl8")
    weight_grad(9, [(PAIR, view("a8"), 1)], view("g9"), h + 2, acc, nat, out)
    weight = part.weight(9)
    input_grad(PLAIN, view("g9"), 2, weight, slopes["sl8"], view("g8"), h + 2, v1, -1)

    need("t2", "s1", "sl7")
    weight_grad(8, [("up", rows_of(view("t2")), 3), (PAIR, view("s1"), 10)], view("g8"), h + 2, acc, nat, out)
    weight = part.weight(8)
    input_grad(JOIN, view("g8"), 1, weight, rows_of(slopes["sl7"]), rows_of(view("g7")), h + 4, v1, -2,
               side=gs1)
    outs = [pltpu.make_async_copy(gs1, gs1_hbm, out_sems.at[0])]
    outs[0].start()

    need("a6", "sl6")
    weight_grad(7, [(PAIR, view("a6"), 2)], view("g7"), h2 + 2, acc, nat, out)
    weight = part.weight(7)
    input_grad(PLAIN, view("g7"), 1, weight, slopes["sl6"], view("g6"), h2 + 4, v2, -2)

    need("t3", "s2", "sl5")
    weight_grad(6, [("up", rows_of(view("t3")), 2), (PAIR, view("s2"), 3)], view("g6"), h2 + 4, acc, nat, out)
    weight = part.weight(6)
    input_grad(JOIN, view("g6"), 2, weight, rows_of(slopes["sl5"]), rows_of(view("g5")), h2 + 4, v2, -2,
               three=True, side=gs2)
    outs.append(pltpu.make_async_copy(gs2, gs2_hbm, out_sems.at[1]))
    outs[-1].start()

    need("a4", "sl4")
    weight_grad(5, [(PAIR, view("a4"), 2)], view("g5"), h3 + 2, acc, nat, out)
    weight = part.weight(5)
    input_grad(PLAIN, view("g5"), 1, weight, slopes["sl4"], view("g4"), h3 + 4, v3, -2, three=True)

    outs.append(pltpu.make_async_copy(view("g4"), g4_hbm, out_sems.at[2]))
    outs[-1].start()

    need("p2")
    weight_grad(4, [(PAIR, view("p2"), 1)], view("g4"), h3 + 4, acc, nat, out)
    half = flat.shape[0] // 2
    for m, (core, target) in enumerate(((sc[7], keep_hbm), (1 - sc[7], send_hbm))):
        rows = pl.ds(pl.multiple_of(core * half, 8), half)
        outs.append(pltpu.make_async_copy(flat.at[rows], target, out_sems.at[3 + m]))
        outs[-1].start()
    for copy in outs:
        copy.wait()


def stage_scratch(stage, own, groups, plan, params):
    def slot(s):
        return tuple(max([back_shape(k)[d] for k in stage["layers"] if SLOTS[k] == s] + [8]) for d in (0, 1))

    slopes = slope_shapes(own, groups)
    return (
        [pltpu.VMEM((plan[3], groups, LANES), bf16)]
        + [pltpu.VMEM(slopes[k], jnp.int16) for k in stage["slopes"]]
        + [pltpu.VMEM(slot(s), bf16) for s in "yx" if any(SLOTS[k] == s for k in stage["layers"])]
        + [pltpu.VMEM((flat_rows(params.shape[0]), LANES), f32)]
    )


def deep(sc, scal, params, kept, rays, own, groups):
    plan = arena_plan(own, groups, DEEP["places"])
    h, h2 = own // 2, own // 4
    args = [kept[k] for k in DEEP["acts"] + DEEP["slopes"]] + [rays]
    rows = split_rows()[0]
    gs1, gs2 = (h + 4, 2, groups, LANES), (h2 + 4, 2, groups, LANES)
    return pl.pallas_call(
        functools.partial(deep_kernel, dict(own=own, groups=groups, plan=plan)),
        out_shape=[
            jax.ShapeDtypeStruct((rows // 2, LANES), f32),
            jax.ShapeDtypeStruct((rows // 2, LANES), f32),
            jax.ShapeDtypeStruct(grad_shapes(own, groups)["g4"], bf16),
            jax.ShapeDtypeStruct(gs1, f32),
            jax.ShapeDtypeStruct(gs2, f32),
        ],
        in_specs=[SMEM, VMEM, VMEM] + [ANY] * (len(args) - 1) + [VMEM],
        out_specs=[ANY] * 5,
        scratch_shapes=stage_scratch(DEEP, own, groups, plan, params)
        + [
            pltpu.VMEM(fwd_shape(10), bf16),
            pltpu.VMEM((1, fwd_shape(10)[1]), f32),
            pltpu.VMEM((4 * FINAL, 2 * LANES), bf16),
            pltpu.VMEM((2 * LANES, 4 * FINAL), bf16),
            pltpu.VMEM((1, 2 * LANES), f32),
            pltpu.VMEM(gs1, f32),
            pltpu.VMEM(gs2, f32),
            pltpu.VMEM((4, 5 * LANES, 2 * LANES), f32),
            pltpu.VMEM((3, 2 * LANES, 4 * FINAL), f32),
            pltpu.VMEM((4 * FINAL, 2 * LANES), f32),
            pltpu.VMEM((9 * (C3 + C2), LANES), f32),
            pltpu.VMEM((9 * (C3 + C2), LANES), bf16),
            pltpu.VMEM((rows, LANES), f32),
            pltpu.SemaphoreType.DMA((len(args),)),
            pltpu.SemaphoreType.DMA((5,)),
        ],
        name="deep",
        cost_estimate=pl.CostEstimate(flops=5 * 10**10, bytes_accessed=5 * 10**7, transcendentals=10**7),
        compiler_params=pltpu.CompilerParams(vmem_limit_bytes=GRANT - 5 * 2**20),
    )(sc, scal, params, *args)


def shallow_kernel(cfg, sc, flat_ref, *refs):
    own, groups = cfg["own"], cfg["groups"]
    h, h2, h3 = own // 2, own // 4, own // 8
    refs = list(refs)
    take = lambda m: [refs.pop(0) for _ in range(m)]
    names = SHALLOW["acts"] + SHALLOW["slopes"] + ("g4", "gs1", "gs2")
    hbm = dict(zip(names, take(len(names))))
    flat, arena = take(2)
    slopes = dict(zip(SHALLOW["slopes"], take(len(SHALLOW["slopes"]))))
    slots = dict(zip("y", take(1)))
    p_ref, gs1, gs2, acc, nat, natural, tmp, sems = refs
    part = Part(SHALLOW, cfg["plan"], arena, slopes, slots, hbm, sems, p_ref, nat, natural)
    view, need = part.view, part.need
    part.fetch("g4")
    part.fetch("sl3")
    part.fetch("gs2", gs2)
    for key in ("a2", "sl2", "p1", "sl1"):
        part.fetch(key)
    part.fetch("gs1", gs1)
    for key in ("a0", "sl0", "xc"):
        part.fetch(key)
    out = (flat, 0)
    flat[...] = jnp.zeros(flat.shape, f32)
    v1, v2 = [(sc[2 * i], sc[2 * i + 1]) for i in range(2)]
    load_flat(flat_ref, p_ref)
    weight = part.weight(4)
    need("g4", "sl3", "gs2")
    input_grad(POOL, view("g4"), 2, weight, fours_of(slopes["sl3"]), fours_of(view("g3")), h3 + 4, v2, -4,
               extra=fours_of(gs2))

    need("a2", "sl2")
    weight_grad(3, [(PAIR, view("a2"), 2)], view("g3"), h2 + 8, acc, nat, out)
    weight = part.weight(3)
    input_grad(PLAIN, view("g3"), 1, weight, slopes["sl2"], view("g2"), h2 + 10, v2, -5)

    need("p1", "sl1", "gs1")
    weight_grad(2, [(PAIR, view("p1"), 1)], view("g2"), h2 + 10, acc, nat, out)
    weight = part.weight(2)
    input_grad(POOL, view("g2"), 2, weight, fours_of(slopes["sl1"]), fours_of(view("g1")), h2 + 10, v1, -10,
               extra=fours_of(gs1))

    need("a0", "sl0", "xc")
    weight_grad(1, [(PAIR, view("a0"), 2)], view("g1"), h + 20, acc, nat, out)
    weight = part.weight(1)
    input_grad(LAST, view("g1"), 1, weight, slopes["sl0"], view("g0"), h + 22, v1, -11)
    first_grad(view("g0"), view("xc"), h + 22, out, tmp)


def shallow(sc, params, kept, g4, gs1, gs2, own, groups):
    plan = arena_plan(own, groups, SHALLOW["places"])
    args = [kept[k] for k in SHALLOW["acts"] + SHALLOW["slopes"]] + [g4, gs1, gs2]
    span = flat_range(SHALLOW["layers"], params.shape[0])
    return pl.pallas_call(
        functools.partial(shallow_kernel, dict(own=own, groups=groups, plan=plan, range=span)),
        out_shape=jax.ShapeDtypeStruct((split_rows()[1], LANES), f32),
        in_specs=[SMEM, VMEM] + [ANY] * len(args),
        out_specs=VMEM,
        scratch_shapes=stage_scratch(SHALLOW, own, groups, plan, params)
        + [
            pltpu.VMEM(gs1.shape, f32),
            pltpu.VMEM(gs2.shape, f32),
            pltpu.VMEM((4, 2 * LANES, 2 * LANES), f32),
            pltpu.VMEM((9 * C3, LANES), f32),
            pltpu.VMEM((9 * C3, LANES), bf16),
            pltpu.VMEM((8, LANES), f32),
            pltpu.SemaphoreType.DMA((len(args),)),
        ],
        name="shallow",
        cost_estimate=pl.CostEstimate(flops=2 * 10**10, bytes_accessed=2 * 10**7, transcendentals=10**7),
        compiler_params=pltpu.CompilerParams(vmem_limit_bytes=GRANT),
    )(sc, params, *args)


def add_up(value, n):
    return value.reshape(n, -1, LANES).sum(0)


def gather_up(value, axes, n):
    return lax.all_to_all(jnp.tile(value, (n, 1)), axes, 0, 0, tiled=True)


def from_others(value):
    strips = lax.axis_size(STRIP)
    if strips != STRIPS:
        whole = gather_up(value, (STRIP,), strips).reshape(strips, *value.shape)
        return [whole[t] for t in range(strips)]
    swaps = [[(i, i ^ x) for i in range(strips)] for x in range(1, strips)]
    return [value] + [lax.ppermute(value, STRIP, swap) for swap in swaps]


def tree_sum(values):
    while len(values) > 1:
        values = [a + b for a, b in zip(values[::2], values[1::2])] + values[len(values) // 2 * 2 :]
    return values[0]


def scatter_up(value):
    strips = lax.axis_size(STRIP)
    if strips != STRIPS:
        return add_up(lax.all_to_all(value, (STRIP,), 0, 0, tiled=True), strips)
    strip = lax.axis_index(STRIP)
    share = value.shape[0] // strips
    parts = [lax.dynamic_slice_in_dim(value, (strip ^ x) * share, share) for x in range(strips)]
    swaps = [[(i, i ^ x) for i in range(strips)] for x in range(strips)]
    return tree_sum(parts[:1] + [lax.ppermute(parts[x], STRIP, swaps[x]) for x in range(1, strips)])


def sum_all(keep, send, low_of):
    plane = lax.axis_size(HI) * lax.axis_size(SIDE)
    swap = [(0, 1), (1, 0)]
    part = keep + lax.ppermute(send, CORE, swap)
    part = lax.all_to_all(part, (HI, SIDE), 0, 0, tiled=True)
    part, low = lax.optimization_barrier((part, low_of()))
    low = lax.all_to_all(low, (CORE, HI, SIDE), 0, 0, tiled=True)
    high = from_others(scatter_up(add_up(part, plane)))
    high, low = lax.optimization_barrier((high, low))
    low = tree_sum(from_others(add_up(low, 2 * plane)))
    part = gather_up(jnp.concatenate([*high, low], axis=0), (HI, SIDE), plane)
    return part, lax.ppermute(part, CORE, swap)


def adam_kernel(chunks, low_rows, sc, mine, other, weights, first, second, *refs):
    outs, loss_ref, norm_ref, grads, news, sems = refs[:3], refs[3], refs[4], refs[5], refs[6:9], refs[9]
    size = weights.shape[0]
    plane, strips = chunks
    low_share = low_rows // (2 * plane)
    step_ = mine.shape[0] // plane
    share = (step_ - low_share) // strips
    for c, parts in enumerate(((mine, other), (other, mine))):

        @pl.when(sc[7] == c)
        def _():
            for m, ref in enumerate(parts):
                for n in range(plane):
                    for t in range(strips):
                        slot = sc[6] ^ t if strips == STRIPS else t
                        row = SPLIT + ((m * plane + n) * strips + t) * share
                        grads[row : row + share] = ref[pl.ds(pl.multiple_of(n * step_ + slot * share, 8), share)]
            for m, ref in enumerate(parts):
                for n in range(plane):
                    start = n * step_ + strips * share
                    row = (m * plane + n) * low_share
                    same = min(max(SPLIT - row, 0), low_share)
                    if same:
                        grads[row : row + same] = ref[start : start + same]
                    if same < low_share:
                        grads[row + same : row + low_share] += ref[start + same : start + low_share]

    whole = size // 1024
    many = divisor(whole, 25)
    steps = whole // many

    def square(i, total):
        g = grads[pl.ds(pl.multiple_of(i * many * 8, 8), many * 8), :]
        return total + jnp.sum((g * g).reshape(many, 8, LANES), axis=0)

    total = lax.fori_loop(0, steps, square, jnp.zeros((8, LANES), f32))
    last = grads[8 * whole : 8 * whole + 8, :]
    index = lax.broadcasted_iota(jnp.int32, (8, LANES), 0) * LANES + lax.broadcasted_iota(jnp.int32, (8, LANES), 1)
    total += jnp.where(index < size - 1024 * whole, last * last, 0.0)
    norm = jnp.sqrt(jnp.sum(total, axis=(0, 1), keepdims=True))
    norm_ref[...] = norm.reshape(1)
    line, lane0 = divmod(size - 1024 * whole, LANES)
    loss_ref[...] = turn(last[line : line + 1], -lane0).reshape(LANES)[:3]
    scale = jnp.minimum(1.0, clip_limit / (norm + 1e-06))

    def update(where, g):
        clipped = g * scale[0, 0]
        one = beta_one * first[where] + (1.0 - beta_one) * clipped
        two = beta_two * second[where] + (1.0 - beta_two) * clipped * clipped
        first_hat = one / (1.0 - beta_one**step_count)
        second_hat = two / (1.0 - beta_two**step_count)
        w = weights[where]
        news[0][where] = w - learn_rate * (first_hat / (jnp.sqrt(second_hat) + adam_eps) + decay_rate * w)
        news[1][where] = one
        news[2][where] = two

    copies = []

    def send(n, where):
        for m in range(3):
            copy = pltpu.make_async_copy(news[m].at[where], outs[m].at[where], sems.at[n, m])
            copy.start()
            copies.append(copy)

    groups = 4
    for n in range(groups):
        first_step, last_step = steps * n // groups, steps * (n + 1) // groups

        def step(i, _):
            g = grads[pl.ds(pl.multiple_of(i * many * 8, 8), many * 8), :].reshape(many * 1024)
            update(pl.ds(pl.multiple_of(i * many * 1024, 1024), many * 1024), g)

        lax.fori_loop(first_step, last_step, step, None)
        if n < groups - 1:
            send(n, pl.ds(first_step * many * 1024, (last_step - first_step) * many * 1024))
    rest = size - 1024 * whole
    if rest:
        update(pl.ds(1024 * whole, rest), last.reshape(1024)[:rest])
    start = steps * (groups - 1) // groups * many * 1024
    send(groups - 1, pl.ds(start, size - start))
    for copy in copies:
        copy.wait()


def adam(sc, mine, other, params, first, second):
    chunks = (lax.axis_size(HI) * lax.axis_size(SIDE), lax.axis_size(STRIP))
    low_rows = split_rows()[1]
    flat = jax.ShapeDtypeStruct(params.shape, f32)
    return pl.pallas_call(
        functools.partial(adam_kernel, chunks, low_rows),
        out_shape=[flat, flat, flat, jax.ShapeDtypeStruct((3,), f32), jax.ShapeDtypeStruct((1,), f32)],
        in_specs=[SMEM] + [VMEM] * 5,
        out_specs=[ANY] * 3 + [VMEM] * 2,
        scratch_shapes=[pltpu.VMEM((SPLIT + 2 * mine.shape[0] - low_rows, LANES), f32)]
        + [pltpu.VMEM(params.shape, f32)] * 3
        + [pltpu.SemaphoreType.DMA((4, 3))],
        name="adam",
        cost_estimate=pl.CostEstimate(flops=10**7, bytes_accessed=14 * 10**6, transcendentals=10**6),
        compiler_params=pltpu.CompilerParams(vmem_limit_bytes=9 * 2**20),
    )(sc, mine, other, params, first, second)


AXES = (STRIP, HI, SIDE, CORE)
GROUP = (HI, SIDE, CORE)


def body(patch, images, fg_masks, ray_targets, params, moment_one, moment_two):
    strips, hi, half, core = (lax.axis_size(a) for a in AXES)
    cols = half * core
    count, rows_here, cols_here = images.shape
    own = rows_here * hi
    strip = lax.axis_index(STRIP)

    got = lax.all_to_all(tiles_of(images, fg_masks, strips), AXES, 0, 0, tiled=True)
    ready, rays = prep(params, jnp.transpose(ray_targets, (0, 1, 3, 2)))
    rays = lax.all_to_all(rays, GROUP, 0, 0, tiled=True)
    rays = rays.reshape(hi, cols, rows_here, cols_here // 4, 4 * RAYS)

    bounds = [
        jnp.stack([-strip * (own // d), patch // d - strip * (own // d)]).astype(jnp.int32)
        for d in (2, 4, 8)
    ]
    sc = jnp.concatenate([*bounds, jnp.stack([strip, lax.axis_index(CORE)]).astype(jnp.int32)])
    tiling = (hi, strips, cols, rows_here, patch)
    kept, scal = forward(sc, got, ready, own, tiling, count * patch * patch)
    groups = patch // 4
    keep, send, g4, gs1, gs2 = deep(sc, scal, params, kept, rays, own, groups)
    mine, other = sum_all(keep, send, lambda: shallow(sc, params, kept, g4, gs1, gs2, own, groups))
    new_params, new_one, new_two, loss_terms, norm = adam(sc, mine, other, params, moment_one, moment_two)
    return (new_params, new_one, new_two, loss_terms, scal[3, 0], norm[0])


def solution(mesh):
    rows, cols = mesh.shape["rows"], mesh.shape["cols"]
    patches = 8
    hi = patches // cols
    split = Mesh(mesh.devices.reshape(rows // hi, hi, cols // 2, 2), AXES)
    tiled = P(None, (STRIP, HI), (SIDE, CORE))
    in_specs = (tiled, tiled, P(None, (STRIP, HI), (SIDE, CORE), None), P(), P(), P())
    out_specs = (P(),) * 6

    def step(images, *rest):
        if images.shape[0] != patches:
            raise ValueError("eight patches")
        part = functools.partial(body, images.shape[1])
        return jax.shard_map(part, mesh=split, in_specs=in_specs, out_specs=out_specs, check_vma=False)(
            images, *rest
        )

    return step
```

```python
import functools
import math

import jax
import jax.numpy as jnp
from jax import lax
from jax.experimental import pallas as pl
from jax.experimental.pallas import tpu as pltpu
from jax.sharding import Mesh, PartitionSpec as P

C1 = 32
C2 = 64
C3 = 128
FINAL = 128
RAYS = 32

beta_one = 0.9
beta_two = 0.999
learn_rate = 0.05
decay_rate = 0.01
adam_eps = 1e-08
clip_limit = 0.005
step_count = 10.0
ray_scale = 16.0

bf16 = jnp.bfloat16
f32 = jnp.float32

LANES = 128
PAIR, PLAIN, POOL, LAST, JOIN = "pair", "plain", "pool", "last", "join"
STRIP, HI, SIDE, CORE = "strip", "hi", "half", "core"
FORWARD = range(1, 10)
GRANT = 60 * 2**20
BLOCK = 4
HEAD_ROWS = 8
HALO = 24
EDGE = 8
VMEM = pl.BlockSpec(memory_space=pltpu.VMEM)
SMEM = pl.BlockSpec(memory_space=pltpu.SMEM)
ANY = pl.BlockSpec(memory_space=pl.ANY)

SHAPES = {
    1: (C1, C1), 2: (C1, C2), 3: (C2, C2), 4: (C2, C3), 5: (C3, C3),
    6: (C3 + C2, C2), 7: (C2, C2), 8: (C2 + C1, C1), 9: (C1, C1), 10: (C1, FINAL),
}

WIDE1 = [[0, 1, 2, 3], [4, None, None, -1]]
WIDE2 = [[0, 1], [2, -1]]
WIDE3 = [[0], [1], [-1]]
POOL1 = [[0, 2, 1, -1]]
POOL2 = [[0, -1], [1, None]]
UP2 = [[0, 2], [1, 3], [4, -1]]
UP3 = [[0], [1], [2], [-1]]
WIDE10 = [[0], [1], [2], [3], [4], [-1]]

INPUTS = {
    1: [(WIDE1, C1)], 2: [(POOL1, C1)], 3: [(WIDE2, C2)], 4: [(POOL2, C2)], 5: [(WIDE3, C3)],
    6: [(UP3, C3), (WIDE2, C2)], 7: [(WIDE2, C2)], 8: [(UP2, C2), (WIDE1, C1)], 9: [(WIDE1, C1)],
    10: [(WIDE1, C1)],
}
COLS = {1: 4, 2: 2, 3: 2, 4: 1, 5: 1, 6: 2, 7: 2, 8: 4, 9: 4, 10: 4}
GRADS = {1: WIDE1, 2: WIDE2, 3: WIDE2, 4: WIDE3, 5: WIDE3, 6: WIDE2, 7: WIDE2, 8: WIDE1, 9: WIDE1,
         10: WIDE10}
BACKS = {
    1: [[[0, 1, 2, 3]]], 2: [[[0, 0, 1, 1]]], 3: [[[0, 1]]], 4: [[[0, 0]]], 5: [[[0]]],
    6: [[[0], [1]], [[0, 1]]], 7: [[[0, 1]]], 8: [[[0, 2], [1, 3]], [[0, 1, 2, 3]]], 9: [[[0, 1, 2, 3]]],
    10: [[[0, 1, 2, 3]]],
}


def fwd_rows(k):
    return 3 if k == 10 else 4


def fwd_shape(k):
    per_row = sum(len(segs) for segs, _ in INPUTS[k]) * LANES
    outs = COLS[k] * SHAPES[k][1]
    return (fwd_rows(k) * per_row, outs if k == 10 else 2 * outs)


def back_shape(k):
    return (2 * sum(len(s) for s in BACKS[k]) * LANES, 4 * len(GRADS[k]) * LANES)


def lanes_iota():
    return lax.broadcasted_iota(jnp.int32, (1, LANES), 1)


def dense_rows(p_ref, offset, n):
    row, lane0 = divmod(offset, LANES)
    value = p_ref[row : row + n, :]
    if lane0 == 0:
        return value
    both = jnp.where(lanes_iota() >= lane0, value, p_ref[row + 1 : row + 1 + n, :])
    return pltpu.roll(both, LANES - lane0, 1)


def load_flat(flat_ref, p_ref, base=0):
    size = flat_ref.shape[0]
    whole = size // 1024
    many = divisor(whole, 25)
    row = base // LANES

    def step(i, _):
        value = flat_ref[pl.ds(pl.multiple_of(i * many * 1024, 1024), many * 1024)]
        p_ref[pl.ds(pl.multiple_of(row + i * many * 8, 8), many * 8), :] = value.reshape(many * 8, LANES)

    lax.fori_loop(0, whole // many, step, None)
    rest = size - whole * 1024
    if rest:
        row += 8 * whole
        full, part = divmod(rest, LANES)
        if full:
            value = flat_ref[pl.ds(whole * 1024, full * LANES)]
            p_ref[row : row + full, :] = value.reshape(full, LANES)
        if part:
            p_ref[row + full : row + full + 1, 0:part] = flat_ref[pl.ds(size - part, part)].reshape(1, part)


def flat_range(layers, size):
    start = offset_of(min(layers)) // 1024 * 1024
    stop = -(-offset_of(max(layers) + 1) // 1024) * 1024
    return start, min(stop, size) - start


def flat_rows(size):
    return -(-size // 1024) * 8


def turn(value, lanes):
    lanes %= LANES
    return pltpu.roll(value, lanes, 1) if lanes else value


def natural_rows(k, p_ref, nat_ref, natural):
    ci, co = SHAPES[k]
    size = 9 * ci * co
    fill = LANES // co
    dense = dense_rows(p_ref, offset_of(k), size // LANES)
    if fill == 1:
        natural[0 : 9 * ci, :] = dense.astype(bf16)
        return
    for m in range(fill):
        nat_ref[pl.ds(m, size // LANES, stride=fill), :] = turn(dense, -co * m)
    natural[0 : 9 * ci, :] = nat_ref[0 : 9 * ci, :].astype(bf16)


def input_starts(k):
    starts = [0]
    for _, ch in INPUTS[k]:
        starts.append(starts[-1] + ch)
    return starts


def band(k, natural, places, first, ch):
    ci, co = SHAPES[k]
    zero = jnp.zeros((ch, co), bf16)
    parts = []
    for a, c in places:
        if c is not None and 0 <= a <= 2 and 0 <= c <= 2:
            row = (a * 3 + c) * ci + first
            parts.append(natural[row : row + ch, 0:co])
        else:
            parts.append(zero)
    return jnp.concatenate(parts, axis=1)


def forward_weights(k, p_ref, natural, fwd_ref, tiled_ref):
    ci, co = SHAPES[k]
    n = COLS[k]
    pair = (0,) if k == 10 else (0, 1)
    row = 0
    for j in range(fwd_rows(k)):
        for (segs, ch), first in zip(INPUTS[k], input_starts(k)):
            for seg in segs:
                for h in seg:
                    places = [(j - q, None if h is None else h - p + 1) for q in pair for p in range(n)]
                    fwd_ref[row : row + ch, :] = band(k, natural, places, first, ch) * 0.5
                    row += ch
    bias = dense_rows(p_ref, offset_of(k) + 9 * ci * co, 1)[:, :co] * 0.5
    tiled_ref[...] = jnp.concatenate([bias] * (n * len(pair)), axis=1)


def backward_weights(k, natural, back_ref):
    half = back_shape(k)[0] // 2
    per = len(GRADS[k]) * LANES
    row = 0
    for (_, ch), backs, first in zip(INPUTS[k], BACKS[k], input_starts(k)):
        for seg in backs:
            for p in seg:
                places = [(2 - j, None if h is None else p - h + 1) for j in range(3) for s in GRADS[k] for h in s]
                value = band(k, natural, places, first, ch)
                zero = jnp.zeros((ch, per), bf16)
                back_ref[row : row + ch, 0 : 3 * per] = value
                back_ref[row : row + ch, 3 * per : 4 * per] = zero
                back_ref[half + row : half + row + ch, 0:per] = zero
                back_ref[half + row : half + row + ch, per : 4 * per] = value
                row += ch


def prep_first(p_ref, w_ref, tiled_ref, wide_ref):
    taps = [turn(p_ref[i * C1 // LANES : i * C1 // LANES + 1, :], -i * C1)[:, :C1] for i in range(10)]
    zero = jnp.zeros((1, C1), f32)
    wide_ref[...] = jnp.zeros(wide_ref.shape, f32)
    for m in range(6):
        for j in range(4):
            parts = []
            for q in range(2):
                for p in range(4):
                    a, c = j - q, m - p
                    parts.append(taps[a * 3 + c] if 0 <= a <= 2 and 0 <= c <= 2 else zero)
            wide_ref[4 * m + j : 4 * m + j + 1, :] = jnp.concatenate(parts, axis=1)
    w_ref[...] = wide_ref[...].astype(bf16) * 0.5
    tiled_ref[...] = jnp.concatenate([taps[9]] * 8, axis=1) * 0.5


def prep_head(p_ref, hw_ref, hwt_ref, hb_ref, nat_ref):
    wide = 1 + RAYS
    at = offset_of(11)
    for e in range(FINAL):
        nat_ref[e : e + 1, :] = dense_rows(p_ref, at + wide * e, 1)
    w = nat_ref[0:FINAL, :]
    b = dense_rows(p_ref, at + wide * FINAL, 1)
    lane = lanes_iota()
    left = right = 0.0
    for q in range(4):
        chunk = (lane >= RAYS * q) & (lane < RAYS * (q + 1))
        rows = slice(FINAL * q, FINAL * (q + 1))
        hw_ref[rows, 0:LANES] = jnp.where(chunk, turn(w, RAYS * q - 1), 0.0).astype(bf16)
        hw_ref[rows, LANES : 2 * LANES] = jnp.where(lane == RAYS * q, turn(w, RAYS * q), 0.0).astype(bf16)
        left += jnp.where(chunk, turn(b, RAYS * q - 1), 0.0)
        right += jnp.where(lane == RAYS * q, turn(b, RAYS * q), 0.0)
    hwt_ref[...] = hw_ref[...].T
    hb_ref[:, 0:LANES] = left
    hb_ref[:, LANES : 2 * LANES] = right


def prep_kernel(flat_ref, rays_hbm, *refs):
    count = 2 * len(FORWARD) + 3
    outs, scratch = refs[:count], refs[count : 2 * count]
    p_ref, nat, natural, wide, rays_ref, sems, ray_sems = refs[2 * count :]
    patches = rays_hbm.shape[0]
    loads = [pltpu.make_async_copy(rays_hbm.at[p], rays_ref.at[p], ray_sems.at[p]) for p in range(patches)]
    for copy in loads:
        copy.start()
    copies = []

    def send(*places):
        for m in places:
            copy = pltpu.make_async_copy(scratch[m], outs[m], sems.at[m])
            copy.start()
            copies.append(copy)

    last = 2 * len(FORWARD)
    load_flat(flat_ref, p_ref)
    prep_first(p_ref, scratch[last], scratch[last + 1], wide)
    send(last, last + 1)
    for i, k in enumerate(FORWARD):
        natural_rows(k, p_ref, nat, natural)
        forward_weights(k, p_ref, natural, scratch[2 * i], scratch[2 * i + 1])
        send(2 * i, 2 * i + 1)
    for p in range(patches):
        loads[p].wait()
        group_rays(rays_ref, scratch[last + 2], p)
    send(last + 2)
    for copy in copies:
        copy.wait()


def group_rays(rays_ref, out_ref, p):
    rows, rays, cols = rays_ref.shape[1:]
    per = LANES // rays
    quarter = cols // 4
    lane = lanes_iota()
    to = lax.broadcasted_iota(jnp.int32, (cols, cols), 0)
    of = lax.broadcasted_iota(jnp.int32, (cols, cols), 1)
    pick = jnp.where(of == (to % quarter) * 4 + to // quarter, 1.0, 0.0).astype(bf16)
    for r in range(rows // per):
        x = rays_ref[p, per * r : per * (r + 1)].reshape(LANES, cols).astype(f32).astype(bf16)
        turned = lax.dot_general(pick, x, (((1,), (1,)), ((), ())), preferred_element_type=f32)
        parts = [turned[quarter * q : quarter * (q + 1)] for q in range(4)]
        for e in range(per):
            total = turn(parts[0], -rays * e)
            for q in range(1, 4):
                total = jnp.where(lane >= rays * q, turn(parts[q], rays * (q - e)), total)
            out_ref[p, per * r + e] = total.astype(bf16)


def prep(flat, rays):
    count, rows, width, cols = rays.shape
    shapes = []
    for k in FORWARD:
        fs = fwd_shape(k)
        shapes += [jax.ShapeDtypeStruct(fs, bf16), jax.ShapeDtypeStruct((1, fs[1]), f32)]
    shapes += [
        jax.ShapeDtypeStruct((LANES, 2 * LANES), bf16),
        jax.ShapeDtypeStruct((1, 2 * LANES), f32),
        jax.ShapeDtypeStruct((count, rows, cols // 4, 4 * width), bf16),
    ]
    outs = pl.pallas_call(
        prep_kernel,
        out_shape=shapes,
        in_specs=[VMEM, ANY],
        out_specs=[ANY] * len(shapes),
        scratch_shapes=[pltpu.VMEM(v.shape, v.dtype) for v in shapes]
        + [
            pltpu.VMEM((flat_rows(flat.shape[0]), LANES), f32),
            pltpu.VMEM((9 * (C3 + C2), LANES), f32),
            pltpu.VMEM((9 * (C3 + C2), LANES), bf16),
            pltpu.VMEM((LANES, 2 * LANES), f32),
            pltpu.VMEM(rays.shape, jnp.int32),
            pltpu.SemaphoreType.DMA((len(shapes),)),
            pltpu.SemaphoreType.DMA((count,)),
        ],
        name="prep",
        cost_estimate=pl.CostEstimate(flops=10**9, bytes_accessed=2 * 10**7, transcendentals=0),
        compiler_params=pltpu.CompilerParams(vmem_limit_bytes=GRANT),
    )(flat, rays)
    ready = {k: tuple(outs[2 * i : 2 * i + 2]) for i, k in enumerate(FORWARD)}
    ready[0] = tuple(outs[-3:-1])
    return ready, outs[-1]


def tiles_kernel(strips, images_ref, masks_ref, out_ref):
    patches, rows, cols = images_ref.shape
    fold_ = LANES // cols
    high = rows // fold_
    below = out_ref.shape[1] - high
    total = jnp.sum(masks_ref[...].astype(f32).reshape(patches * rows, cols))
    top = jnp.floor(total * (1.0 / 16384.0))
    middle = jnp.floor((total - 16384.0 * top) * (1.0 / 128.0))
    low = total - 16384.0 * top - 128.0 * middle
    lane = lax.broadcasted_iota(jnp.int32, (below, LANES), 1)
    row = lax.broadcasted_iota(jnp.int32, (below, LANES), 0)
    digits = jnp.where(lane == 0, low, jnp.where(lane == 1, middle, jnp.where(lane == 2, top, 0.0)))
    digits = jnp.where(row == 0, digits, 0.0)
    for p in range(patches):
        x = images_ref[p]
        x = jnp.concatenate([x[high * m : high * (m + 1)] for m in range(fold_)], axis=1)
        value = jnp.concatenate([x, digits], axis=0).astype(bf16)
        for s in range(strips):
            out_ref[patches * s + p] = value


def tiles_of(images, masks, strips):
    patches, rows, cols = images.shape
    height = -(-(rows * cols // LANES + 1) // 16) * 16
    return pl.pallas_call(
        functools.partial(tiles_kernel, strips),
        out_shape=jax.ShapeDtypeStruct((strips * patches, height, LANES), bf16),
        in_specs=[VMEM] * 2,
        out_specs=VMEM,
        name="tiles",
    )(images, masks)


def layer_shapes():
    return [(3, 3, 1, C1)] + [(3, 3, *SHAPES[k]) for k in range(1, 11)] + [(FINAL, 1 + RAYS)]


def offset_of(k):
    return sum(math.prod(v) + v[-1] for v in layer_shapes()[:k])


def divisor(count, limit):
    return max(d for d in range(1, min(count, limit) + 1) if count % d == 0)


def mm(a, b):
    return lax.dot_general(a, b, (((1,), (0,)), ((), ())), preferred_element_type=f32)


def mm_t(a, b):
    return lax.dot_general(a, b, (((0,), (0,)), ((), ())), preferred_element_type=f32)


def mm_n(a, b):
    return lax.dot_general(a, b, (((1,), (1,)), ((), ())), preferred_element_type=f32)


def shifted(v):
    zero = jnp.zeros((v.shape[0], 1, v.shape[2]), v.dtype)
    left = jnp.concatenate([zero, v[:, :-1]], axis=1)
    right = jnp.concatenate([v[:, 1:], zero], axis=1)
    return left, right


def lane_of(width=LANES):
    return lax.broadcasted_iota(jnp.int32, (1, 1, width), 2)


def flat2(v):
    return v.reshape(v.shape[0] * v.shape[1], v.shape[2])


def segments(v, three):
    left, right = shifted(v)
    if three:
        return [v, right, left]
    return [v, jnp.where(lane_of() < 64, right, left)]


def rows_of(view):
    return view.reshape(view.shape[0] * 2, *view.shape[2:])


def fours_of(view):
    return view.reshape(view.shape[0] // 2, 2, *view.shape[1:])


def store(view, index, v, three):
    for s, part in enumerate(segments(v, three)):
        view[(*index, s)] = part.astype(bf16)


def lhs_parts(kind, view, base, T, j, repeat):
    segs = range(view.shape[-3])
    if kind == "up":
        at = base + (-1, 0, 0, 1)[j]
        parts = [flat2(view[pl.ds(at, T), s]) for s in segs]
        return parts[:1] + parts if repeat else parts
    p, q = divmod(j + 1, 2)
    return [flat2(view[pl.ds(base + p - 1, T), q, s]) for s in segs]


def lhs_of(sources, r, T, repeat):
    parts = []
    for j in range(4):
        for kind, view, off in sources:
            parts += lhs_parts(kind, view, r + off, T, j, repeat)
    return jnp.concatenate(parts, axis=1)


def each_block(first, last, T, block):
    T = min(T, last - first)
    for i in range(-(-(last - first) // T)):
        block(min(first + i * T, last - T), T)


def clear(view, start, stop):
    def step(i, _):
        view[i] = jnp.zeros(view.shape[1:], view.dtype)

    lax.fori_loop(start, stop, step, None)


def clear_outside(view, count, pad, lo, hi):
    for i in (*range(pad), *range(pad + count, 2 * pad + count)):
        view[i] = jnp.zeros(view.shape[1:], view.dtype)

    @pl.when(lo > 0)
    def _():
        clear(view, pad, pad + jnp.minimum(lo, count))

    @pl.when(hi < count)
    def _():
        clear(view, pad + jnp.maximum(hi, 0), pad + count)


def silu(u):
    t = jnp.tanh(u)
    a = u * t + u
    return a, (t - a * t) + a


SLOPE_STEP = 1.0 / 26000.0
SLOPE_LOW = 0.125


def pack_slope(v):
    return (v * 13000.0 + (13000.5 + 26000.0 * SLOPE_LOW)).astype(jnp.int32).astype(jnp.int16)


def unpack_slope(v):
    return v.astype(jnp.int32).astype(f32) * SLOPE_STEP - SLOPE_LOW


def split_pair(v, T):
    g = v.shape[0] // T
    half = v.shape[1] // 2
    return [v[:, half * q : half * (q + 1)].reshape(T, g, half) for q in range(2)]


def pooled(x, level):
    lane = lane_of()
    if level == 1:
        near = x + pltpu.roll(x, LANES - C1, 2)
        far = x + pltpu.roll(x, C1, 2)
        left, right = shifted(far)
        return [jnp.where((lane & 32) == 0, near, jnp.where(lane < 64, right, left))]
    y = x + pltpu.roll(x, C2, 2)
    left, right = shifted(y)
    return [jnp.where(lane < 64, y, left), right]


def conv(sources, w, bias, out, slopes, count, lo, valid, three=False, pool=None, limit=BLOCK):
    def block(r, T):
        a, slope = silu(mm(lhs_of(sources, r, T, True), w[...]) + bias[...])
        rows, slope = split_pair(a, T), split_pair(slope, T)
        for q in range(2):
            slopes[pl.ds(r, T), q] = pack_slope(slope[q])
            store(out, (pl.ds(r + 1, T), q), rows[q], three)
        if pool:
            x = sum(v.astype(bf16).astype(f32) for v in rows) * 0.25
            for s, part in enumerate(pooled(x, pool[1])):
                pool[0][pl.ds(r + 2, T), s] = part.astype(bf16)

    each_block(0, count, limit, block)
    clear_outside(out, count, 1, valid[0] - lo, valid[1] - lo)
    if pool:
        clear_outside(pool[0], count, 2, valid[0] - lo, valid[1] - lo)


def first_conv(tiling, own, strip, valid, got, w_ref, bias_ref, out, slopes, xcols, x_ref, xt_ref, v_ref):
    hi, strips, across, per, width = tiling
    count = own // 2 + 22
    rows = own + 2 * HALO
    reach = -(-HALO // per)
    wide = width // across
    high = per * wide // LANES
    x_ref[...] = jnp.zeros(x_ref.shape, f32)
    for d in range(-reach, hi + reach):
        tile = strip * hi + d
        start = HALO + d * per
        first, last = max(0, -start), min(per, rows - start)

        @pl.when((tile >= 0) & (tile < strips * hi))
        def _():
            parts = [got[tile * across + c].astype(f32)[:high] for c in range(across)]
            here = [[v[:, wide * m : wide * (m + 1)] for v in parts] for m in range(LANES // wide)]
            value = jnp.concatenate([jnp.concatenate(v, axis=1) for v in here], axis=0)
            x_ref[start + first : start + last, :] = value[first:last]

    groups = width // 4
    xt_ref[0:EDGE] = jnp.zeros((EDGE, LANES), f32)
    xt_ref[EDGE + width : 2 * EDGE + width] = jnp.zeros((EDGE, LANES), f32)
    xt_ref[EDGE : EDGE + width] = x_ref[...].T
    for m in range(6):
        v_ref[m] = xt_ref[pl.ds(EDGE + m - 1, groups, stride=4), :]
    lane = lax.broadcasted_iota(jnp.int32, (1, LANES), 1)
    for at in range(count):
        total = jnp.zeros((groups, LANES), f32)
        for m in range(6):
            turned = turn(v_ref[m], 4 * m - (2 * at + 1))
            total = jnp.where((lane >= 4 * m) & (lane < 4 * m + 4), turned, total)
        xcols[at] = total.astype(bf16)
    def block(r, T):
        a, slope = silu(mm(flat2(xcols[pl.ds(r, T)]), w_ref[...]) + bias_ref[...])
        rows_, slope = split_pair(a, T), split_pair(slope, T)
        for q in range(2):
            slopes[pl.ds(r, T), q] = pack_slope(slope[q])
            store(out, (pl.ds(r + 1, T), q), rows_[q], False)

    each_block(0, count, BLOCK, block)
    clear_outside(out, count, 1, valid[0] + 11, valid[1] + 11)


def act_shapes(own, groups):
    h, h2, h3 = own // 2, own // 4, own // 8
    pairs = dict(
        a0=(h + 24, 2), s1=(h + 22, 2), p1=(h2 + 12, 1), a2=(h2 + 12, 2), s2=(h2 + 10, 2), p2=(h3 + 6, 2),
        a4=(h3 + 6, 3), t3=(h3 + 4, 3), a6=(h2 + 6, 2), t2=(h2 + 4, 2), a8=(h + 4, 2), a9=(h + 4, 2),
    )
    shapes = {k: (n, 2, segs, groups, LANES) for k, (n, segs) in pairs.items()}
    shapes["xc"] = (h + 22, groups, LANES)
    return shapes


def slope_shapes(own, groups):
    h, h2, h3 = own // 2, own // 4, own // 8
    counts = [h + 22, h + 20, h2 + 10, h2 + 8, h3 + 4, h3 + 2, h2 + 4, h2 + 2, h + 2, h + 2]
    return {f"sl{k}": (n, 2, groups, LANES) for k, n in enumerate(counts)}


def grad_shapes(own, groups):
    h, h2, h3 = own // 2, own // 4, own // 8
    pairs = {
        10: (h + 4, 6), 9: (h + 6, 2), 8: (h + 6, 2), 7: (h2 + 6, 2), 6: (h2 + 8, 2), 5: (h3 + 6, 3),
        4: (h3 + 8, 3), 3: (h2 + 12, 2), 2: (h2 + 14, 2), 1: (h + 24, 2), 0: (h + 22, 1),
    }
    return {f"g{k}": (n, 2, segs, groups, LANES) for k, (n, segs) in pairs.items()}


def loss_scales(got, tiling, pixels, scal_ref):
    _, _, across, per, width = tiling
    high = per * (width // across) // LANES
    digits = jnp.sum(got[...].astype(f32), axis=0)[high : high + 1, :]
    lane = lanes_iota()
    digits = jnp.where(lane == 0, digits, jnp.where(lane == 1, 128.0 * digits, 16384.0 * digits))
    fg = jnp.sum(jnp.where(lane < 3, digits, 0.0), axis=1, keepdims=True) * jnp.ones((1, LANES), f32)
    scal_ref[0:1] = 0.5 / fg
    scal_ref[1:2] = 0.5 / (pixels - fg)
    scal_ref[2:3] = 1.0 / (fg * RAYS)
    scal_ref[3:4] = fg


def forward_kernel(cfg, sc, got, w0, b0, *refs):
    own, tiling = cfg["own"], cfg["tiling"]
    h, h2, h3 = own // 2, own // 4, own // 8
    refs = list(refs)
    take = lambda m: [refs.pop(0) for _ in range(m)]
    w_hbm, bias = take(9), take(9)
    names = list(cfg["outs"])
    outs = dict(zip(names, take(len(names))))
    scal_ref = take(1)[0]
    here = dict(zip(names, take(len(names))))
    w_vmem = take(9)
    x_ref, xt_ref, v_ref, w_sem, out_sem = refs
    fetch = {}
    for i, k in enumerate(FORWARD):
        fetch[k] = pltpu.make_async_copy(w_hbm[i], w_vmem[i], w_sem.at[i])
        fetch[k].start()
    sent = []

    def send(*keys):
        for key in keys:
            copy = pltpu.make_async_copy(here[key], outs[key], out_sem.at[names.index(key)])
            copy.start()
            sent.append(copy)

    v1, v2, v3 = [(sc[2 * i], sc[2 * i + 1]) for i in range(3)]
    loss_scales(got, tiling, cfg["pixels"], scal_ref)
    first_conv(tiling, own, sc[6], v1, got, w0, b0, here["a0"], here["sl0"], here["xc"],
               x_ref, xt_ref, v_ref)
    send("a0", "sl0", "xc")

    def layer(k, out, sources, count, lo, valid, three=False, pool=None):
        fetch[k].wait()
        conv(sources, w_vmem[k - 1], bias[k - 1], here[out], here[f"sl{k}"], count, lo, valid, three, pool)
        send(out, f"sl{k}")

    layer(1, "s1", [(PAIR, here["a0"], 2)], h + 20, -10, v1, pool=(rows_of(here["p1"]), 1))
    send("p1")
    layer(2, "a2", [(PAIR, here["p1"], 1)], h2 + 10, -5, v2)
    layer(3, "s2", [(PAIR, here["a2"], 2)], h2 + 8, -4, v2, pool=(rows_of(here["p2"]), 2))
    send("p2")
    layer(4, "a4", [(PAIR, here["p2"], 1)], h3 + 4, -2, v3, True)
    layer(5, "t3", [(PAIR, here["a4"], 2)], h3 + 2, -1, v3, True)
    layer(6, "a6", [("up", rows_of(here["t3"]), 2), (PAIR, here["s2"], 3)], h2 + 4, -2, v2)
    layer(7, "t2", [(PAIR, here["a6"], 2)], h2 + 2, -1, v2)
    layer(8, "a8", [("up", rows_of(here["t2"]), 3), (PAIR, here["s1"], 10)], h + 2, -1, v1)
    layer(9, "a9", [(PAIR, here["a8"], 1)], h + 2, -1, v1)
    for copy in sent:
        copy.wait()


def forward(sc, got, ready, own, tiling, pixels):
    groups = tiling[-1] // 4
    shapes = {k: jax.ShapeDtypeStruct(v, bf16) for k, v in act_shapes(own, groups).items()}
    shapes |= {k: jax.ShapeDtypeStruct(v, jnp.int16) for k, v in slope_shapes(own, groups).items()}
    weights = [ready[k][0] for k in FORWARD]
    biases = [ready[k][1] for k in FORWARD]
    width = tiling[-1]
    outs = pl.pallas_call(
        functools.partial(forward_kernel, dict(own=own, tiling=tiling, outs=tuple(shapes), pixels=float(pixels))),
        out_shape=[*shapes.values(), jax.ShapeDtypeStruct((8, LANES), f32)],
        in_specs=[SMEM] + [VMEM] * 3 + [ANY] * 9 + [VMEM] * 9,
        out_specs=[ANY] * len(shapes) + [VMEM],
        scratch_shapes=[pltpu.VMEM(v.shape, v.dtype) for v in shapes.values()]
        + [pltpu.VMEM(w.shape, bf16) for w in weights]
        + [
            pltpu.VMEM((LANES, width), f32),
            pltpu.VMEM((width + 2 * EDGE, LANES), f32),
            pltpu.VMEM((6, groups, LANES), f32),
            pltpu.SemaphoreType.DMA((9,)),
            pltpu.SemaphoreType.DMA((len(shapes),)),
        ],
        name="forward",
        cost_estimate=pl.CostEstimate(flops=2 * 10**10, bytes_accessed=5 * 10**7, transcendentals=10**7),
        compiler_params=pltpu.CompilerParams(vmem_limit_bytes=GRANT),
    )(sc, got, *ready[0], *weights, *biases)
    return dict(zip(shapes, outs)), outs[-1]


def sum_back(k, acc):
    ci, co = SHAPES[k]
    n = COLS[k]
    pieces = {}
    for a in range(3):
        value = acc(a)
        base = start = 0
        for segs, ch in INPUTS[k]:
            if segs is UP2:
                unique = [[(0, 1), (2, 3)], [(4,), (-1,)]]
            elif segs is UP3:
                unique = [[(0, 1)], [(2,)], [(-1,)]]
            else:
                unique = [[() if c is None else (c,) for c in seg] for seg in segs]
            uses = {}
            for seg in unique:
                for columns in seg:
                    for col in columns:
                        for p in range(n):
                            c = col - p + 1
                            if 0 <= c <= 2:
                                uses.setdefault(c, []).append((base, p))
                    base += ch
            for c, places in uses.items():
                total = None
                for row, p in places:
                    piece = value[row : row + ch, p * co : (p + 1) * co]
                    total = piece if total is None else total + piece
                pieces[(a * 3 + c) * ci + start] = total
            start += ch
    return pieces


def place(out, value, offset):
    out, base = out
    row, lane0 = divmod(offset - base * LANES, LANES)
    n = value.shape[0]
    if lane0 == 0:
        out[row : row + n, :] += value
        return
    lane = lax.broadcasted_iota(jnp.int32, (1, LANES), 1)
    turned = pltpu.roll(value, lane0, 1)
    out[row : row + n, :] += jnp.where(lane >= lane0, turned, 0.0)
    out[row + 1 : row + 1 + n, :] += jnp.where(lane < lane0, turned, 0.0)


def fold(row, co):
    total = row[:, 0:LANES]
    for m in range(1, row.shape[1] // LANES):
        total = total + row[:, LANES * m : LANES * (m + 1)]
    width = LANES
    while width > co:
        width //= 2
        total = total + pltpu.roll(total, width, 1)
    lane = lax.broadcasted_iota(jnp.int32, (1, LANES), 1)
    return jnp.where(lane < co, total, 0.0)


def place_layer(k, pieces, db, nat, out):
    ci, co = SHAPES[k]
    n = 9 * ci * co // LANES
    fill = LANES // co
    for row, total in pieces.items():
        nat[row : row + total.shape[0], 0:co] = total
    if fill == 1:
        value = nat[0:n, :]
    else:
        value = jnp.concatenate([nat[pl.ds(m, n, stride=fill), :][:, :co] for m in range(fill)], axis=1)
    place(out, value, offset_of(k))
    place(out, fold(db, co), offset_of(k) + 9 * ci * co)


def head_part(own, scal, x, w, bias, hw, hwt, hb, rays, grad, acc, dhead, nat, out):
    _, cols, per = rays.shape[:3]
    x, grad = rows_of(x), rows_of(grad)
    groups = x.shape[2]
    T = divisor(math.gcd(own, per), HEAD_ROWS)
    M = T * groups
    fg_scale, bg_scale, ray_scale_ = scal[0:1], scal[1:2], scal[2:3]
    lane = lax.broadcasted_iota(jnp.int32, (1, LANES), 1)
    is_logit = (lane & 31) == 0
    ones = jnp.ones((8, M), bf16)
    dhead[...] = jnp.zeros(dhead.shape, f32)

    def block(i, carry):
        dbh, fg_loss, bg_loss, ray_loss = carry
        r = i * T
        slabs = [
            jnp.concatenate([flat2(x[pl.ds(r + 4 + d, T), s]) for s in range(2)], axis=1) for d in (-1, 0, 1)
        ]
        a, slope = silu(mm(jnp.concatenate(slabs, axis=1), w[...]) + bias[...])
        slope = 0.5 + 0.5 * slope
        feat = a.astype(bf16)
        head = mm(feat, hw[...]) + hb[...]
        dist, logit = head[:, :LANES], head[:, LANES:]
        part, first = r // per, r % per
        ray = jnp.concatenate([rays[part, c, pl.ds(first, T)] for c in range(cols)], axis=1)
        ray = flat2(ray.astype(f32))
        y = jnp.where(ray > 0.0, 1.0, 0.0)
        diff = dist - ray * (1.0 / ray_scale)
        smooth = jnp.sqrt(diff * diff + 1.0)
        g_dist = diff / smooth * (y * ray_scale_)
        cross = jnp.maximum(logit, 0.0) - logit * y + jnp.log(1.0 + jnp.exp(-jnp.abs(logit)))
        cross = jnp.where(is_logit, cross, 0.0)
        sig = 1.0 / (1.0 + jnp.exp(-logit))
        g_logit = jnp.where(is_logit, (sig - y) * (y * fg_scale + (1.0 - y) * bg_scale), 0.0)
        fg_loss += jnp.sum((cross * y).reshape(M // 8, 8, LANES), axis=0)
        bg_loss += jnp.sum((cross * (1.0 - y)).reshape(M // 8, 8, LANES), axis=0)
        ray_loss += jnp.sum((smooth * y).reshape(M // 8, 8, LANES), axis=0)
        g_head = jnp.concatenate([g_dist, g_logit], axis=1).astype(bf16)
        dhead[...] += mm_t(feat, g_head)
        gz = mm(g_head, hwt[...]) * slope
        center = gz.astype(bf16)
        for s in range(4):
            grad[pl.ds(r + 4, T), s] = center[:, LANES * s : LANES * (s + 1)].reshape(T, groups, LANES)
        left = shifted(gz[:, 3 * LANES :].reshape(T, groups, LANES))[0]
        right = shifted(gz[:, :LANES].reshape(T, groups, LANES))[1]
        grad[pl.ds(r + 4, T), 4] = right.astype(bf16)
        grad[pl.ds(r + 4, T), 5] = left.astype(bf16)
        return dbh + mm(ones, g_head), fg_loss, bg_loss, ray_loss

    zero = jnp.zeros((8, LANES), f32)
    start = (jnp.zeros((8, 2 * LANES), f32), zero, zero, zero)
    carry = start
    for i in range(own // T):
        carry = block(i, carry)
    dbh, *losses = carry
    clear(grad, 0, 4)
    clear(grad, own + 4, own + 8)
    g = jnp.concatenate([flat2(grad[pl.ds(4, own), s]) for s in range(4)], axis=1)
    for a in range(3):
        acc[a] = mm_t(jnp.concatenate([flat2(x[pl.ds(3 + a, own), s]) for s in range(2)], axis=1), g)
    db = mm(jnp.ones((8, own * groups), bf16), g)
    place_layer(10, sum_back(10, lambda a: acc[a]), db[0:1], nat, out)
    both = jnp.zeros((FINAL, LANES), f32)
    for q in range(4):
        rows = dhead[FINAL * q : FINAL * (q + 1), :]
        piece, first = rows[:, :LANES], rows[:, LANES:]
        if q:
            piece = pltpu.roll(piece, LANES - RAYS * q, 1)
            first = pltpu.roll(first, LANES - RAYS * q, 1)
        both += jnp.where(lane == 0, first, pltpu.roll(piece, 1, 1))
    wide = 1 + RAYS
    nat[0:FINAL, :] = jnp.where(lane < wide, both, 0.0)
    at = offset_of(11)
    flat, base = out
    for e in range(FINAL):
        row, lane0 = divmod(at - base * LANES + wide * e, LANES)
        value = pltpu.roll(nat[e : e + 1, :], lane0, 1) if lane0 else nat[e : e + 1, :]
        if lane0 + wide <= LANES:
            flat[row : row + 1, :] += value
        else:
            flat[row : row + 1, :] += jnp.where(lane >= lane0, value, 0.0)
            flat[row + 1 : row + 2, :] += jnp.where(lane < lane0, value, 0.0)
    dist_sum, logit_sum = fold(dbh[0:1, :LANES], RAYS), fold(dbh[0:1, LANES:], RAYS)
    value = jnp.where(lane == 0, logit_sum, pltpu.roll(dist_sum, 1, 1))
    place(out, jnp.where(lane < wide, value, 0.0), at + FINAL * wide)
    terms = jnp.zeros((1, LANES), f32)
    for m, part in enumerate(losses):
        terms = jnp.where(lane == m, jnp.sum(part), terms)
    place(out, terms, offset_of(12))


def weight_grad(k, sources, grad, count, acc, nat, out):
    rows = sum(v.shape[-3] for _, v, _ in sources) * LANES
    groups = grad.shape[3]
    g = jnp.concatenate([flat2(grad[pl.ds(2, count), q, 0]) for q in range(2)], axis=1)
    for j in range(4):
        parts = []
        for kind, view, off in sources:
            parts += lhs_parts(kind, view, off, count, j, False)
        acc[j, 0:rows] = mm_t(jnp.concatenate(parts, axis=1), g)
    db = mm(jnp.ones((8, count * groups), bf16), g)
    pieces = sum_back(k, lambda a: acc[a, 0:rows, 0:LANES] + acc[a + 1, 0:rows, LANES : 2 * LANES])
    place_layer(k, pieces, db[0:1], nat, out)


def input_grad(mode, grad, goff, w, slopes, out, count, valid, lo, three=False, extra=None, side=None, limit=BLOCK):
    def block(r, T):
        groups = grad.shape[3]
        acc = mm_n(lhs_of([(PAIR, grad, goff)], r, T, False), w[...])
        if mode == JOIN:
            parts = [acc[:, LANES * m : LANES * (m + 1)].reshape(T, groups, LANES) for m in range(6)]
            gz = ((parts[0] + parts[1]) + (parts[3] + parts[4])) * unpack_slope(slopes[pl.ds(r, T)])
            store(out, (pl.ds(r + 4, T),), gz, three)
            for q in range(2):
                side[pl.ds(r, T), q] = parts[2 + 3 * q]
            return
        vals = split_pair(acc, T)
        for q in range(2):
            if mode == POOL:
                for e in range(2):
                    total = vals[q] * 0.25
                    if start <= r < stop:
                        total += extra[pl.ds(r - start, T), q, e]
                    store(out, (pl.ds(r + 1, T), q, e), total * unpack_slope(slopes[pl.ds(r, T), q, e]), three)
                continue
            gz = vals[q] * unpack_slope(slopes[pl.ds(r, T), q])
            if mode == LAST:
                out[pl.ds(r, T), q, 0] = gz.astype(bf16)
            else:
                store(out, (pl.ds(r + 2, T), q), gz, three)

    start = stop = 0
    if mode == POOL:
        start = (count - extra.shape[0]) // 2
        stop = start + extra.shape[0]
    for first, last in ((0, start), (start, stop), (stop, count)):
        if first < last:
            each_block(first, last, limit, block)
    low, high = valid[0] - lo, valid[1] - lo
    if mode == PLAIN:
        clear_outside(out, count, 2, low, high)
    elif mode == LAST:
        clear_outside(out, count, 0, low, high)
    elif mode == JOIN:
        clear_outside(out, count, 4, low, high)
    else:
        clear_outside(out, count, 1, low // 2, high // 2)


def first_grad(grad, xcols, count, out, tmp):
    groups = grad.shape[3]

    def block(r, T, carry):
        g = jnp.concatenate([flat2(grad[pl.ds(r, T), q, 0]) for q in range(2)], axis=1)
        return carry[0] + mm_t(flat2(xcols[pl.ds(r, T)]), g), carry[1] + mm(jnp.ones((8, T * groups), bf16), g)

    T = divisor(count, 18)
    start = (jnp.zeros((LANES, 2 * LANES), f32), jnp.zeros((8, 2 * LANES), f32))
    dw, db = lax.fori_loop(0, count // T, lambda i, c: block(i * T, T, c), start)
    tmp[...] = jnp.zeros(tmp.shape, f32)
    for a in range(3):
        for c in range(3):
            total = None
            for q in range(2):
                for p in range(4):
                    m, j = p + c, a + q
                    at = (q * 4 + p) * C1
                    piece = dw[4 * m + j : 4 * m + j + 1, at : at + C1]
                    total = piece if total is None else total + piece
            row, at = divmod((a * 3 + c) * C1, LANES)
            tmp[row : row + 1, at : at + C1] = total
    place(out, tmp[...], 0)
    place(out, fold(db[0:1], C1), 9 * C1)


def arena_plan(own, groups, places):
    sizes = act_shapes(own, groups) | grad_shapes(own, groups)
    tiles = {k: math.prod(v[:-2]) for k, v in sizes.items()}
    at, top = {}, 0
    for lists in places:
        ends = []
        for names in lists:
            spot = top
            for name in names:
                at[name] = spot
                spot += tiles[name]
            ends.append(spot)
        top = max(ends)
    return sizes, tiles, at, top


SLOTS = {k: "x" if k in (8, 6) else "y" for k in SHAPES}
DEEP = dict(
    acts=("a9", "a8", "t2", "s1", "a6", "t3", "s2", "a4", "p2"),
    slopes=("sl9", "sl8", "sl7", "sl6", "sl5", "sl4"),
    layers=(10, 9, 8, 7, 6, 5),
    places=([["g10"]], [["g9"], ["g7"], ["g5"]], [["g8"], ["g6"], ["g4"]], [["a9", "a8"]], [["t2", "s1"]],
            [["a6", "t3", "s2", "a4", "p2"]]),
)
SHALLOW = dict(
    acts=("a2", "p1", "a0", "xc"),
    slopes=("sl3", "sl2", "sl1", "sl0"),
    layers=(4, 3, 2, 1),
    places=([["g4"]], [["g3"]], [["g2"]], [["g1"]], [["g0"]], [["a2", "p1", "a0", "xc"]]),
)
SPLIT = 504
STRIPS = 4


def split_rows():
    plane, strips = lax.axis_size(HI) * lax.axis_size(SIDE), lax.axis_size(STRIP)
    share = 16 * plane
    low = -(-offset_of(4) // (LANES * share)) * share
    share *= strips
    return -(-(offset_of(12) + 3 - SPLIT * LANES) // (LANES * share)) * share, low


class Part:
    def __init__(self, stage, plan, arena, slopes, slots, hbm, sems, p_ref, nat, natural):
        self.stage, self.arena, self.slopes, self.hbm, self.sems = stage, arena, slopes, hbm, sems
        self.sizes, self.tiles, self.at, _ = plan
        self.slots, self.p_ref, self.nat, self.natural = slots, p_ref, nat, natural
        self.copies = {}

    def view(self, name):
        return self.arena.at[pl.ds(self.at[name], self.tiles[name])].reshape(*self.sizes[name])

    def fetch(self, key, target=None):
        if target is None:
            target = self.slopes[key] if key in self.slopes else self.view(key)
        copy = pltpu.make_async_copy(self.hbm[key], target, self.sems.at[list(self.hbm).index(key)])
        copy.start()
        self.copies[key] = copy

    def need(self, *keys):
        for key in keys:
            self.copies[key].wait()

    def weight(self, k):
        rows, lanes = back_shape(k)
        ref = self.slots[SLOTS[k]].at[pl.ds(0, rows), pl.ds(0, lanes)]
        natural_rows(k, self.p_ref, self.nat, self.natural)
        backward_weights(k, self.natural, ref)
        return ref


def deep_kernel(cfg, sc, scal, flat_ref, *refs):
    own, groups = cfg["own"], cfg["groups"]
    h, h2, h3 = own // 2, own // 4, own // 8
    refs = list(refs)
    take = lambda m: [refs.pop(0) for _ in range(m)]
    names = DEEP["acts"] + DEEP["slopes"]
    hbm = dict(zip(names, take(len(names))))
    rays = take(1)[0]
    keep_hbm, send_hbm, g4_hbm, gs1_hbm, gs2_hbm = take(5)
    arena = take(1)[0]
    slopes = dict(zip(DEEP["slopes"], take(len(DEEP["slopes"]))))
    slots = dict(zip("yx", take(2)))
    p_ref, w10, bias10, hw, hwt, hb, gs1, gs2, acc, acc10, dhead, nat, natural, flat, sems, out_sems = refs
    part = Part(DEEP, cfg["plan"], arena, slopes, slots, hbm, sems, p_ref, nat, natural)
    view, need = part.view, part.need
    part.fetch("a9")
    for key in ("sl9", "a8", "sl8", "t2", "s1", "sl7", "a6", "sl6", "t3", "s2", "sl5", "a4", "sl4", "p2"):
        part.fetch(key)
    out = (flat, SPLIT)
    flat[...] = jnp.zeros(flat.shape, f32)
    v1, v2, v3 = [(sc[2 * i], sc[2 * i + 1]) for i in range(3)]
    load_flat(flat_ref, p_ref)
    natural_rows(10, p_ref, nat, natural)
    forward_weights(10, p_ref, natural, w10, bias10)
    prep_head(p_ref, hw, hwt, hb, nat)
    need("a9")
    head_part(own, scal, view("a9"), w10, bias10, hw, hwt, hb, rays, view("g10"), acc10, dhead, nat, out)

    weight = part.weight(10)
    need("sl9")
    input_grad(PLAIN, view("g10"), 1, weight, slopes["sl9"], view("g9"), h + 2, v1, -1)

    need("a8", "sl8")
    weight_grad(9, [(PAIR, view("a8"), 1)], view("g9"), h + 2, acc, nat, out)
    weight = part.weight(9)
    input_grad(PLAIN, view("g9"), 2, weight, slopes["sl8"], view("g8"), h + 2, v1, -1)

    need("t2", "s1", "sl7")
    weight_grad(8, [("up", rows_of(view("t2")), 3), (PAIR, view("s1"), 10)], view("g8"), h + 2, acc, nat, out)
    weight = part.weight(8)
    input_grad(JOIN, view("g8"), 1, weight, rows_of(slopes["sl7"]), rows_of(view("g7")), h + 4, v1, -2,
               side=gs1)
    outs = [pltpu.make_async_copy(gs1, gs1_hbm, out_sems.at[0])]
    outs[0].start()

    need("a6", "sl6")
    weight_grad(7, [(PAIR, view("a6"), 2)], view("g7"), h2 + 2, acc, nat, out)
    weight = part.weight(7)
    input_grad(PLAIN, view("g7"), 1, weight, slopes["sl6"], view("g6"), h2 + 4, v2, -2)

    need("t3", "s2", "sl5")
    weight_grad(6, [("up", rows_of(view("t3")), 2), (PAIR, view("s2"), 3)], view("g6"), h2 + 4, acc, nat, out)
    weight = part.weight(6)
    input_grad(JOIN, view("g6"), 2, weight, rows_of(slopes["sl5"]), rows_of(view("g5")), h2 + 4, v2, -2,
               three=True, side=gs2)
    outs.append(pltpu.make_async_copy(gs2, gs2_hbm, out_sems.at[1]))
    outs[-1].start()

    need("a4", "sl4")
    weight_grad(5, [(PAIR, view("a4"), 2)], view("g5"), h3 + 2, acc, nat, out)
    weight = part.weight(5)
    input_grad(PLAIN, view("g5"), 1, weight, slopes["sl4"], view("g4"), h3 + 4, v3, -2, three=True)

    outs.append(pltpu.make_async_copy(view("g4"), g4_hbm, out_sems.at[2]))
    outs[-1].start()

    need("p2")
    weight_grad(4, [(PAIR, view("p2"), 1)], view("g4"), h3 + 4, acc, nat, out)
    half = flat.shape[0] // 2
    for m, (core, target) in enumerate(((sc[7], keep_hbm), (1 - sc[7], send_hbm))):
        rows = pl.ds(pl.multiple_of(core * half, 8), half)
        outs.append(pltpu.make_async_copy(flat.at[rows], target, out_sems.at[3 + m]))
        outs[-1].start()
    for copy in outs:
        copy.wait()


def stage_scratch(stage, own, groups, plan, params):
    def slot(s):
        return tuple(max([back_shape(k)[d] for k in stage["layers"] if SLOTS[k] == s] + [8]) for d in (0, 1))

    slopes = slope_shapes(own, groups)
    return (
        [pltpu.VMEM((plan[3], groups, LANES), bf16)]
        + [pltpu.VMEM(slopes[k], jnp.int16) for k in stage["slopes"]]
        + [pltpu.VMEM(slot(s), bf16) for s in "yx" if any(SLOTS[k] == s for k in stage["layers"])]
        + [pltpu.VMEM((flat_rows(params.shape[0]), LANES), f32)]
    )


def deep(sc, scal, params, kept, rays, own, groups):
    plan = arena_plan(own, groups, DEEP["places"])
    h, h2 = own // 2, own // 4
    args = [kept[k] for k in DEEP["acts"] + DEEP["slopes"]] + [rays]
    rows = split_rows()[0]
    gs1, gs2 = (h + 4, 2, groups, LANES), (h2 + 4, 2, groups, LANES)
    return pl.pallas_call(
        functools.partial(deep_kernel, dict(own=own, groups=groups, plan=plan)),
        out_shape=[
            jax.ShapeDtypeStruct((rows // 2, LANES), f32),
            jax.ShapeDtypeStruct((rows // 2, LANES), f32),
            jax.ShapeDtypeStruct(grad_shapes(own, groups)["g4"], bf16),
            jax.ShapeDtypeStruct(gs1, f32),
            jax.ShapeDtypeStruct(gs2, f32),
        ],
        in_specs=[SMEM, VMEM, VMEM] + [ANY] * (len(args) - 1) + [VMEM],
        out_specs=[ANY] * 5,
        scratch_shapes=stage_scratch(DEEP, own, groups, plan, params)
        + [
            pltpu.VMEM(fwd_shape(10), bf16),
            pltpu.VMEM((1, fwd_shape(10)[1]), f32),
            pltpu.VMEM((4 * FINAL, 2 * LANES), bf16),
            pltpu.VMEM((2 * LANES, 4 * FINAL), bf16),
            pltpu.VMEM((1, 2 * LANES), f32),
            pltpu.VMEM(gs1, f32),
            pltpu.VMEM(gs2, f32),
            pltpu.VMEM((4, 5 * LANES, 2 * LANES), f32),
            pltpu.VMEM((3, 2 * LANES, 4 * FINAL), f32),
            pltpu.VMEM((4 * FINAL, 2 * LANES), f32),
            pltpu.VMEM((9 * (C3 + C2), LANES), f32),
            pltpu.VMEM((9 * (C3 + C2), LANES), bf16),
            pltpu.VMEM((rows, LANES), f32),
            pltpu.SemaphoreType.DMA((len(args),)),
            pltpu.SemaphoreType.DMA((5,)),
        ],
        name="deep",
        cost_estimate=pl.CostEstimate(flops=5 * 10**10, bytes_accessed=5 * 10**7, transcendentals=10**7),
        compiler_params=pltpu.CompilerParams(vmem_limit_bytes=GRANT - 5 * 2**20),
    )(sc, scal, params, *args)


def shallow_kernel(cfg, sc, flat_ref, *refs):
    own, groups = cfg["own"], cfg["groups"]
    h, h2, h3 = own // 2, own // 4, own // 8
    refs = list(refs)
    take = lambda m: [refs.pop(0) for _ in range(m)]
    names = SHALLOW["acts"] + SHALLOW["slopes"] + ("g4", "gs1", "gs2")
    hbm = dict(zip(names, take(len(names))))
    flat, arena = take(2)
    slopes = dict(zip(SHALLOW["slopes"], take(len(SHALLOW["slopes"]))))
    slots = dict(zip("y", take(1)))
    p_ref, gs1, gs2, acc, nat, natural, tmp, sems = refs
    part = Part(SHALLOW, cfg["plan"], arena, slopes, slots, hbm, sems, p_ref, nat, natural)
    view, need = part.view, part.need
    part.fetch("g4")
    part.fetch("sl3")
    part.fetch("gs2", gs2)
    for key in ("a2", "sl2", "p1", "sl1"):
        part.fetch(key)
    part.fetch("gs1", gs1)
    for key in ("a0", "sl0", "xc"):
        part.fetch(key)
    out = (flat, 0)
    flat[...] = jnp.zeros(flat.shape, f32)
    v1, v2 = [(sc[2 * i], sc[2 * i + 1]) for i in range(2)]
    load_flat(flat_ref, p_ref)
    weight = part.weight(4)
    need("g4", "sl3", "gs2")
    input_grad(POOL, view("g4"), 2, weight, fours_of(slopes["sl3"]), fours_of(view("g3")), h3 + 4, v2, -4,
               extra=fours_of(gs2))

    need("a2", "sl2")
    weight_grad(3, [(PAIR, view("a2"), 2)], view("g3"), h2 + 8, acc, nat, out)
    weight = part.weight(3)
    input_grad(PLAIN, view("g3"), 1, weight, slopes["sl2"], view("g2"), h2 + 10, v2, -5)

    need("p1", "sl1", "gs1")
    weight_grad(2, [(PAIR, view("p1"), 1)], view("g2"), h2 + 10, acc, nat, out)
    weight = part.weight(2)
    input_grad(POOL, view("g2"), 2, weight, fours_of(slopes["sl1"]), fours_of(view("g1")), h2 + 10, v1, -10,
               extra=fours_of(gs1))

    need("a0", "sl0", "xc")
    weight_grad(1, [(PAIR, view("a0"), 2)], view("g1"), h + 20, acc, nat, out)
    weight = part.weight(1)
    input_grad(LAST, view("g1"), 1, weight, slopes["sl0"], view("g0"), h + 22, v1, -11)
    first_grad(view("g0"), view("xc"), h + 22, out, tmp)


def shallow(sc, params, kept, g4, gs1, gs2, own, groups):
    plan = arena_plan(own, groups, SHALLOW["places"])
    args = [kept[k] for k in SHALLOW["acts"] + SHALLOW["slopes"]] + [g4, gs1, gs2]
    span = flat_range(SHALLOW["layers"], params.shape[0])
    return pl.pallas_call(
        functools.partial(shallow_kernel, dict(own=own, groups=groups, plan=plan, range=span)),
        out_shape=jax.ShapeDtypeStruct((split_rows()[1], LANES), f32),
        in_specs=[SMEM, VMEM] + [ANY] * len(args),
        out_specs=VMEM,
        scratch_shapes=stage_scratch(SHALLOW, own, groups, plan, params)
        + [
            pltpu.VMEM(gs1.shape, f32),
            pltpu.VMEM(gs2.shape, f32),
            pltpu.VMEM((4, 2 * LANES, 2 * LANES), f32),
            pltpu.VMEM((9 * C3, LANES), f32),
            pltpu.VMEM((9 * C3, LANES), bf16),
            pltpu.VMEM((8, LANES), f32),
            pltpu.SemaphoreType.DMA((len(args),)),
        ],
        name="shallow",
        cost_estimate=pl.CostEstimate(flops=2 * 10**10, bytes_accessed=2 * 10**7, transcendentals=10**7),
        compiler_params=pltpu.CompilerParams(vmem_limit_bytes=GRANT),
    )(sc, params, *args)


def add_up(value, n):
    return value.reshape(n, -1, LANES).sum(0)


def gather_up(value, axes, n):
    return lax.all_to_all(jnp.tile(value, (n, 1)), axes, 0, 0, tiled=True)


def from_others(value):
    strips = lax.axis_size(STRIP)
    if strips != STRIPS:
        whole = gather_up(value, (STRIP,), strips).reshape(strips, *value.shape)
        return [whole[t] for t in range(strips)]
    swaps = [[(i, i ^ x) for i in range(strips)] for x in range(1, strips)]
    return [value] + [lax.ppermute(value, STRIP, swap) for swap in swaps]


def tree_sum(values):
    while len(values) > 1:
        values = [a + b for a, b in zip(values[::2], values[1::2])] + values[len(values) // 2 * 2 :]
    return values[0]


def scatter_up(value):
    strips = lax.axis_size(STRIP)
    if strips != STRIPS:
        return add_up(lax.all_to_all(value, (STRIP,), 0, 0, tiled=True), strips)
    strip = lax.axis_index(STRIP)
    share = value.shape[0] // strips
    parts = [lax.dynamic_slice_in_dim(value, (strip ^ x) * share, share) for x in range(strips)]
    swaps = [[(i, i ^ x) for i in range(strips)] for x in range(strips)]
    return tree_sum(parts[:1] + [lax.ppermute(parts[x], STRIP, swaps[x]) for x in range(1, strips)])


def sum_all(keep, send, low_of):
    plane = lax.axis_size(HI) * lax.axis_size(SIDE)
    swap = [(0, 1), (1, 0)]
    part = keep + lax.ppermute(send, CORE, swap)
    part = lax.all_to_all(part, (HI, SIDE), 0, 0, tiled=True)
    part, low = lax.optimization_barrier((part, low_of()))
    low = lax.all_to_all(low, (CORE, HI, SIDE), 0, 0, tiled=True)
    high = from_others(scatter_up(add_up(part, plane)))
    high, low = lax.optimization_barrier((high, low))
    low = tree_sum(from_others(add_up(low, 2 * plane)))
    part = gather_up(jnp.concatenate([*high, low], axis=0), (HI, SIDE), plane)
    return part, lax.ppermute(part, CORE, swap)


def adam_kernel(chunks, low_rows, sc, mine, other, weights, first, second, *refs):
    outs, loss_ref, norm_ref, grads, news, sems = refs[:3], refs[3], refs[4], refs[5], refs[6:9], refs[9]
    size = weights.shape[0]
    plane, strips = chunks
    low_share = low_rows // (2 * plane)
    step_ = mine.shape[0] // plane
    share = (step_ - low_share) // strips
    for c, parts in enumerate(((mine, other), (other, mine))):

        @pl.when(sc[7] == c)
        def _():
            for m, ref in enumerate(parts):
                for n in range(plane):
                    for t in range(strips):
                        slot = sc[6] ^ t if strips == STRIPS else t
                        row = SPLIT + ((m * plane + n) * strips + t) * share
                        grads[row : row + share] = ref[pl.ds(pl.multiple_of(n * step_ + slot * share, 8), share)]
            for m, ref in enumerate(parts):
                for n in range(plane):
                    start = n * step_ + strips * share
                    row = (m * plane + n) * low_share
                    same = min(max(SPLIT - row, 0), low_share)
                    if same:
                        grads[row : row + same] = ref[start : start + same]
                    if same < low_share:
                        grads[row + same : row + low_share] += ref[start + same : start + low_share]

    whole = size // 1024
    many = divisor(whole, 25)
    steps = whole // many

    def square(i, total):
        g = grads[pl.ds(pl.multiple_of(i * many * 8, 8), many * 8), :]
        return total + jnp.sum((g * g).reshape(many, 8, LANES), axis=0)

    total = lax.fori_loop(0, steps, square, jnp.zeros((8, LANES), f32))
    last = grads[8 * whole : 8 * whole + 8, :]
    index = lax.broadcasted_iota(jnp.int32, (8, LANES), 0) * LANES + lax.broadcasted_iota(jnp.int32, (8, LANES), 1)
    total += jnp.where(index < size - 1024 * whole, last * last, 0.0)
    norm = jnp.sqrt(jnp.sum(total, axis=(0, 1), keepdims=True))
    norm_ref[...] = norm.reshape(1)
    line, lane0 = divmod(size - 1024 * whole, LANES)
    loss_ref[...] = turn(last[line : line + 1], -lane0).reshape(LANES)[:3]
    scale = jnp.minimum(1.0, clip_limit / (norm + 1e-06))

    def update(where, g):
        clipped = g * scale[0, 0]
        one = beta_one * first[where] + (1.0 - beta_one) * clipped
        two = beta_two * second[where] + (1.0 - beta_two) * clipped * clipped
        first_hat = one / (1.0 - beta_one**step_count)
        second_hat = two / (1.0 - beta_two**step_count)
        w = weights[where]
        news[0][where] = w - learn_rate * (first_hat / (jnp.sqrt(second_hat) + adam_eps) + decay_rate * w)
        news[1][where] = one
        news[2][where] = two

    copies = []

    def send(n, where):
        for m in range(3):
            copy = pltpu.make_async_copy(news[m].at[where], outs[m].at[where], sems.at[n, m])
            copy.start()
            copies.append(copy)

    groups = 4
    for n in range(groups):
        first_step, last_step = steps * n // groups, steps * (n + 1) // groups

        def step(i, _):
            g = grads[pl.ds(pl.multiple_of(i * many * 8, 8), many * 8), :].reshape(many * 1024)
            update(pl.ds(pl.multiple_of(i * many * 1024, 1024), many * 1024), g)

        lax.fori_loop(first_step, last_step, step, None)
        if n < groups - 1:
            send(n, pl.ds(first_step * many * 1024, (last_step - first_step) * many * 1024))
    rest = size - 1024 * whole
    if rest:
        update(pl.ds(1024 * whole, rest), last.reshape(1024)[:rest])
    start = steps * (groups - 1) // groups * many * 1024
    send(groups - 1, pl.ds(start, size - start))
    for copy in copies:
        copy.wait()


def adam(sc, mine, other, params, first, second):
    chunks = (lax.axis_size(HI) * lax.axis_size(SIDE), lax.axis_size(STRIP))
    low_rows = split_rows()[1]
    flat = jax.ShapeDtypeStruct(params.shape, f32)
    return pl.pallas_call(
        functools.partial(adam_kernel, chunks, low_rows),
        out_shape=[flat, flat, flat, jax.ShapeDtypeStruct((3,), f32), jax.ShapeDtypeStruct((1,), f32)],
        in_specs=[SMEM] + [VMEM] * 5,
        out_specs=[ANY] * 3 + [VMEM] * 2,
        scratch_shapes=[pltpu.VMEM((SPLIT + 2 * mine.shape[0] - low_rows, LANES), f32)]
        + [pltpu.VMEM(params.shape, f32)] * 3
        + [pltpu.SemaphoreType.DMA((4, 3))],
        name="adam",
        cost_estimate=pl.CostEstimate(flops=10**7, bytes_accessed=14 * 10**6, transcendentals=10**6),
        compiler_params=pltpu.CompilerParams(vmem_limit_bytes=9 * 2**20),
    )(sc, mine, other, params, first, second)


AXES = (STRIP, HI, SIDE, CORE)
GROUP = (HI, SIDE, CORE)


def body(patch, images, fg_masks, ray_targets, params, moment_one, moment_two):
    strips, hi, half, core = (lax.axis_size(a) for a in AXES)
    cols = half * core
    count, rows_here, cols_here = images.shape
    own = rows_here * hi
    strip = lax.axis_index(STRIP)

    got = lax.all_to_all(tiles_of(images, fg_masks, strips), AXES, 0, 0, tiled=True)
    ready, rays = prep(params, jnp.transpose(ray_targets, (0, 1, 3, 2)))
    rays = lax.all_to_all(rays, GROUP, 0, 0, tiled=True)
    rays = rays.reshape(hi, cols, rows_here, cols_here // 4, 4 * RAYS)

    bounds = [
        jnp.stack([-strip * (own // d), patch // d - strip * (own // d)]).astype(jnp.int32)
        for d in (2, 4, 8)
    ]
    sc = jnp.concatenate([*bounds, jnp.stack([strip, lax.axis_index(CORE)]).astype(jnp.int32)])
    tiling = (hi, strips, cols, rows_here, patch)
    kept, scal = forward(sc, got, ready, own, tiling, count * patch * patch)
    groups = patch // 4
    keep, send, g4, gs1, gs2 = deep(sc, scal, params, kept, rays, own, groups)
    mine, other = sum_all(keep, send, lambda: shallow(sc, params, kept, g4, gs1, gs2, own, groups))
    new_params, new_one, new_two, loss_terms, norm = adam(sc, mine, other, params, moment_one, moment_two)
    return (new_params, new_one, new_two, loss_terms, scal[3, 0], norm[0])


def solution(mesh):
    rows, cols = mesh.shape["rows"], mesh.shape["cols"]
    patches = 8
    hi = patches // cols
    split = Mesh(mesh.devices.reshape(rows // hi, hi, cols // 2, 2), AXES)
    tiled = P(None, (STRIP, HI), (SIDE, CORE))
    in_specs = (tiled, tiled, P(None, (STRIP, HI), (SIDE, CORE), None), P(), P(), P())
    out_specs = (P(),) * 6

    def step(images, *rest):
        if images.shape[0] != patches:
            raise ValueError("eight patches")
        part = functools.partial(body, images.shape[1])
        return jax.shard_map(part, mesh=split, in_specs=in_specs, out_specs=out_specs, check_vma=False)(
            images, *rest
        )

    return step
```
